32 devices in a mesh: seq: 8 (over z, x), ctx: 4 (over y, core).
Axes of the slice: x: 2, y: 2, z: 4, core: 2. Of those that a mesh axis runs over, the one named last changes fastest.
Arguments:
- tokens: bfloat16 [16, 1024, 768], P('seq', 'ctx'), may hold values from -6 to 6
- prior_logits: bfloat16 [16, 12, 1024, 1024], P('seq', None, 'ctx'), may hold values from -6 to 6
- doc_ids: int32 [16, 1024], P('seq', 'ctx'), may hold values from 0 to 255, as said below
- w_query: bfloat16 [768, 768], P('seq'), may hold values from -0.21875 to 0.21875
- w_key: bfloat16 [768, 768], P('seq'), may hold values from -0.21875 to 0.21875
- w_value: bfloat16 [768, 768], P('seq'), may hold values from -0.21875 to 0.21875
- w_out: bfloat16 [768, 768], P('seq'), may hold values from -0.875 to 0.875
- b_query: bfloat16 [768], P('seq'), may hold values from -3 to 3
- b_value: bfloat16 [768], P('seq'), may hold values from -3 to 3
- b_out: bfloat16 [768], P('seq'), may hold values from -3 to 3
- first_norm_gain: bfloat16 [768], P('seq'), may hold values from 0.5 to 1.5
- norm1_shift: bfloat16 [768], P('seq'), may hold values from -3 to 3
- w_in: bfloat16 [768, 3072], P('seq'), may hold values from -0.21875 to 0.21875
- b_in: bfloat16 [3072], P('seq'), may hold values from -3 to 3
- w_down: bfloat16 [3072, 768], P('seq'), may hold values from -0.109375 to 0.109375
- b_down: bfloat16 [768], P('seq'), may hold values from -3 to 3
- norm2_gain: bfloat16 [768], P('seq'), may hold values from 0.5 to 1.5
- norm2_shift: bfloat16 [768], P('seq'), may hold values from -3 to 3
- cotangent: bfloat16 [16, 1024, 768], P('seq', 'ctx'), may hold values from -6 to 6
Outputs:
- output: bfloat16 [16, 1024, 768], P('seq', 'ctx')
- raw_logits: bfloat16 [16, 12, 1024, 1024], P('seq', None, 'ctx')
- grad_tokens: float32 [16, 1024, 768], P('seq', 'ctx')
- grad_prior: bfloat16 [16, 12, 1024, 1024], P('seq', None, 'ctx')
- grad_w_query: float32 [768, 768], P('seq')
- grad_w_key: float32 [768, 768], P('seq')
- grad_w_value: float32 [768, 768], P('seq')
- grad_w_out: float32 [768, 768], P('seq')
- grad_b_query: float32 [768], P('seq')
- grad_b_value: float32 [768], P('seq')
- grad_b_out: float32 [768], P('seq')
- grad_norm1_gain: float32 [768], P('seq')
- grad_norm1_shift: float32 [768], P('seq')
- grad_w_in: float32 [768, 3072], P('seq')
- grad_b_in: float32 [3072], P('seq')
- grad_w_down: float32 [3072, 768], P('seq')
- grad_b_down: float32 [768], P('seq')
- grad_norm2_gain: float32 [768], P('seq')
- grad_norm2_shift: float32 [768], P('seq')
The draws below stay inside these ranges and needn't reach their ends.
Inputs may be any that keep to these rules, and one draw needn't show every extreme that they name: `doc_ids`: in every sequence the document numbers start at 0 and rise by 0 or 1 from one token to the next, up to at most 255, which the first sequence reaches. In each aligned group of 2 sequences, one sequence has a document holding a token of its first 256 tokens and one of its last 256 tokens.
All inputs are finite; a program needn't handle non-finite values.
Results may differ from the reference program's by a relative error of at most 0.013.
Values may be sent and summed in bfloat16 or wider, within the bound.
No kernel may reach another device: no remote copies, remote signals or barrier semaphores. Data moves between devices by JAX's collectives and lax.ppermute only.
A program may use at most 256 MiB of HBM per device.

```python
import math
import jax
import jax.numpy as jnp
from jax import lax

D = 768
HEADS = 12
HEAD_DIM = 64
FF = 3072
SEQ_DEV = 2
SHARD = 256
SEQS = 16
LEN = 1024


def draw_doc_ids(key, part):
    groups = SEQS // SEQ_DEV
    ctx_count = LEN // SHARD
    rate_key, flag_key, pick_key, end_key = jax.random.split(jax.random.fold_in(key, 17), 4)
    level = jax.random.randint(rate_key, (SEQS, 1), 1, 8)
    rate = jnp.left_shift(jnp.ones_like(level), level)
    flags = jax.random.randint(flag_key, (SEQS, LEN), 0, 1024) < rate
    position = jnp.arange(LEN)[None, :]
    chosen = jax.random.randint(pick_key, (groups, 1), 0, SEQ_DEV)
    is_chosen = (jnp.arange(SEQ_DEV)[None, :] == chosen).reshape(SEQS, 1)
    first_end = jax.random.randint(end_key, (SEQS, 1), (ctx_count - 1) * SHARD + 1, LEN + 1)
    flags = flags & (position > 0) & jnp.logical_not(is_chosen & (position < first_end))
    first_row = jnp.arange(SEQS)[:, None] == 0
    filled = position >= LEN - SHARD + 1
    flags = jnp.where(first_row, filled, flags)
    counts = jnp.cumsum(flags.astype(jnp.int32), axis=1)
    return jnp.minimum(counts, SHARD - 1).astype(jnp.int32)


def raised(entries, key, source, target, blocks, factor):
    def block_of(axis_at):
        return (jnp.arange(entries.shape[axis_at]) // (entries.shape[axis_at] // blocks)).reshape((-1,) + (1,) * (entries.ndim - 1 - axis_at))

    near = jax.random.permutation(key, blocks)[block_of(target)]
    far = (block_of(target) + blocks // 2) % blocks
    return jnp.where((block_of(source) == near) | (block_of(source) == far), factor * entries, entries)


def block_levels(rng, shape, pieces, smallest, largest):
    def one(axis_at, shards_of):
        heights = jax.random.uniform(jax.random.fold_in(jax.random.fold_in(rng, 6), axis_at), (shards_of,), jnp.float32, smallest / len(pieces), largest / len(pieces))
        return jnp.repeat(jnp.exp(heights), shape[axis_at] // shards_of).reshape((-1,) + (1,) * (len(shape) - axis_at - 1))

    gain = one(*pieces[0])
    for cut in pieces[1:]:
        gain = gain * one(*cut)
    return gain


def centred(own_key, shape, deviation, bound, cuts=(), held_as=jnp.bfloat16):
    drawn = jax.random.normal(own_key, shape, jnp.float32) * deviation
    if len(cuts) > 0:
        drawn = block_levels(own_key, shape, cuts, -0.22, 0.18) * drawn
    return jnp.clip(drawn, min=-bound, max=bound).astype(held_as)


def bell_draw_with(stream_key, dims, spread, bound, pieces, heavy, kind=jnp.bfloat16):
    drawn = spread * jax.random.normal(stream_key, dims, jnp.float32)
    if pieces:
        drawn = drawn * block_levels(stream_key, dims, pieces, -0.22, 0.18)
    return jnp.clip(raised(drawn, jax.random.fold_in(stream_key, 3), *heavy), -bound, bound).astype(kind)


def setup_inputs(seed: int = 0) -> dict:
    streams_of = jax.random.split(jax.random.key(seed), 20)
    return {
        "tokens": bell_draw_with(streams_of[0], (SEQS, LEN, D), 1.0, 6.0, ((0, 8), (1, 4)), (0, 2, 8, 2.0)),
        "prior_logits": centred(streams_of[1], (SEQS, HEADS, LEN, LEN), 1.0, 6.0, ((0, 8), (2, 4))),
        "doc_ids": draw_doc_ids(jax.random.fold_in(streams_of[19], 71), 0),
        "w_query": centred(streams_of[3], (D, D), D ** -0.5, 0.21875, ((0, 8),)),
        "w_key": centred(streams_of[4], (D, D), D ** -0.5, 0.21875, ((0, 8),)),
        "w_value": centred(streams_of[5], (D, D), D ** -0.5, 0.21875, ((0, 8),)),
        "w_out": centred(streams_of[6], (D, D), (D // 16) ** -0.5, 0.875, ((0, 8),)),
        "b_query": centred(streams_of[7], (D,), 0.5, 3.0, ((0, 8),)),
        "b_value": centred(streams_of[8], (D,), 0.5, 3.0, ((0, 8),)),
        "b_out": centred(streams_of[9], (D,), 0.5, 3.0, ((0, 8),)),
        "first_norm_gain": jnp.clip(1.0 + 0.1 * jax.random.normal(streams_of[10], (D,), jnp.float32), 0.5, 1.5).astype(jnp.bfloat16),
        "norm1_shift": centred(streams_of[11], (D,), 0.5, 3.0, ((0, 8),)),
        "w_in": centred(streams_of[12], (D, FF), D ** -0.5, 0.21875, ((0, 8),)),
        "b_in": centred(streams_of[13], (FF,), 0.5, 3.0, ((0, 8),)),
        "w_down": centred(streams_of[14], (FF, D), FF ** -0.5, 0.109375, ((0, 8),)),
        "b_down": centred(streams_of[15], (D,), 0.5, 3.0, ((0, 8),)),
        "norm2_gain": jnp.clip(1.0 + 0.1 * jax.random.normal(streams_of[16], (D,), jnp.float32), 0.5, 1.5).astype(jnp.bfloat16),
        "norm2_shift": centred(streams_of[17], (D,), 0.5, 3.0, ((0, 8),)),
        "cotangent": centred(streams_of[18], (SEQS, LEN, D), 1.0, 6.0, ((0, 8), (1, 4))),
    }


EPSILON = 1e-05
NEGATIVE = -1e+30
TOP_ACCURACY = lax.Precision.HIGHEST

@jax.custom_vjp
def low(v):
    return lax.optimization_barrier(v.astype(jnp.bfloat16)).astype(jnp.float32)

@jax.custom_vjp
def low_back(v):
    return v

def low_keep(v):
    return (low(v), None)

def low_pass(kept, grad):
    return (grad,)

def back_keep(v):
    return (v, None)

def back_low(kept, grad):
    return (low(grad),)
low.defvjp(low_keep, low_pass)
low_back.defvjp(back_keep, back_low)

def norm_rows(hidden_in, scales, shifts):
    row_mean = lax.optimization_barrier(jnp.mean(hidden_in, -1, keepdims=True))
    centered = hidden_in - row_mean
    variance = lax.optimization_barrier(jnp.mean(centered * centered, -1, keepdims=True))
    return centered * lax.rsqrt(variance + EPSILON) * scales + shifts

def project(input_rows, weight_matrix):
    return jnp.einsum('kgj,jb->kgb', input_rows, weight_matrix, precision=TOP_ACCURACY)

def attend(blocks):
    queries, keys_all, values, priors, documents = blocks
    score_scale = 1.0 / math.sqrt(HEAD_DIM)
    query_heads = queries.reshape(LEN, HEADS, HEAD_DIM)
    key_heads = keys_all.reshape(LEN, HEADS, HEAD_DIM)
    value_heads = values.reshape(LEN, HEADS, HEAD_DIM)
    raw_logits = low_back(jnp.einsum('qhe,khe->hqk', query_heads, key_heads, precision=TOP_ACCURACY) * score_scale + priors)
    same_doc = (documents[:, None] == documents[None, :])[None]
    masked = jnp.where(same_doc, raw_logits, NEGATIVE)
    row_max = lax.optimization_barrier(jnp.max(masked, -1, keepdims=True))
    exp_terms = jnp.exp(masked - row_max)
    probs_low = low(exp_terms / lax.optimization_barrier(jnp.sum(exp_terms, -1, keepdims=True)))
    mixed_heads = jnp.einsum('hqk,khe->qhe', probs_low, value_heads, precision=TOP_ACCURACY)
    return (mixed_heads.reshape(LEN, HEADS * HEAD_DIM), raw_logits)

def reference(tokens, prior_logits, doc_ids, w_query, w_key, w_value, w_out, b_query, b_value, b_out, first_norm_gain, norm1_shift, w_in, b_in, w_down, b_down, norm2_gain, norm2_shift, cotangent):
    floats = tuple((tensor.astype(jnp.float32) for tensor in (tokens, prior_logits, w_query, w_key, w_value, w_out, b_query, b_value, b_out, first_norm_gain, norm1_shift, w_in, b_in, w_down, b_down, norm2_gain, norm2_shift)))

    def forward_layer(inputs, priors, weight_q, weight_k, weight_v, weight_o, bias_q, bias_v, bias_o, gain_one, shift_one, weight_i, bias_i, weight_d, bias_d, second_norm_gain, shift_two):
        queries = low(low_back(project(inputs, weight_q) + bias_q))
        keys_all = low(low_back(project(inputs, weight_k)))
        values = low(low_back(project(inputs, weight_v) + bias_v))
        mixed, raw_logits = lax.map(jax.checkpoint(attend), (queries, keys_all, values, priors, doc_ids))
        mixed = low(low_back(mixed))
        branch = low_back(project(mixed, weight_o) + bias_o)
        first = norm_rows(inputs + branch, gain_one, shift_one)
        inner = low(first)
        hidden = low(jax.nn.gelu(low_back(project(inner, weight_i) + bias_i), approximate=False))
        second = low_back(project(hidden, weight_d) + bias_d)
        return (norm_rows(first + second, second_norm_gain, shift_two), raw_logits)
    (output, raw_logits), pullback = jax.vjp(forward_layer, *floats)
    grads = pullback((cotangent.astype(jnp.float32), jnp.zeros_like(raw_logits)))
    return (output.astype(jnp.bfloat16), raw_logits.astype(jnp.bfloat16), grads[0], grads[1].astype(jnp.bfloat16), grads[2], grads[3], grads[4], grads[5], grads[6], grads[7], grads[8], grads[9], grads[10], grads[11], grads[12], grads[13], grads[14], grads[15], grads[16])
```

```python
import functools
import math

import jax
import jax.numpy as jnp
from jax import lax
from jax.experimental import pallas as pl
from jax.experimental.pallas import tpu as pltpu
from jax.sharding import PartitionSpec as P

EPSILON = 1e-05
NEGATIVE = -1e30
BF = jnp.bfloat16
F32 = jnp.float32
VM = pltpu.VMEM
ANY = pl.ANY
VMEM_LIMIT = 60 * 1024 * 1024
GROUPS = 3


def dot(a, b):
    return lax.dot_general(a, b, (((1,), (0,)), ((), ())), preferred_element_type=F32)


def dot_nt(a, b):
    return lax.dot_general(a, b, (((1,), (1,)), ((), ())), preferred_element_type=F32)


def dot_tn(a, b):
    return lax.dot_general(a, b, (((0,), (0,)), ((), ())), preferred_element_type=F32)


def vmem(shape=None, index=None):
    if shape is None:
        return pl.BlockSpec(memory_space=VM)
    return pl.BlockSpec(shape, index)


def params(n_grid=0):
    return pltpu.CompilerParams(
        vmem_limit_bytes=VMEM_LIMIT,
        dimension_semantics=("arbitrary",) * n_grid if n_grid else None,
    )


def smem():
    return pl.BlockSpec(memory_space=pltpu.SMEM)


def swap(value, axis, size, bit):
    step = 1 << bit
    return lax.ppermute(value, axis, [(i, i ^ step) for i in range(size)])


def gather_seq(block, size, order):
    held = block[None]
    for bit in order:
        held = jnp.concatenate([held, swap(held, "seq", size, bit)], 0)
    return held


def reduce_seq(held, size, order):
    for bit in reversed(order):
        half = held.shape[0] // 2
        got = swap(held[half:], "seq", size, bit)
        held = (held[:half].astype(F32) + got.astype(F32)).astype(held.dtype)
    return held


def place(index, order):
    out = 0
    for step, bit in enumerate(order):
        out = out | (((index >> bit) & 1) << step)
    return out


def turn_kernel(scal, t0, t1, t2, t3, out_ref):
    mc = scal[1]
    seqs, _, width = t0.shape
    shard = out_ref.shape[2] // 4
    for j, tok in enumerate((t0, t1, t2, t3)):
        where = pl.multiple_of((mc ^ j) * shard, shard)
        for s in range(seqs):
            out_ref[s, :, pl.ds(where, shard)] = tok[s, :shard, :].T


def attend_kernel(
    order, shards, aliased,
    scal, t0, t1, t2, t3, doc_ref, w_own, w_got, bias_ref, prior_ref, *rest,
):
    if aliased:
        rest = rest[1:]
    raw_ref, e_ref, q_ref, k_ref, v_ref, o_ref, inv_ref, w_s, kt_s, mask_s = rest
    s, h = pl.program_id(0), pl.program_id(1)
    pm, mc, core = scal[0], scal[1], scal[2]
    rows = w_own.shape[1]
    half = w_own.shape[2]
    cols = q_ref.shape[2]
    shard = q_ref.shape[1]
    head = cols // 4

    @pl.when((s == 0) & (h == 0))
    def _():
        for i in range(shards):
            at = place(i, order) ^ pm
            mine, other = w_own[at], w_got[at]
            first = core == 0
            w_s[i * rows:(i + 1) * rows, :half] = jnp.where(first, mine, other)
            w_s[i * rows:(i + 1) * rows, half:] = jnp.where(first, other, mine)

    @pl.when(h == 0)
    def _():
        q = dot(t0[s, :shard, :], w_s[:, :cols]) + bias_ref[0:1, :]
        q_ref[0] = (q.astype(BF).astype(F32) * (1.0 / math.sqrt(head))).astype(BF)
        mine = doc_ref[0]
        for j, tok in enumerate((t0, t1, t2, t3)):
            where = pl.multiple_of((mc ^ j) * shard, shard)
            kv = dot(tok[s, :shard, :], w_s[:, cols:])
            k_ref[0, pl.ds(where, shard), :] = kv[:, :cols].astype(BF)
            v_ref[0, pl.ds(where, shard), :] = (kv[:, cols:] + bias_ref[1:2, :]).astype(BF)
            docs = tok[s, shard:shard + 1, :shard].astype(F32)
            mask_s[:, pl.ds(where, shard)] = jnp.where(mine == docs, 0.0, NEGATIVE)
        kt_s[...] = k_ref[0].T

    lane = lax.broadcasted_iota(jnp.int32, (shard, cols), 1) // head
    this = lane == h
    qm = jnp.where(this, q_ref[0].astype(F32), 0.0).astype(BF)
    length = k_ref.shape[1]
    lane_k = lax.broadcasted_iota(jnp.int32, (length, cols), 1) // head
    v_one = jnp.where(lane_k == h, v_ref[0].astype(F32), 1.0).astype(BF)
    step = 64
    for r in range(0, shard, step):
        logits = dot(qm[r:r + step], kt_s[...]) + prior_ref[0, 0, r:r + step, :].astype(F32)
        raw_ref[0, 0, r:r + step, :] = logits.astype(BF)
        masked = logits + mask_s[r:r + step, :]
        top = jnp.max(masked, -1, keepdims=True)
        e_ref[0, 0, r:r + step, :] = jnp.exp(masked - top).astype(BF)
    o = dot(e_ref[0, 0], v_one)
    total = jnp.max(jnp.where(lane == (h + 1) % 4, o, 0.0), -1, keepdims=True)
    inv = 1.0 / total
    o_ref[0] = jnp.where(this, o * inv, o_ref[0])
    inv_ref[0] = jnp.where(this, inv, inv_ref[0])


def gelu_parts(x):
    z = jnp.abs(x) * 0.7071067811865476
    t = 1.0 / (1.0 + 0.3275911 * z)
    e = jnp.exp(-0.5 * x * x)
    poly = t * (0.254829592 + t * (-0.284496736 + t * (1.421413741 + t * (-1.453152027 + t * 1.061405429))))
    tail = 0.5 * poly * e
    phi = jnp.where(x >= 0, 1.0 - tail, tail)
    return x * phi, phi + x * (e * 0.3989422804014327)


def moments(x):
    mean = jnp.mean(x, -1, keepdims=True)
    centered = x - mean
    inverse = lax.rsqrt(jnp.mean(centered * centered, -1, keepdims=True) + EPSILON)
    return centered * inverse, inverse


def norm_back(grad, normed, inverse, gain):
    scaled = grad * gain
    return inverse * (
        scaled - jnp.mean(scaled, -1, keepdims=True)
        - normed * jnp.mean(scaled * normed, -1, keepdims=True)
    )


def copies_of(pairs, sem, base):
    return [pltpu.make_async_copy(src, dst, sem.at[base + i]) for i, (src, dst) in enumerate(pairs)]


def forward_kernel(
    oi, oo, od, shards,
    scal, o0, o1, o2, tok_ref, cot_ref, vec_ref, bin_ref,
    wo_own, wo_got, i0, i1, i2, i3, d_own, d_got,
    out_ref, first_n_ref, inv1_ref, inner_ref, hid_ref, dg_ref, dsum2_ref, dsec_ref, vg_ref,
    wo_s, wi_s, wd_s, first_s, acc_s, sem,
):
    mc, core = scal[1], scal[2]
    p_o, p_i, p_d = scal[3], scal[4], scal[5]
    my_y = mc >> 1
    rows = wo_own.shape[1]
    half = wo_own.shape[2]
    sub = d_own.shape[2]
    seqs, shard, width = tok_ref.shape
    n_rows = seqs * shard
    base = 0
    in_copies, down_copies = [], []
    for j, ref in enumerate((i0, i1, i2, i3)):
        in_copies.append(copies_of(
            [(ref.at[place(s, oi) ^ p_i], wi_s.at[j, pl.ds(s * rows, rows)]) for s in range(shards)], sem, base))
        base += shards
        src = d_own if j % 2 == 0 else d_got
        down_copies.append(copies_of(
            [(src.at[place(s, od) ^ p_d, my_y ^ (j >> 1)], wd_s.at[j, pl.ds(s * sub, sub)]) for s in range(shards)], sem, base))
        base += shards
    for j in range(4):
        for c in in_copies[j] + down_copies[j]:
            c.start()
    first_core = core == 0
    for i in range(shards):
        at = place(i, oo) ^ p_o
        mine, other = wo_own[at], wo_got[at]
        wo_s[i * rows:(i + 1) * rows, :half] = jnp.where(first_core, mine, other)
        wo_s[i * rows:(i + 1) * rows, half:] = jnp.where(first_core, other, mine)
    mixed = jnp.concatenate([r[...].reshape(n_rows, -1).astype(BF) for r in (o0, o1, o2)], 1)
    tokens = tok_ref[...].reshape(n_rows, width).astype(F32)
    normed, inverse = moments(tokens + (dot(mixed, wo_s[...]) + vec_ref[0:1, :]))
    first_n_ref[...] = normed
    inv1_ref[...] = inverse
    first = normed * vec_ref[1:2, :] + vec_ref[2:3, :]
    first_s[...] = first
    inner_ref[...] = first.astype(BF)
    for j in range(4):
        for c in in_copies[j]:
            c.wait()
        for r in range(0, n_rows, 128):
            pre = dot(inner_ref[r:r + 128, :], wi_s[j]) + bin_ref[mc ^ j]
            hid, dg = gelu_parts(pre)
            hid_ref[j, r:r + 128, :] = hid.astype(BF)
            dg_ref[j, r:r + 128, :] = dg.astype(BF)
        for c in down_copies[j]:
            c.wait()
        part = dot(hid_ref[j], wd_s[j])
        acc_s[...] = part if j == 0 else acc_s[...] + part
    normed, inverse = moments(first_s[...] + (acc_s[...] + vec_ref[3:4, :]))
    gain = vec_ref[4:5, :]
    out_ref[...] = (normed * gain + vec_ref[5:6, :]).astype(BF).reshape(seqs, shard, width)
    dy = cot_ref[...].reshape(n_rows, width).astype(F32)
    dsum2 = norm_back(dy, normed, inverse, gain)
    dsum2_ref[...] = dsum2
    dsec = dsum2.astype(BF)
    dsec_ref[...] = dsec
    vg_ref[0:1, :] = jnp.sum(dy * normed, 0, keepdims=True)
    vg_ref[1:2, :] = jnp.sum(dy, 0, keepdims=True)
    vg_ref[2:3, :] = jnp.sum(dsec.astype(F32), 0, keepdims=True)


def backward_kernel(
    oi, oo, od, shards,
    scal, o0, o1, o2, first_n, inv1, inner, hid, dg, dsum2, dsec, vec_ref,
    wo_own, wo_got, i0, i1, i2, i3, d_own, d_got,
    gi0, gi1, gi2, gi3, gd_keep, gd_send, go_keep, go_send, dsum1_ref, dmix_ref, vg_ref, gbin_ref,
    wo_s, wi_s, wd_s, acc_s, sem,
):
    mc, core = scal[1], scal[2]
    p_o, p_i, p_d = scal[3], scal[4], scal[5]
    my_y = mc >> 1
    rows = wo_own.shape[1]
    half = wo_own.shape[2]
    sub = d_own.shape[2]
    n_rows, width = dsec.shape
    base = 0
    in_copies, down_copies = [], []
    for j, ref in enumerate((i0, i1, i2, i3)):
        src = d_own if j % 2 == 0 else d_got
        down_copies.append(copies_of(
            [(src.at[place(s, od) ^ p_d, my_y ^ (j >> 1)], wd_s.at[j, pl.ds(s * sub, sub)]) for s in range(shards)], sem, base))
        base += shards
        in_copies.append(copies_of(
            [(ref.at[place(s, oi) ^ p_i], wi_s.at[j, pl.ds(s * rows, rows)]) for s in range(shards)], sem, base))
        base += shards
    for j in range(4):
        for c in down_copies[j] + in_copies[j]:
            c.start()
    first_core = core == 0
    for i in range(shards):
        at = place(i, oo) ^ p_o
        mine, other = wo_own[at], wo_got[at]
        wo_s[i * rows:(i + 1) * rows, :half] = jnp.where(first_core, mine, other)
        wo_s[i * rows:(i + 1) * rows, half:] = jnp.where(first_core, other, mine)
    for j, gi in enumerate((gi0, gi1, gi2, gi3)):
        gd = gd_keep if j % 2 == 0 else gd_send
        grad_d = dot_tn(hid[j], dsec[...]).astype(BF)
        for s in range(shards):
            gd[place(s, od) ^ p_d, my_y ^ (j >> 1)] = grad_d[s * sub:(s + 1) * sub]
        for c in down_copies[j]:
            c.wait()
        dpre = (dot_nt(dsec[...], wd_s[j]) * dg[j].astype(F32)).astype(BF)
        gbin_ref[mc ^ j] = jnp.sum(dpre.astype(F32), 0, keepdims=True)
        grad_i = dot_tn(inner[...], dpre).astype(BF)
        for s in range(shards):
            gi[place(s, oi) ^ p_i] = grad_i[s * rows:(s + 1) * rows]
        for c in in_copies[j]:
            c.wait()
        part = dot_nt(dpre, wi_s[j])
        acc_s[...] = (dsum2[...] if j == 0 else acc_s[...]) + part
    dfirst = acc_s[...]
    normed = first_n[...]
    dsum1 = norm_back(dfirst, normed, inv1[...], vec_ref[1:2, :])
    dsum1_ref[...] = dsum1
    dbranch = dsum1.astype(BF)
    vg_ref[0:1, :] = jnp.sum(dfirst * normed, 0, keepdims=True)
    vg_ref[1:2, :] = jnp.sum(dfirst, 0, keepdims=True)
    vg_ref[2:3, :] = jnp.sum(dbranch.astype(F32), 0, keepdims=True)
    dmix_ref[...] = dot_nt(dbranch, wo_s[...]).astype(BF).reshape(dmix_ref.shape)
    mixed = jnp.concatenate([r[...].reshape(n_rows, -1).astype(BF) for r in (o0, o1, o2)], 1)
    grad_o = dot_tn(mixed, dbranch).astype(BF)
    for s in range(shards):
        block = grad_o[s * rows:(s + 1) * rows]
        at = place(s, oo) ^ p_o
        go_keep[at] = jnp.where(first_core, block[:, :half], block[:, half:])
        go_send[at] = jnp.where(first_core, block[:, half:], block[:, :half])


def attend_back_kernel(
    order, shards, aliased,
    scal, e_ref, dm_ref, q_ref, k_ref, v_ref, o_ref, inv_ref, xt_ref, *rest,
):
    if aliased:
        rest = rest[1:]
    (gp_ref, g_keep, g_send, dq_ref, dkv_ref, vg_ref,
     vt_s, qt_s, dmt_s, dmi_s, dl_s, dkt_s, dvt_s, dq_s) = rest
    s, h = pl.program_id(0), pl.program_id(1)
    pm, mc, core = scal[0], scal[1], scal[2]
    shard, cols = q_ref.shape[1:]
    length = k_ref.shape[1]
    head = cols // 4
    seqs = dq_ref.shape[0]

    @pl.when(h == 0)
    def _():
        vt_s[...] = v_ref[0].T
        dmi = (dm_ref[0].astype(F32) * inv_ref[0]).astype(BF)
        dmi_s[...] = dmi
        dl_s[...] = dmi.astype(F32) * o_ref[0]
        qt_s[...] = q_ref[0].T
        dmt_s[...] = dmi.T

    lane = lax.broadcasted_iota(jnp.int32, (shard, cols), 1) // head
    this = lane == h
    dmm = jnp.where(this, dmi_s[...].astype(F32), 0.0).astype(BF)
    delta = jnp.sum(jnp.where(this, dl_s[...], 0.0), -1, keepdims=True)
    step = 64
    for r in range(0, shard, step):
        dp = dot(dmm[r:r + step], vt_s[...])
        gp_ref[0, 0, r:r + step, :] = (
            e_ref[0, 0, r:r + step, :].astype(F32) * (dp - delta[r:r + step])
        ).astype(BF)
    g = gp_ref[0, 0]
    dq = dot(g, k_ref[0]) * (1.0 / math.sqrt(head))
    dq_s[s] = jnp.where(this, dq, dq_s[s])
    at = pl.multiple_of(h * head, head)
    dkt_s[pl.ds(at, head), :] = dot(qt_s[pl.ds(at, head), :], g).astype(BF)
    dvt_s[pl.ds(at, head), :] = dot(dmt_s[pl.ds(at, head), :], e_ref[0, 0]).astype(BF)

    @pl.when(h == 3)
    def _():
        dq_ref[s] = dq_s[s].astype(BF)
        dkv_ref[s, :, :cols] = dkt_s[...].T
        dkv_ref[s, :, cols:] = dvt_s[...].T

    @pl.when((h == 3) & (s == seqs - 1))
    def _():
        grad_kv = None
        grad_q = None
        ones = jnp.ones((8, length), BF)
        sum_v = None
        sum_q = None
        for i in range(seqs):
            part = dot(xt_ref[i], dkv_ref[i])
            grad_kv = part if i == 0 else grad_kv + part
            mine = pl.multiple_of(mc * shard, shard)
            part = dot(xt_ref[i, :, pl.ds(mine, shard)], dq_ref[i])
            grad_q = part if i == 0 else grad_q + part
            part = dot(ones, dkv_ref[i, :, cols:])
            sum_v = part if i == 0 else sum_v + part
            part = dot(ones[:, :shard], dq_ref[i])
            sum_q = part if i == 0 else sum_q + part
        vg_ref[0:1, :] = sum_q[0:1]
        vg_ref[1:2, :] = sum_v[0:1]
        grad = jnp.concatenate([grad_q.astype(BF), grad_kv.astype(BF)], 1)
        rows = g_keep.shape[1]
        half = g_keep.shape[2]
        first_core = core == 0
        for i in range(shards):
            block = grad[i * rows:(i + 1) * rows]
            to = place(i, order) ^ pm
            g_keep[to] = jnp.where(first_core, block[:, :half], block[:, half:])
            g_send[to] = jnp.where(first_core, block[:, half:], block[:, :half])


def token_kernel(
    order, shards,
    scal, dq0, dq1, dq2, dkv0, dkv1, dkv2, own0, got0, own1, got1, own2, got2, dsum1,
    p0, p1, p2, p3, w_s,
):
    pms, mc, core = scal[0], scal[1], scal[2]
    rows, half = own0.shape[1:]
    seqs, shard, cols = dq0.shape
    first_core = core == 0
    for g, (own, got) in enumerate(((own0, got0), (own1, got1), (own2, got2))):
        for i in range(shards):
            at = place(i, order) ^ pms
            mine, other = own[at, :, :half], got[at, :, :half]
            w_s[g, i * rows:(i + 1) * rows, :half] = jnp.where(first_core, mine, other)
            w_s[g, i * rows:(i + 1) * rows, half:] = jnp.where(first_core, other, mine)
    for j, out in reversed(list(enumerate((p0, p1, p2, p3)))):
        where = pl.multiple_of((mc ^ j) * shard, shard)
        for s in range(seqs):
            total = None
            for g, (dq, dkv) in enumerate(((dq0, dkv0), (dq1, dkv1), (dq2, dkv2))):
                part = dot_nt(dkv[s, pl.ds(where, shard), :], w_s[g, :, cols:])
                if j == 0:
                    part = part + dot_nt(dq[s], w_s[g, :, :cols])
                total = part if total is None else total + part
            if j == 0:
                total = total + dsum1[s * shard:(s + 1) * shard, :]
            out[s] = total.astype(out.dtype)


def on_device(
    n, order,
    tokens, prior_logits, doc_ids, w_query, w_key, w_value, w_out, b_query, b_value, b_out,
    first_norm_gain, norm1_shift, w_in, b_in, w_down, b_down, norm2_gain, norm2_shift, cotangent,
):
    seqs, shard, width = tokens.shape
    heads, length = prior_logits.shape[1], prior_logits.shape[3]
    ctx = length // shard
    head = width // heads
    rows = w_query.shape[0]
    ff = w_in.shape[1]
    sub = w_down.shape[0] // 4
    cols = width // GROUPS
    per = heads // GROUPS
    half = (3 * cols) // 2
    n_rows = seqs * shard
    me_s = lax.axis_index("seq")
    me_c = lax.axis_index("ctx")
    core, my_y = me_c & 1, me_c >> 1
    pm = place(me_s, order)
    scal = jnp.stack([pm, me_c, core, pm, pm, pm]).astype(jnp.int32)
    own_core = core == 0

    docs = jnp.pad(doc_ids.astype(BF)[:, None, :], ((0, 0), (0, 15), (0, width - shard)))
    tok0 = jnp.concatenate([tokens, docs], 1)
    tok2 = swap(tok0, "ctx", ctx, 1)
    both = swap(jnp.stack([tok0, tok2]), "ctx", ctx, 0)
    tok = (tok0, both[0], tok2, both[1])
    doc_col = doc_ids.astype(F32)[:, :, None]

    vec = jnp.concatenate(
        [b_query, b_value, b_out, first_norm_gain, norm1_shift, b_down, norm2_gain, norm2_shift, b_in])[None]
    vec = gather_seq(vec, n, order)[:, 0]
    spots = place(jnp.arange(n), order) ^ pm
    vec = jnp.take(vec, spots, axis=0).astype(F32)
    small = vec[:, :8 * rows].reshape(n, 8, rows).transpose(1, 0, 2).reshape(8, width)
    bin_all = vec[:, 8 * rows:].reshape(n, 2, 2, sub).transpose(2, 1, 0, 3).reshape(4, 1, n * sub)
    vecs = small[2:8]

    def tile(g):
        cut = slice(g * cols, (g + 1) * cols)
        parts = [w_query[:, cut], w_key[:, cut], w_value[:, cut]]
        whole = jnp.concatenate(parts, 1)
        return jnp.where(own_core, whole[:, :half], whole[:, half:])

    def o_tile():
        return jnp.where(own_core, w_out[:, :half], w_out[:, half:])

    tiles = [tile(g) for g in range(GROUPS)] + [o_tile()]
    own = [gather_seq(t, n, order) for t in tiles]
    got = [swap(o, "ctx", ctx, 0) for o in own]

    in_part = w_in.reshape(rows, n, 2, 2, sub)
    in_part = lax.dynamic_slice(in_part, (0, 0, core, my_y, 0), (rows, n, 1, 1, sub)).reshape(rows, n * sub)
    in0 = gather_seq(in_part, n, order)
    in2 = swap(in0, "ctx", ctx, 1)
    in1 = swap(in0, "ctx", ctx, 0)
    in3 = swap(in2, "ctx", ctx, 0)
    down_part = lax.dynamic_slice(w_down.reshape(2, 2 * sub, width), (core, 0, 0), (1, 2 * sub, width))[0]
    d_own = gather_seq(down_part, n, order)
    d_got = swap(d_own, "ctx", ctx, 0).reshape(n, 2, sub, width)
    d_own = d_own.reshape(n, 2, sub, width)

    sds = jax.ShapeDtypeStruct
    x_t = pl.pallas_call(
        turn_kernel,
        out_shape=sds((seqs, width, length), BF),
        in_specs=[smem()] + [vmem()] * 4,
        out_specs=vmem(),
        compiler_params=params(),
        name="turn",
    )(scal, *tok)

    def per_seq(rows_, cols_):
        return pl.BlockSpec((1, rows_, cols_), lambda s, h: (s, 0, 0))

    def big(g):
        return pl.BlockSpec((1, 1, shard, length), lambda s, h: (s, g * per + h, 0, 0))

    local_big = pl.BlockSpec((1, 1, shard, length), lambda s, h: (s, h, 0, 0))
    raw = None
    kept = []
    for g in range(GROUPS):
        bias = jnp.zeros((8, cols), F32).at[0].set(small[0, g * cols:(g + 1) * cols]).at[1].set(
            small[1, g * cols:(g + 1) * cols])
        args = [scal, *tok, doc_col, own[g], got[g], bias, prior_logits]
        specs = [smem()] + [vmem()] * 4 + [per_seq(shard, 1), vmem(), vmem(), vmem(), big(g)]
        alias = {}
        if raw is not None:
            alias = {len(args): 0}
            args.append(raw)
            specs.append(pl.BlockSpec(memory_space=ANY))
        raw, *rest = pl.pallas_call(
            functools.partial(attend_kernel, order, n, raw is not None),
            grid=(seqs, per),
            out_shape=[
                sds(prior_logits.shape, BF),
                sds((seqs, per, shard, length), BF),
                sds((seqs, shard, cols), BF),
                sds((seqs, length, cols), BF),
                sds((seqs, length, cols), BF),
                sds((seqs, shard, cols), F32),
                sds((seqs, shard, cols), F32),
            ],
            in_specs=specs,
            out_specs=[big(g), local_big, per_seq(shard, cols), per_seq(length, cols), per_seq(length, cols),
                       per_seq(shard, cols), per_seq(shard, cols)],
            scratch_shapes=[VM((width, 3 * cols), BF), VM((cols, length), BF), VM((shard, length), F32)],
            input_output_aliases=alias,
            compiler_params=params(2),
            name=f"attend{g}",
        )(*args)
        kept.append(rest)

    weights = [own[3], got[3], in0, in1, in2, in3, d_own, d_got]
    weight_specs = [vmem(), vmem()] + [pl.BlockSpec(memory_space=ANY)] * 6
    weight_scratch = [VM((width, width), BF), VM((4, width, n * sub), BF), VM((4, n * sub, width), BF)]
    o_parts = [k[4] for k in kept]
    output, first_n, inv1, inner, hid, dg, dsum2, dsec, vg2 = pl.pallas_call(
        functools.partial(forward_kernel, order, order, order, n),
        out_shape=[
            sds((seqs, shard, width), BF), sds((n_rows, width), F32), sds((n_rows, 1), F32), sds((n_rows, width), BF),
            sds((4, n_rows, n * sub), BF), sds((4, n_rows, n * sub), BF), sds((n_rows, width), F32),
            sds((n_rows, width), BF), sds((8, width), F32),
        ],
        in_specs=[smem()] + [vmem()] * 7 + weight_specs,
        out_specs=[vmem()] * 9,
        scratch_shapes=weight_scratch + [VM((n_rows, width), F32), VM((n_rows, width), F32),
                                         pltpu.SemaphoreType.DMA((8 * n,))],
        compiler_params=params(),
        name="ff_fwd",
    )(scal, *o_parts, tokens, cotangent, vecs, bin_all, *weights)

    gi0, gi1, gi2, gi3, gd_keep, gd_send, go_keep, go_send, dsum1, dmix, vg1, gbin = pl.pallas_call(
        functools.partial(backward_kernel, order, order, order, n),
        out_shape=[sds((n, rows, n * sub), BF)] * 4 + [sds((n, 2, sub, width), BF)] * 2
        + [sds((n, rows, half), BF)] * 2 + [
            sds((n_rows, width), F32), sds((seqs, shard, width), BF), sds((8, width), F32), sds((4, 1, n * sub), F32)],
        in_specs=[smem()] + [vmem()] * 11 + weight_specs,
        out_specs=[vmem()] * 12,
        scratch_shapes=weight_scratch + [VM((n_rows, width), F32), pltpu.SemaphoreType.DMA((8 * n,))],
        compiler_params=params(),
        name="ff_bwd",
    )(scal, *o_parts, first_n, inv1, inner, hid, dg, dsum2, dsec, vecs, *weights)

    def add(a, b):
        return (a.astype(F32) + b.astype(F32)).astype(BF)

    gd = add(gd_keep, swap(gd_send, "ctx", ctx, 0)).reshape(n, 2 * sub, width)
    gd = reduce_seq(gd, n, order)[0]
    gd = add(gd, swap(gd, "ctx", ctx, 1))
    gd_other = swap(gd, "ctx", ctx, 0)
    grad_w_down = jnp.where(own_core, jnp.concatenate([gd, gd_other]), jnp.concatenate([gd_other, gd])).astype(F32)

    gi_a = add(gi0, swap(gi1, "ctx", ctx, 0))
    gi_b = add(gi2, swap(gi3, "ctx", ctx, 0))
    gi = add(gi_a, swap(gi_b, "ctx", ctx, 1))
    gi = reduce_seq(gi, n, order)[0]
    gi_y = swap(gi, "ctx", ctx, 1)
    pair = jnp.where(my_y == 0, jnp.stack([gi, gi_y]), jnp.stack([gi_y, gi]))
    pair_other = swap(pair, "ctx", ctx, 0)
    quad = jnp.where(own_core, jnp.stack([pair, pair_other]), jnp.stack([pair_other, pair]))
    grad_w_in = quad.reshape(2, 2, rows, n, sub).transpose(2, 3, 0, 1, 4).reshape(rows, ff).astype(F32)

    def finish(keep, send):
        held = add(keep, swap(send, "ctx", ctx, 0))
        held = reduce_seq(held, n, order)[0]
        held = add(held, swap(held, "ctx", ctx, 1))
        other = swap(held, "ctx", ctx, 0)
        lo = jnp.where(own_core, held, other)
        hi = jnp.where(own_core, other, held)
        return jnp.concatenate([lo, hi], 1).astype(F32)

    grad_w_out = finish(go_keep, go_send)

    gp = None
    grads, dqs, dkvs, vgs = [], [], [], []
    for g in range(GROUPS):
        e, q, k, v, o, inv = kept[g]
        args = [scal, e, dmix, q, k, v, o, inv, x_t]
        specs = [smem(), local_big, pl.BlockSpec((1, shard, cols), lambda s, h, g=g: (s, 0, g)),
                 per_seq(shard, cols), per_seq(length, cols), per_seq(length, cols), per_seq(shard, cols),
                 per_seq(shard, cols), vmem()]
        alias = {}
        if gp is not None:
            alias = {len(args): 0}
            args.append(gp)
            specs.append(pl.BlockSpec(memory_space=ANY))
        gp, keep, send, dq, dkv, vg = pl.pallas_call(
            functools.partial(attend_back_kernel, order, n, gp is not None),
            grid=(seqs, per),
            out_shape=[
                sds(prior_logits.shape, BF), sds((n, rows, half), BF), sds((n, rows, half), BF),
                sds((seqs, shard, cols), BF), sds((seqs, length, 2 * cols), BF), sds((8, cols), F32),
            ],
            in_specs=specs,
            out_specs=[big(g)] + [vmem()] * 5,
            scratch_shapes=[
                VM((cols, length), BF), VM((cols, shard), BF), VM((cols, shard), BF), VM((shard, cols), BF),
                VM((shard, cols), F32), VM((cols, length), BF), VM((cols, length), BF), VM((seqs, shard, cols), F32),
            ],
            input_output_aliases=alias,
            compiler_params=params(2),
            name=f"attend_back{g}",
        )(*args)
        grads.append(finish(keep, send))
        dqs.append(dq)
        dkvs.append(dkv)
        vgs.append(vg)

    pieces = pl.pallas_call(
        functools.partial(token_kernel, order, n),
        out_shape=[sds((seqs, shard, width), F32)] + [sds((seqs, shard, width), BF)] * 3,
        in_specs=[smem()] + [vmem()] * 13,
        out_specs=[vmem()] * 4,
        scratch_shapes=[VM((GROUPS, width, 3 * cols), BF)],
        compiler_params=params(),
        name="token_grad",
    )(scal, *dqs, *dkvs, own[0], got[0], own[1], got[1], own[2], got[2], dsum1)
    from_core = swap(jnp.stack([pieces[1], pieces[3]]), "ctx", ctx, 0)
    across = add(pieces[2], from_core[1])
    grad_tokens = pieces[0] + from_core[0].astype(F32) + swap(across, "ctx", ctx, 1).astype(F32)

    def by_shard(row):
        return row.reshape(n, rows)

    sums = [
        jnp.concatenate([vg[0] for vg in vgs]), jnp.concatenate([vg[1] for vg in vgs]),
        vg1[2], vg1[0], vg1[1], vg2[2], vg2[0], vg2[1],
    ]
    bin_nat = gbin.reshape(2, 2, n, sub).transpose(2, 1, 0, 3).reshape(n, 4 * sub)
    table = jnp.concatenate([by_shard(v) for v in sums] + [bin_nat], 1)
    back = place(jnp.arange(n), order)
    inverse_spots = [0] * n
    for i in range(n):
        inverse_spots[place(i, order)] = i
    table = jnp.take(table, jnp.array(inverse_spots) ^ me_s, axis=0)
    del back
    table = reduce_seq(table, n, order)[0]
    table = table + swap(table, "ctx", ctx, 1)
    table = table + swap(table, "ctx", ctx, 0)
    cut = [table[i * rows:(i + 1) * rows] for i in range(8)]
    g_bq, g_bv, g_bo, g_g1, g_s1, g_bd, g_g2, g_s2 = cut
    g_bin = table[8 * rows:]

    def columns(i):
        return jnp.concatenate([gr[:, i * cols:(i + 1) * cols] for gr in grads], 1)

    return (
        output, raw, grad_tokens, gp,
        columns(0), columns(1), columns(2), grad_w_out,
        g_bq, g_bv, g_bo, g_g1, g_s1, grad_w_in, g_bin, grad_w_down, g_bd, g_g2, g_s2,
    )


def solution(mesh):
    n = mesh.shape["seq"]
    order = tuple(reversed(range(n.bit_length() - 1)))
    in_specs = (
        P("seq", "ctx", None), P("seq", None, "ctx", None), P("seq", "ctx"),
        P("seq", None), P("seq", None), P("seq", None), P("seq", None),
        P("seq"), P("seq"), P("seq"), P("seq"), P("seq"),
        P("seq", None), P("seq"), P("seq", None), P("seq"), P("seq"), P("seq"),
        P("seq", "ctx", None),
    )
    out_specs = (
        P("seq", "ctx", None), P("seq", None, "ctx", None), P("seq", "ctx", None), P("seq", None, "ctx", None),
        P("seq", None), P("seq", None), P("seq", None), P("seq", None),
        P("seq"), P("seq"), P("seq"), P("seq"), P("seq"),
        P("seq", None), P("seq"), P("seq", None), P("seq"), P("seq"), P("seq"),
    )
    return jax.shard_map(
        functools.partial(on_device, n, order),
        mesh=mesh, in_specs=in_specs, out_specs=out_specs, check_vma=False,
    )
```

```python
import functools
import math

import jax
import jax.numpy as jnp
from jax import lax
from jax.experimental import pallas as pl
from jax.experimental.pallas import tpu as pltpu
from jax.sharding import PartitionSpec as P

EPSILON = 1e-05
NEGATIVE = -1e30
BF = jnp.bfloat16
F32 = jnp.float32
VM = pltpu.VMEM
ANY = pl.ANY
VMEM_LIMIT = 60 * 1024 * 1024
GROUPS = 3


def dot(a, b):
    return lax.dot_general(a, b, (((1,), (0,)), ((), ())), preferred_element_type=F32)


def dot_nt(a, b):
    return lax.dot_general(a, b, (((1,), (1,)), ((), ())), preferred_element_type=F32)


def dot_tn(a, b):
    return lax.dot_general(a, b, (((0,), (0,)), ((), ())), preferred_element_type=F32)


def vmem(shape=None, index=None):
    if shape is None:
        return pl.BlockSpec(memory_space=VM)
    return pl.BlockSpec(shape, index)


def params(n_grid=0):
    return pltpu.CompilerParams(
        vmem_limit_bytes=VMEM_LIMIT,
        dimension_semantics=("arbitrary",) * n_grid if n_grid else None,
    )


def smem():
    return pl.BlockSpec(memory_space=pltpu.SMEM)


def after(value, *marks):
    return lax.optimization_barrier((value, *marks))[0]


def swap_by(value, axis, size, step):
    return lax.ppermute(value, axis, [(i, i ^ step) for i in range(size)])


def swap(value, axis, size, bit):
    return swap_by(value, axis, size, 1 << bit)


def far_steps(far):
    a, b = 1 << far[0], 1 << far[1]
    return (a, b, a | b)


def add(*parts):
    total = parts[0].astype(F32)
    for part in parts[1:]:
        total = total + part.astype(F32)
    return total.astype(BF)


def place(index, order):
    out = 0
    for step, bit in enumerate(order):
        out = out | (((index >> bit) & 1) << step)
    return out


def prep_kernel(scal, tok, docs, wq, wk, wv, wo, wi, wd, *rest):
    vecs, (a0, rest_w, ffq, tok_ref) = rest[:9], rest[9:]
    mc, core = scal[1], scal[2]
    my_y = mc >> 1
    rows, width = wq.shape
    half = a0.shape[1]
    cols = (2 * half) // 3
    cut = half - cols
    low = core == 0
    sub = ffq.shape[1]
    seqs, shard = tok.shape[:2]

    def pick(g):
        at = g * cols
        first = jnp.concatenate([wq[:, at:at + cols], wk[:, at:at + cut]], 1)
        second = jnp.concatenate([wk[:, at + cut:at + cols], wv[:, at:at + cols]], 1)
        return jnp.where(low, first, second)

    a0[:rows] = pick(0)
    a0[rows:] = jnp.zeros_like(a0[rows:])
    table = jnp.zeros((16, half), F32)
    p = 0
    lines = []
    line = []
    for v in vecs:
        step = rows if v.shape[1] == rows else v.shape[1] // 4
        for i in range(v.shape[1] // step):
            line.append(v[:, i * step:(i + 1) * step].astype(F32))
            p += step
            if p % half == 0:
                lines.append(jnp.concatenate(line, 1))
                line = []
    if line:
        line.append(jnp.zeros((1, half - p % half), F32))
        lines.append(jnp.concatenate(line, 1))
    lines.append(jnp.zeros((16 - len(lines), half), F32))
    a0[rows:] = jnp.concatenate(lines, 0).astype(BF)
    del table
    rest_w[:, :half] = pick(1)
    rest_w[:, half:2 * half] = pick(2)
    rest_w[:, 2 * half:] = jnp.where(low, wo[:, :half], wo[:, half:])
    block = 2 * core + my_y
    ffq[1] = wd[pl.ds(pl.multiple_of(block * sub, sub), sub), :]
    for s in range(width // sub):
        got = [wi[:, (4 * s + b) * sub:(4 * s + b + 1) * sub] for b in range(4)]
        near = jnp.where(my_y == 0, got[0], got[1])
        far = jnp.where(my_y == 0, got[2], got[3])
        ffq[0, :, s * sub:(s + 1) * sub] = jnp.where(low, near, far)
    for s in range(seqs):
        tok_ref[s, :shard, :] = tok[s]
        tok_ref[s, shard:, :] = jnp.zeros_like(tok_ref[s, shard:, :])
        tok_ref[s, shard:shard + 1, :shard] = docs[s:s + 1, :].astype(F32).astype(BF)


def join_kernel(a, b, c, d, out):
    lead = out.ndim == 4
    for i, ref in enumerate((a, b, c, d)):
        if lead:
            out[:, i] = ref[...]
        else:
            out[i] = ref[...]


def fetch(lo, hi, at):
    m = lo.shape[0]
    return jnp.where(at < m, lo[at & (m - 1)], hi[at & (m - 1)])


def weights_in(out, order, pm, core, rows, shards, own, got, at_col, half):
    first = core == 0
    for i in range(shards):
        at = place(i, order) ^ pm
        m = own[0].shape[0]
        pick = lambda ref: ref[at & (m - 1), :rows, at_col:at_col + half]
        in_lo = at < m
        mine = jnp.where(in_lo, pick(own[0]), pick(own[1]))
        other = jnp.where(in_lo, pick(got[0]), pick(got[1]))
        out[i * rows:(i + 1) * rows, :half] = jnp.where(first, mine, other)
        out[i * rows:(i + 1) * rows, half:2 * half] = jnp.where(first, other, mine)


def vector_kernel(order, shards, rows, sub, scal, lo, hi, vec_ref, bin_ref):
    pm = scal[0]
    half = lo.shape[2]
    m = lo.shape[0]
    for s in range(shards):
        at = place(s, order) ^ pm
        block = jnp.where(at < m, lo[at & (m - 1), rows:, :], hi[at & (m - 1), rows:, :]).astype(F32)
        for i in range(8):
            p = i * rows
            vec_ref[i:i + 1, s * rows:(s + 1) * rows] = block[p // half:p // half + 1, p % half:p % half + rows]
        for b in range(4):
            p = 8 * rows + b * sub
            c = 2 * (b & 1) + (b >> 1)
            bin_ref[c, :, s * sub:(s + 1) * sub] = block[p // half:p // half + 1, p % half:p % half + sub]


def turn_kernel(scal, t0, t1, t2, t3, out_ref):
    mc = scal[1]
    seqs, _, width = t0.shape
    shard = out_ref.shape[2] // 4
    for j, tok in enumerate((t0, t1, t2, t3)):
        where = pl.multiple_of((mc ^ j) * shard, shard)
        for s in range(seqs):
            out_ref[s, :, pl.ds(where, shard)] = tok[s, :shard, :].T


def attend_kernel(
    order, shards, seq, group, aliased,
    scal, t0, t1, t2, t3, doc_ref, own_lo, own_hi, got_lo, got_hi, bias_ref, prior_ref, *rest,
):
    if aliased:
        rest = rest[1:]
    raw_ref, e_ref, q_ref, k_ref, v_ref, o_ref, inv_ref, w_s, kt_s, mask_s, vx_s = rest
    h = pl.program_id(0)
    pm, mc, core = scal[0], scal[1], scal[2]
    rows = w_s.shape[0] // shards
    half = w_s.shape[1] // 2
    shard, cols = q_ref.shape
    head = cols // 4

    @pl.when(h == 0)
    def _():
        weights_in(w_s, order, pm, core, rows, shards, (own_lo, own_hi), (got_lo, got_hi), 0, half)
        q = dot(t0[0, :shard, :], w_s[:, :cols]) + bias_ref[0:1, :]
        q_ref[...] = (q.astype(BF).astype(F32) * (1.0 / math.sqrt(head))).astype(BF)
        mine = jnp.broadcast_to(doc_ref[seq:seq + 1, :].astype(F32), (128, shard)).T[:, :1]
        for j, tok in enumerate((t0, t1, t2, t3)):
            where = pl.multiple_of((mc ^ j) * shard, shard)
            kv = dot(tok[0, :shard, :], w_s[:, cols:])
            k_ref[pl.ds(where, shard), :] = kv[:, :cols].astype(BF)
            v = kv[:, cols:] + bias_ref[1:2, :]
            v_ref[pl.ds(where, shard), :] = v.astype(BF)
            even = (lax.broadcasted_iota(jnp.int32, (shard, cols), 1) // head) % 2 == 0
            vx_s[0, pl.ds(where, shard), :] = jnp.where(even, v, 1.0).astype(BF)
            vx_s[1, pl.ds(where, shard), :] = jnp.where(even, 1.0, v).astype(BF)
            docs = tok[0, shard:shard + 1, :shard].astype(F32)
            mask_s[:, pl.ds(where, shard)] = jnp.where(mine == docs, 0.0, NEGATIVE)
        kt_s[...] = k_ref[...].T

    lane = lax.broadcasted_iota(jnp.int32, (shard, cols), 1) // head
    this = lane == h
    qm = jnp.where(this, q_ref[...].astype(F32), 0.0).astype(BF)
    step = 64
    for r in range(0, shard, step):
        logits = dot(qm[r:r + step], kt_s[...]) + prior_ref[0, 0, r:r + step, :].astype(F32)
        raw_ref[0, 0, r:r + step, :] = logits.astype(BF)
        masked = logits + mask_s[r:r + step, :]
        top = jnp.max(masked, -1, keepdims=True)
        e_ref[0, r:r + step, :] = jnp.exp(masked - top).astype(BF)
    o = dot(e_ref[0], vx_s[h & 1])
    total = jnp.max(jnp.where(lane == (h ^ 1), o, 0.0), -1, keepdims=True)
    inv = 1.0 / total
    o_ref[...] = jnp.where(this, o * inv, o_ref[...])
    inv_ref[...] = jnp.where(this, inv, inv_ref[...])


def gelu_parts(x):
    z = jnp.abs(x) * 0.7071067811865476
    t = 1.0 / (1.0 + 0.3275911 * z)
    e = jnp.exp(-0.5 * x * x)
    poly = t * (0.254829592 + t * (-0.284496736 + t * (1.421413741 + t * (-1.453152027 + t * 1.061405429))))
    tail = 0.5 * poly * e
    phi = jnp.where(x >= 0, 1.0 - tail, tail)
    return x * phi, phi + x * (e * 0.3989422804014327)


def moments(x):
    mean = jnp.mean(x, -1, keepdims=True)
    centered = x - mean
    inverse = lax.rsqrt(jnp.mean(centered * centered, -1, keepdims=True) + EPSILON)
    return centered * inverse, inverse


def norm_back(grad, normed, inverse, gain):
    scaled = grad * gain
    return inverse * (
        scaled - jnp.mean(scaled, -1, keepdims=True)
        - normed * jnp.mean(scaled * normed, -1, keepdims=True)
    )


def block_copy(lo, hi, at, dst, sem):
    m = lo.shape[0]
    spot = at & (m - 1)

    @pl.when(at < m)
    def _():
        pltpu.make_async_copy(lo.at[spot], dst, sem).start()

    @pl.when(at >= m)
    def _():
        pltpu.make_async_copy(hi.at[spot], dst, sem).start()

    return pltpu.make_async_copy(lo.at[spot], dst, sem)


def ff_sources(f, which):
    lo, hi, ylo, yhi_i, yhi_d, clo, chi, cylo, cyhi_i, cyhi_d = f
    yhi, cyhi = (yhi_i, cyhi_i) if which == 0 else (yhi_d, cyhi_d)
    return [(lo.at[which], hi.at[which]), (clo.at[which], chi.at[which]),
            (ylo.at[which], yhi), (cylo.at[which], cyhi)]


def ff_copies(f, which, dst, order, pm, shards, rows, sem):
    out = []
    for j, (lo, hi) in enumerate(ff_sources(f, which)):
        out.append([block_copy(lo, hi, place(s, order) ^ pm, dst.at[j, pl.ds(s * rows, rows)], sem.at[j * shards + s])
                    for s in range(shards)])
    return out


def forward_kernel(
    order, shards,
    scal, o00, o01, o10, o11, o20, o21, tok_ref, cot_ref, vec_ref, bin_ref, wl, wh, wgl, wgh, *rest,
):
    f, rest = rest[:10], rest[10:]
    (out_ref, mix_ref, first_n_ref, inv1_ref, inner_ref, hid_ref, dg_ref, dsum2_ref, dsec_ref, vg_ref,
     wo_s, wi_s, wd_s, first_s, acc_s, isem, dsem) = rest
    pm, mc, core = scal[0], scal[1], scal[2]
    seqs, shard, width = tok_ref.shape
    rows = width // shards
    n_rows = seqs * shard
    in_copies = ff_copies(f, 0, wi_s, order, pm, shards, rows, isem)
    down_copies = ff_copies(f, 1, wd_s, order, pm, shards, rows, dsem)
    weights_in(wo_s, order, pm, core, rows, shards, (wl, wh), (wgl, wgh), 0, width // 2)
    mixed = jnp.concatenate(
        [jnp.concatenate([a[...].astype(BF), b[...].astype(BF)], 0) for a, b in ((o00, o01), (o10, o11), (o20, o21))], 1)
    mix_ref[...] = mixed
    tokens = tok_ref[...].reshape(n_rows, width).astype(F32)
    normed, inverse = moments(tokens + (dot(mixed, wo_s[...]) + vec_ref[2:3, :]))
    first_n_ref[...] = normed
    inv1_ref[...] = inverse
    first = normed * vec_ref[3:4, :] + vec_ref[4:5, :]
    first_s[...] = first
    inner_ref[...] = first.astype(BF)
    for j in range(4):
        for c in in_copies[j]:
            c.wait()
        for r in range(0, n_rows, 128):
            pre = dot(inner_ref[r:r + 128, :], wi_s[j]) + bin_ref[mc ^ j]
            hid, dg = gelu_parts(pre)
            hid_ref[j, r:r + 128, :] = hid.astype(BF)
            dg_ref[j, r:r + 128, :] = dg.astype(BF)
        for c in down_copies[j]:
            c.wait()
        part = dot(hid_ref[j], wd_s[j])
        acc_s[...] = part if j == 0 else acc_s[...] + part
    normed, inverse = moments(first_s[...] + (acc_s[...] + vec_ref[5:6, :]))
    gain = vec_ref[6:7, :]
    out_ref[...] = (normed * gain + vec_ref[7:8, :]).astype(BF).reshape(seqs, shard, width)
    dy = cot_ref[...].reshape(n_rows, width).astype(F32)
    dsum2 = norm_back(dy, normed, inverse, gain)
    dsum2_ref[...] = dsum2
    dsec = dsum2.astype(BF)
    dsec_ref[...] = dsec
    vg_ref[0:1, :] = jnp.sum(dy * normed, 0, keepdims=True)
    vg_ref[1:2, :] = jnp.sum(dy, 0, keepdims=True)
    vg_ref[2:3, :] = jnp.sum(dsec.astype(F32), 0, keepdims=True)


def down_grad_kernel(order, shards, scal, hid, dsec, keep, send):
    pm = scal[0]
    sub = keep.shape[2]
    for j in (1, 3, 0, 2):
        out = keep if j % 2 == 0 else send
        grad = dot_tn(hid[j], dsec[...]).astype(BF)
        for s in range(shards):
            out[j >> 1, place(s, order) ^ pm] = grad[s * sub:(s + 1) * sub]


def in_grad_kernel(order, shards, scal, inner, dg, dsec, *rest):
    f, (keep, send, dpre_ref, gbin_ref, wd_s, sem) = rest[:10], rest[10:]
    pm, mc = scal[0], scal[1]
    rows = keep.shape[2]
    down_copies = ff_copies(f, 1, wd_s, order, pm, shards, rows, sem)
    for j in (1, 3, 0, 2):
        out = keep if j % 2 == 0 else send
        for c in down_copies[j]:
            c.wait()
        dpre = (dot_nt(dsec[...], wd_s[j]) * dg[j].astype(F32)).astype(BF)
        dpre_ref[j] = dpre
        gbin_ref[mc ^ j] = jnp.sum(dpre.astype(F32), 0, keepdims=True)
        grad = dot_tn(inner[...], dpre).astype(BF)
        for s in range(shards):
            out[j >> 1, place(s, order) ^ pm] = grad[s * rows:(s + 1) * rows]


def first_grad_kernel(
    order, shards, scal, mix_ref, first_n, inv1, dpre, dsum2, vec_ref, wl, wh, wgl, wgh, *rest,
):
    f, (go_keep, go_send, dsum1_ref, dmix_ref, vg_ref, wo_s, wi_s, sem) = rest[:10], rest[10:]
    pm, core = scal[0], scal[2]
    n_rows, width = dsum2.shape
    rows = width // shards
    half = width // 2
    in_copies = ff_copies(f, 0, wi_s, order, pm, shards, rows, sem)
    weights_in(wo_s, order, pm, core, rows, shards, (wl, wh), (wgl, wgh), 0, half)
    dfirst = dsum2[...]
    for j in range(4):
        for c in in_copies[j]:
            c.wait()
        dfirst = dfirst + dot_nt(dpre[j], wi_s[j])
    normed = first_n[...]
    dsum1 = norm_back(dfirst, normed, inv1[...], vec_ref[3:4, :])
    dsum1_ref[...] = dsum1
    dbranch = dsum1.astype(BF)
    vg_ref[0:1, :] = jnp.sum(dfirst * normed, 0, keepdims=True)
    vg_ref[1:2, :] = jnp.sum(dfirst, 0, keepdims=True)
    vg_ref[2:3, :] = jnp.sum(dbranch.astype(F32), 0, keepdims=True)
    dmix_ref[...] = dot_nt(dbranch, wo_s[...]).astype(BF)
    grad_o = dot_tn(mix_ref[...], dbranch).astype(BF)
    first_core = core == 0
    for s in range(shards):
        block = grad_o[s * rows:(s + 1) * rows]
        at = place(s, order) ^ pm
        go_keep[at] = jnp.where(first_core, block[:, :half], block[:, half:])
        go_send[at] = jnp.where(first_core, block[:, half:], block[:, :half])


def attend_back_kernel(
    aliased,
    scal, e_ref, dm_ref, q_ref, k_ref, v_ref, o_ref, inv_ref, *rest,
):
    if aliased:
        rest = rest[1:]
    gp_ref, dq_ref, dkv_ref, vt_s, qt_s, dmt_s, dmi_s, dl_s, dkt_s, dvt_s, dq_s = rest
    h = pl.program_id(0)
    shard, cols = q_ref.shape
    head = cols // 4

    @pl.when(h == 0)
    def _():
        vt_s[...] = v_ref[...].T
        dmi = (dm_ref[...].astype(F32) * inv_ref[...]).astype(BF)
        dmi_s[...] = dmi
        dl_s[...] = dmi.astype(F32) * o_ref[...]
        qt_s[...] = q_ref[...].T
        dmt_s[...] = dmi.T

    lane = lax.broadcasted_iota(jnp.int32, (shard, cols), 1) // head
    this = lane == h
    dmm = jnp.where(this, dmi_s[...].astype(F32), 0.0).astype(BF)
    delta = jnp.sum(jnp.where(this, dl_s[...], 0.0), -1, keepdims=True)
    step = 64
    for r in range(0, shard, step):
        dp = dot(dmm[r:r + step], vt_s[...])
        gp_ref[0, 0, r:r + step, :] = (
            e_ref[0, r:r + step, :].astype(F32) * (dp - delta[r:r + step])
        ).astype(BF)
    g = gp_ref[0, 0]
    dq = dot(g, k_ref[...]) * (1.0 / math.sqrt(head))
    dq_s[...] = jnp.where(this, dq, dq_s[...])
    at = pl.multiple_of(h * head, head)
    dkt_s[pl.ds(at, head), :] = dot(qt_s[pl.ds(at, head), :], g).astype(BF)
    dvt_s[pl.ds(at, head), :] = dot(dmt_s[pl.ds(at, head), :], e_ref[0]).astype(BF)

    @pl.when(h == 3)
    def _():
        dq_ref[...] = dq_s[...].astype(BF)
        dkv_ref[:, :cols] = dkt_s[...].T
        dkv_ref[:, cols:] = dvt_s[...].T


def table_rows(s, sums, gbin, rows, sub, half):
    pieces = [v[:, s * rows:(s + 1) * rows] for v in sums]
    for b in range(4):
        pieces.append(gbin[2 * (b & 1) + (b >> 1), :, s * sub:(s + 1) * sub])
    lines, line, p = [], [], 0
    for piece in pieces:
        line.append(piece)
        p += piece.shape[1]
        if p % half == 0:
            lines.append(jnp.concatenate(line, 1))
            line = []
    if line:
        line.append(jnp.zeros((1, half - p % half), F32))
        lines.append(jnp.concatenate(line, 1))
    lines.append(jnp.zeros((8 - len(lines), half), F32))
    value = jnp.concatenate(lines, 0)
    high = value.astype(BF)
    return jnp.concatenate([high.astype(F32), value - high.astype(F32)], 0).astype(BF)


def weight_grad_kernel(order, shards, kind, sub, scal, xt_ref, dq0, dq1, dkv0, dkv1, *rest):
    pm, mc, core = scal[0], scal[1], scal[2]
    shard, cols = dq0.shape
    length = dkv0.shape[0]
    extra, (g_keep, g_send, vg_ref) = rest[:-3], rest[-3:]
    mine = pl.multiple_of(mc * shard, shard)
    ones = jnp.ones((8, length), BF)
    grad_kv = dot(xt_ref[0], dkv0[...]) + dot(xt_ref[1], dkv1[...])
    grad_q = dot(xt_ref[0, :, pl.ds(mine, shard)], dq0[...]) + dot(xt_ref[1, :, pl.ds(mine, shard)], dq1[...])
    vg_ref[1:2, :] = (dot(ones, dkv0[:, cols:]) + dot(ones, dkv1[:, cols:]))[0:1]
    vg_ref[0:1, :] = (dot(ones[:, :shard], dq0[...]) + dot(ones[:, :shard], dq1[...]))[0:1]
    grad = jnp.concatenate([grad_q.astype(BF), grad_kv.astype(BF)], 1)
    rows = grad.shape[0] // shards
    half = grad.shape[1] // 2
    first_core = core == 0
    if kind == 2:
        vg0, vg1, ff1, ff2, gbin = extra
        sums = [
            jnp.concatenate([vg0[i:i + 1, :], vg1[i:i + 1, :], vg_ref[i:i + 1, :]], 1) for i in range(2)
        ] + [ff1[2:3, :], ff1[0:1, :], ff1[1:2, :], ff2[2:3, :], ff2[0:1, :], ff2[1:2, :]]
    for i in range(shards):
        block = grad[i * rows:(i + 1) * rows]
        to = place(i, order) ^ pm
        g_keep[to, :rows, :half] = jnp.where(first_core, block[:, :half], block[:, half:])
        g_send[to, :rows, :half] = jnp.where(first_core, block[:, half:], block[:, :half])
        if kind == 0:
            go_keep, go_send = extra
            g_keep[to, :, half:] = go_keep[to]
            g_send[to, :, half:] = go_send[to]
        if kind == 2:
            table = table_rows(i, sums, gbin, rows, sub, half)
            g_keep[to, rows:, :] = table
            g_send[to, rows:, :] = table


def sum_kernel(rows, *refs):
    parts, out = refs[:-1], refs[-1]
    for i in range(out.shape[0]):
        total = parts[0][i].astype(F32)
        for part in parts[1:]:
            total = total + part[i].astype(F32)
        out[i, :rows] = total[:rows].astype(BF)
        value = total[rows:rows + 8] + total[rows + 8:]
        high = value.astype(BF).astype(F32)
        out[i, rows:] = jnp.concatenate([high, value - high], 0).astype(BF)


def token_kernel(
    order, shards,
    scal, dq00, dq01, dq10, dq11, dq20, dq21, dkv00, dkv01, dkv10, dkv11, dkv20, dkv21,
    a_lo, a_hi, ag_lo, ag_hi, b_lo, b_hi, bg_lo, bg_hi, dsum1,
    p0, p1, p2, p3, w_s,
):
    pm, mc, core = scal[0], scal[1], scal[2]
    rows = w_s.shape[1] // shards
    half = w_s.shape[2] // 2
    shard, cols = dq00.shape
    weights_in(w_s.at[0], order, pm, core, rows, shards, (a_lo, a_hi), (ag_lo, ag_hi), 0, half)
    weights_in(w_s.at[1], order, pm, core, rows, shards, (b_lo, b_hi), (bg_lo, bg_hi), 0, half)
    weights_in(w_s.at[2], order, pm, core, rows, shards, (b_lo, b_hi), (bg_lo, bg_hi), half, half)
    dqs = ((dq00, dq10, dq20), (dq01, dq11, dq21))
    dkvs = ((dkv00, dkv10, dkv20), (dkv01, dkv11, dkv21))
    for j, out in reversed(list(enumerate((p0, p1, p2, p3)))):
        where = pl.multiple_of((mc ^ j) * shard, shard)
        for s in range(2):
            total = None
            for g in range(3):
                part = dot_nt(dkvs[s][g][pl.ds(where, shard), :], w_s[g, :, cols:])
                if j == 0:
                    part = part + dot_nt(dqs[s][g][...], w_s[g, :, :cols])
                total = part if total is None else total + part
            if j == 0:
                total = total + dsum1[s * shard:(s + 1) * shard, :]
            out[s] = total.astype(out.dtype)


def finish_kernel(rows, sub, shards, scal, g0, g0c, g1, g1c, g2, g2c, ff, ffc, wq, wk, wv, wo, wi, wd, tab):
    mc, core = scal[1], scal[2]
    low = core == 0
    my_y = mc >> 1
    half = g1.shape[1]
    cols = wq.shape[1] // 3
    cut = half - cols

    def both(mine, other):
        mine, other = mine.astype(F32), other.astype(F32)
        return jnp.where(low, mine, other), jnp.where(low, other, mine)

    groups = [both(g0[:, :half], g0c[:, :half]), both(g1[...], g1c[...]), both(g2[:rows], g2c[:rows])]
    for g, (first, second) in enumerate(groups):
        at = g * cols
        wq[:, at:at + cols] = first[:, :cols]
        wk[:, at:at + cut] = first[:, cols:]
        wk[:, at + cut:at + cols] = second[:, :cols - cut]
        wv[:, at:at + cols] = second[:, cols - cut:]
    first, second = both(g0[:, half:], g0c[:, half:])
    wo[:, :half] = first
    wo[:, half:] = second
    tab[...] = g2[rows:rows + 8, :].astype(F32) + g2[rows + 8:, :].astype(F32)
    quads = []
    for i in range(2):
        a0, a1 = both(ff[0, i], ffc[0, i])
        b0, b1 = both(ff[1, i], ffc[1, i])
        near = my_y == 0
        quads.append([jnp.where(near, a0, b0), jnp.where(near, b0, a0), jnp.where(near, a1, b1), jnp.where(near, b1, a1)])
    for b in range(4):
        wd[b * sub:(b + 1) * sub, :] = quads[1][b]
        for s in range(shards):
            at = (4 * s + b) * sub
            wi[:, at:at + sub] = quads[0][b][:, s * sub:(s + 1) * sub]


def on_device(
    n, far, near,
    tokens, prior_logits, doc_ids, w_query, w_key, w_value, w_out, b_query, b_value, b_out,
    first_norm_gain, norm1_shift, w_in, b_in, w_down, b_down, norm2_gain, norm2_shift, cotangent,
):
    seqs, shard, width = tokens.shape
    heads, length = prior_logits.shape[1], prior_logits.shape[3]
    ctx = length // shard
    rows = w_query.shape[0]
    sub = w_down.shape[0] // 4
    cols = width // GROUPS
    per = heads // GROUPS
    half = (3 * cols) // 2
    n_rows = seqs * shard
    m = n // 2
    order = far + near
    me_s = lax.axis_index("seq")
    me_c = lax.axis_index("ctx")
    core = me_c & 1
    pm = place(me_s, order)
    scal = jnp.stack([pm, me_c, core]).astype(jnp.int32)
    sds = jax.ShapeDtypeStruct
    hbm = pl.BlockSpec(memory_space=ANY)

    def kernel(body, outs, ins, args, scratch=(), grid=None, alias=None, flops=0, moved=0, exps=0, name=None):
        return pl.pallas_call(
            body,
            out_shape=outs,
            in_specs=ins[0],
            out_specs=ins[1],
            scratch_shapes=scratch,
            input_output_aliases=alias or {},
            compiler_params=params(len(grid) if grid else 0),
            cost_estimate=pl.CostEstimate(flops=flops, bytes_accessed=moved, transcendentals=exps),
            name=name,
            **({"grid": grid} if grid else {}),
        )(*args)

    def by_core(value):
        return swap(value, "ctx", ctx, 0)

    def by_y(value):
        return swap(value, "ctx", ctx, 1)

    def by_x(value):
        return swap(value, "seq", n, near[-1])

    def whole(*shape):
        return pl.BlockSpec(shape, lambda *i: (0,) * len(shape))

    vectors = [b_query, b_value, b_out, first_norm_gain, norm1_shift, b_down, norm2_gain, norm2_shift, b_in]
    a0, b0, ffq, tok0 = kernel(
        prep_kernel,
        [sds((rows + 16, half), BF), sds((rows, 3 * half), BF), sds((2, rows, width), BF),
         sds((seqs, shard + 16, width), BF)],
        ([smem()] + [vmem()] * 17, [vmem()] * 4),
        (scal, tokens, doc_ids, w_query, w_key, w_value, w_out, w_in, w_down, *[v.reshape(1, -1) for v in vectors]),
        moved=6 * 10**6, name="prep",
    )

    def spread(held, name):
        parts = [held] + [swap_by(held, "seq", n, step) for step in far_steps(far)]
        lead = held.ndim == 3
        shape = (2, 4, *held.shape[1:]) if lead else (4, *held.shape)
        out, = kernel(join_kernel, [sds(shape, BF)], ([vmem()] * 4, [vmem()]), parts, moved=10**6, name=name)
        for bit in near[:-1]:
            out = jnp.concatenate([out, swap(out, "seq", n, bit)], 1 if lead else 0)
        return out

    a_lo = spread(a0, "join_a")
    tok2 = by_y(tok0)
    tok1 = by_core(tok0)
    ag_lo = by_core(a_lo)
    a_hi = by_x(a_lo)
    b_lo = spread(after(b0, a_lo), "join_b")
    ag_hi = by_core(a_hi)
    tok3 = by_core(tok2)
    tok = (tok0, tok1, tok2, tok3)
    b_hi = by_x(b_lo)
    bg_lo = by_core(b_lo)
    f_lo = spread(after(ffq, b_lo), "join_f")
    vecs, bin_all = kernel(
        functools.partial(vector_kernel, order, n, rows, sub),
        [sds((8, width), F32), sds((4, 1, width), F32)],
        ([smem()] + [vmem()] * 2, [vmem()] * 2), (scal, a_lo, a_hi), moved=10**6, name="vectors",
    )

    raw = None
    kept = []

    def attend(g, s, scal, arrays):
        nonlocal raw
        big = pl.BlockSpec((1, 1, shard, length), lambda h: (s, g * per + h, 0, 0))
        tok_spec = pl.BlockSpec((1, shard + 16, width), lambda h: (s, 0, 0))
        block = max(g - 1, 0)
        w_spec = pl.BlockSpec((m, arrays[0].shape[1], half), lambda h: (0, 0, block))
        args = [scal, *tok, doc_ids, *arrays, vecs, prior_logits]
        specs = [smem()] + [tok_spec] * 4 + [vmem()] + [w_spec] * 4 + [pl.BlockSpec((8, cols), lambda h: (0, g)), big]
        alias = {}
        if raw is not None:
            alias = {len(args): 0}
            args.append(raw)
            specs.append(hbm)
        raw, *rest = kernel(
            functools.partial(attend_kernel, order, n, s, g, raw is not None),
            [sds(prior_logits.shape, BF), sds((per, shard, length), BF), sds((shard, cols), BF),
             sds((length, cols), BF), sds((length, cols), BF), sds((shard, cols), F32), sds((shard, cols), F32)],
            (specs, [big, pl.BlockSpec((1, shard, length), lambda h: (h, 0, 0)), whole(shard, cols), whole(length, cols),
                     whole(length, cols), whole(shard, cols), whole(shard, cols)]),
            args, [VM((width, 3 * cols), BF), VM((cols, length), BF), VM((shard, length), F32), VM((2, length, cols), BF)],
            grid=(per,), alias=alias, flops=5 * 10**9, moved=10 * 10**6, exps=10**6, name=f"attend{g}{s}",
        )
        kept.append(rest)
        return rest[2]

    a_set = (a_lo, a_hi, ag_lo, ag_hi)
    mark = attend(0, 0, after(scal, b_lo), a_set)
    bg_hi = by_core(b_hi)
    b_set = (b_lo, b_hi, bg_lo, bg_hi)
    attend(0, 1, after(scal, f_lo), a_set)
    f_hi, f_ylo = by_x(f_lo), by_y(f_lo)
    fc_lo = by_core(f_lo)
    attend(1, 0, scal, b_set)
    x_t, = kernel(turn_kernel, [sds((seqs, width, length), BF)], ([smem()] + [vmem()] * 4, [vmem()]),
                  (scal, *tok), moved=12 * 10**6, name="turn")
    attend(1, 1, after(scal, kept[-1][4], f_hi, f_ylo), b_set)
    f_yhi_i, f_yhi_d = by_y(f_hi[0]), by_x(f_ylo[1])
    fc_hi, fc_ylo = by_core(f_hi), by_core(f_ylo)
    attend(2, 0, after(scal, x_t), b_set)
    attend(2, 1, after(scal, f_yhi_i, f_yhi_d), b_set)
    fc_yhi_i, fc_yhi_d = by_core(f_yhi_i), by_core(f_yhi_d)
    f = (f_lo, f_hi, f_ylo, f_yhi_i, f_yhi_d, fc_lo, fc_hi, fc_ylo, fc_yhi_i, fc_yhi_d)

    o_spec = pl.BlockSpec((m, rows, half), lambda i: (0, 0, 2))
    w_scratch = VM((4, width, width), BF)
    sems = pltpu.SemaphoreType.DMA((4 * n,))
    output, mixed, first_n, inv1, inner, hid, dg, dsum2, dsec, ff2 = kernel(
        functools.partial(forward_kernel, order, n),
        [
            sds((seqs, shard, width), BF), sds((n_rows, width), BF), sds((n_rows, width), F32), sds((n_rows, 1), F32),
            sds((n_rows, width), BF), sds((4, n_rows, width), BF), sds((4, n_rows, width), BF),
            sds((n_rows, width), F32), sds((n_rows, width), BF), sds((8, width), F32),
        ],
        ([smem()] + [vmem()] * 10 + [o_spec] * 4 + [hbm] * 10, [vmem()] * 10),
        (scal, *[k[4] for k in kept], tokens, cotangent, vecs, bin_all, *b_set, *f),
        [VM((width, width), BF), w_scratch, w_scratch, VM((n_rows, width), F32), VM((n_rows, width), F32), sems, sems],
        grid=(1,), flops=6 * 10**9, moved=25 * 10**6, exps=2 * 10**6, name="ff_fwd",
    )
    pair = [sds((2, n, rows, width), BF)] * 2
    d_keep, d_send = kernel(
        functools.partial(down_grad_kernel, order, n), pair,
        ([smem()] + [vmem()] * 2, [vmem()] * 2), (scal, hid, dsec), flops=3 * 10**9, moved=8 * 10**6, name="down_grad",
    )
    d_got = by_core(d_send)
    i_keep, i_send, dpre, gbin = kernel(
        functools.partial(in_grad_kernel, order, n),
        pair + [sds((4, n_rows, width), BF), sds((4, 1, width), F32)],
        ([smem()] + [vmem()] * 3 + [hbm] * 10, [vmem()] * 4),
        (after(scal, d_keep), inner, dg, dsec, *f), [w_scratch, sems], flops=6 * 10**9, moved=20 * 10**6, name="in_grad",
    )
    i_got = by_core(i_send)
    go_keep, go_send, dsum1, dmix, ff1 = kernel(
        functools.partial(first_grad_kernel, order, n),
        [sds((n, rows, half), BF)] * 2 + [sds((n_rows, width), F32), sds((n_rows, width), BF), sds((8, width), F32)],
        ([smem()] + [vmem()] * 6 + [o_spec] * 4 + [hbm] * 10, [vmem()] * 5),
        (scal, mixed, first_n, inv1, dpre, dsum2, vecs, *b_set, *f), [VM((width, width), BF), w_scratch, sems],
        grid=(1,), flops=4 * 10**9, moved=15 * 10**6, name="first_grad",
    )

    gp = None
    dqs, dkvs, vgs = [], [], []

    def back(g, s, scal):
        nonlocal gp
        e, q, k, v, o, inv = kept[g * seqs + s]
        big = pl.BlockSpec((1, 1, shard, length), lambda h: (s, g * per + h, 0, 0))
        args = [scal, e, dmix, q, k, v, o, inv]
        specs = [smem(), pl.BlockSpec((1, shard, length), lambda h: (h, 0, 0)),
                 pl.BlockSpec((shard, cols), lambda h: (s, g)),
                 whole(shard, cols), whole(length, cols), whole(length, cols), whole(shard, cols), whole(shard, cols)]
        alias = {}
        if gp is not None:
            alias = {len(args): 0}
            args.append(gp)
            specs.append(hbm)
        gp, dq, dkv = kernel(
            functools.partial(attend_back_kernel, gp is not None),
            [sds(prior_logits.shape, BF), sds((shard, cols), BF), sds((length, 2 * cols), BF)],
            (specs, [big, whole(shard, cols), whole(length, 2 * cols)]),
            args,
            [VM((cols, length), BF), VM((cols, shard), BF), VM((cols, shard), BF), VM((shard, cols), BF),
             VM((shard, cols), F32), VM((cols, length), BF), VM((cols, length), BF), VM((shard, cols), F32)],
            grid=(per,), alias=alias, flops=5 * 10**9, moved=10 * 10**6, name=f"back{g}{s}",
        )
        dqs.append(dq)
        dkvs.append(dkv)
        return dq

    def weight_grad(g, scal):
        extra = ([go_keep, go_send], [], vgs + [ff1, ff2, gbin])[g]
        shape = ((n, rows, 2 * half), (n, rows, half), (n, rows + 16, half))[g]
        keep, send, vg = kernel(
            functools.partial(weight_grad_kernel, order, n, g, sub),
            [sds(shape, BF)] * 2 + [sds((8, cols), F32)],
            ([smem()] + [vmem()] * (5 + len(extra)), [vmem()] * 3),
            (scal, x_t, *dqs[-2:], *dkvs[-2:], *extra),
            flops=2 * 10**9, moved=8 * 10**6, name=f"weight_grad{g}",
        )
        vgs.append(vg)
        return keep, send, vg

    def rest_near(held, axis, plus):
        for bit in reversed(near[:-1]):
            k = held.shape[axis] // 2
            keep = lax.slice_in_dim(held, 0, k, axis=axis)
            held = plus(keep, swap(lax.slice_in_dim(held, k, 2 * k, axis=axis), "seq", n, bit))
        return held

    def far_sum(blocks, plus):
        got = [swap_by(b, "seq", n, step) for b, step in zip(blocks[1:], far_steps(far))]
        return plus(blocks[0], *got)

    q_i = by_y(add(i_keep[1, m:], i_got[1, m:]))
    q_d = by_x(add(d_keep[1, m:], d_got[1, m:]))
    back(0, 0, scal)
    mark = back(0, 1, scal)
    hi = jnp.stack([add(i_keep[0, m:], i_got[0, m:], q_i), add(d_keep[0, m:], d_got[0, m:])])
    ylo = jnp.stack([add(i_keep[1, :m], i_got[1, :m]), add(d_keep[1, :m], d_got[1, :m], q_d)])
    x_got, y_got = by_x(hi), by_y(ylo)
    keep, send, vg = weight_grad(0, after(scal, hi, ylo))
    g0_got = by_core(send)
    mark = back(1, 0, after(scal, vg))
    g0_keep = keep
    mark = back(1, 1, after(scal, g0_got))
    lo = jnp.stack([add(i_keep[0, :m], i_got[0, :m], x_got[0], y_got[0]), add(d_keep[0, :m], d_got[0, :m], x_got[1], y_got[1])], 1)
    lo = rest_near(lo, 0, add)
    g0_x = by_x(after(add(g0_keep[m:], g0_got[m:]), mark))
    ff = far_sum([lo[i] for i in range(4)], add)
    g1_keep, g1_send, vg = weight_grad(1, after(scal, lo))
    g1_got = by_core(g1_send)
    mark = back(2, 0, after(scal, vg))
    g0 = rest_near(add(g0_keep[:m], g0_got[:m], g0_x), 0, add)
    g1_x = by_x(add(g1_keep[m:], g1_got[m:]))
    mark = back(2, 1, after(scal, g0))
    g0 = far_sum([g0[i] for i in range(4)], add)
    ff_y = by_y(ff)
    g2_keep, g2_send, _ = weight_grad(2, after(scal, ff))
    g2_got = by_core(g2_send)
    g1 = rest_near(add(g1_keep[:m], g1_got[:m], g1_x), 0, add)

    def plus_table(*parts):
        flat = parts[0].ndim == 2
        parts = [p[None] if flat else p for p in parts]
        out, = kernel(functools.partial(sum_kernel, rows), [sds(parts[0].shape, BF)],
                      ([vmem()] * len(parts), [vmem()]), parts, moved=10**6, name="sum_table")
        return out[0] if flat else out

    g2_x = by_x(plus_table(g2_keep[m:], g2_got[m:]))
    g1 = far_sum([g1[i] for i in range(4)], add)
    pieces = kernel(
        functools.partial(token_kernel, order, n),
        [sds((seqs, shard, width), F32)] + [sds((seqs, shard, width), BF)] * 3,
        ([smem()] + [vmem()] * 12 + [whole(m, a.shape[1], half) for a in a_set]
         + [whole(m, rows, 2 * half)] * 4 + [vmem()], [vmem()] * 4),
        (after(scal, g2_got), *dqs, *dkvs, *a_set, *b_set, dsum1),
        [VM((GROUPS, width, 3 * cols), BF)], grid=(1,), flops=10 * 10**9, moved=15 * 10**6, name="token_grad",
    )
    from_core = (by_core(pieces[1]), by_core(pieces[3]))
    across = by_y(add(pieces[2], from_core[1]))
    g2 = rest_near(plus_table(g2_keep[:m], g2_got[:m], g2_x), 0, plus_table)
    g2 = far_sum([g2[i] for i in range(4)], plus_table)
    g0 = add(g0, by_y(g0))
    g1 = add(g1, by_y(g1))
    g2 = plus_table(g2, by_y(g2))
    ff = jnp.stack([ff, ff_y])
    grad_tokens = pieces[0] + from_core[0].astype(F32) + across.astype(F32)
    g_wq, g_wk, g_wv, g_wo, g_wi, g_wd, table = kernel(
        functools.partial(finish_kernel, rows, sub, n),
        [sds(w.shape, F32) for w in (w_query, w_key, w_value, w_out, w_in, w_down)] + [sds((8, half), F32)],
        ([smem()] + [vmem()] * 8, [vmem()] * 7),
        (scal, g0, by_core(g0), g1, by_core(g1), g2, by_core(g2), ff, by_core(ff)),
        moved=6 * 10**6, name="finish",
    )
    table = table.reshape(-1)
    cut = [table[i * rows:(i + 1) * rows] for i in range(8)]
    g_bq, g_bv, g_bo, g_g1, g_s1, g_bd, g_g2, g_s2 = cut
    g_bin = table[8 * rows:8 * rows + 4 * sub]
    return (
        output, raw, grad_tokens, gp, g_wq, g_wk, g_wv, g_wo,
        g_bq, g_bv, g_bo, g_g1, g_s1, g_wi, g_bin, g_wd, g_bd, g_g2, g_s2,
    )


def solution(mesh):
    n = mesh.shape["seq"]
    top = n.bit_length() - 1
    far, near = (top - 2, top - 1), tuple(reversed(range(top - 2)))
    in_specs = (
        P("seq", "ctx", None), P("seq", None, "ctx", None), P("seq", "ctx"),
        P("seq", None), P("seq", None), P("seq", None), P("seq", None),
        P("seq"), P("seq"), P("seq"), P("seq"), P("seq"),
        P("seq", None), P("seq"), P("seq", None), P("seq"), P("seq"), P("seq"),
        P("seq", "ctx", None),
    )
    out_specs = (
        P("seq", "ctx", None), P("seq", None, "ctx", None), P("seq", "ctx", None), P("seq", None, "ctx", None),
        P("seq", None), P("seq", None), P("seq", None), P("seq", None),
        P("seq"), P("seq"), P("seq"), P("seq"), P("seq"),
        P("seq", None), P("seq"), P("seq", None), P("seq"), P("seq"), P("seq"),
    )
    return jax.shard_map(
        functools.partial(on_device, n, far, near),
        mesh=mesh, in_specs=in_specs, out_specs=out_specs, check_vma=False,
    )
```

```python
import functools
import math

import jax
import jax.numpy as jnp
from jax import lax
from jax.experimental import pallas as pl
from jax.experimental.pallas import tpu as pltpu
from jax.sharding import PartitionSpec as P

EPSILON = 1e-05
NEGATIVE = -1e30
BF = jnp.bfloat16
F32 = jnp.float32
VM = pltpu.VMEM
ANY = pl.ANY
GROUPS = 3


def dot(a, b):
    return lax.dot_general(a, b, (((1,), (0,)), ((), ())), preferred_element_type=F32)


def dot_nt(a, b):
    return lax.dot_general(a, b, (((1,), (1,)), ((), ())), preferred_element_type=F32)


def dot_tn(a, b):
    return lax.dot_general(a, b, (((0,), (0,)), ((), ())), preferred_element_type=F32)


def vmem(shape=None, index=None):
    if shape is None:
        return pl.BlockSpec(memory_space=VM)
    return pl.BlockSpec(shape, index)


def params(n_grid, limit):
    return pltpu.CompilerParams(
        vmem_limit_bytes=limit * 1024 * 1024,
        dimension_semantics=("arbitrary",) * n_grid if n_grid else None,
    )


def smem():
    return pl.BlockSpec(memory_space=pltpu.SMEM)


def after(value, *marks):
    return lax.optimization_barrier((value, *marks))[0]


def swap_by(value, axis, size, step):
    return lax.ppermute(value, axis, [(i, i ^ step) for i in range(size)])


def swap(value, axis, size, bit):
    return swap_by(value, axis, size, 1 << bit)


def far_steps(far):
    a, b = 1 << far[0], 1 << far[1]
    return (a, b, a | b)


def add(*parts):
    total = parts[0].astype(F32)
    for part in parts[1:]:
        total = total + part.astype(F32)
    return total.astype(BF)


def place(index, order):
    out = 0
    for step, bit in enumerate(order):
        out = out | (((index >> bit) & 1) << step)
    return out


def column_half(wq, wk, wv, g, half, low):
    cols = (2 * half) // 3
    cut = half - cols
    at = g * cols
    first = jnp.concatenate([wq[:, at:at + cols], wk[:, at:at + cut]], 1)
    second = jnp.concatenate([wk[:, at + cut:at + cols], wv[:, at:at + cols]], 1)
    return jnp.where(low, first, second)


def prep_first_kernel(scal, tok, docs, wq, wk, wv, *rest):
    vecs, (a0, tok_ref) = rest[:9], rest[9:]
    seqs, shard = tok.shape[:2]
    rows = wq.shape[0]
    half = a0.shape[1]
    for s in range(seqs):
        tok_ref[s, :shard, :] = tok[s]
        tok_ref[s, shard:, :] = jnp.zeros_like(tok_ref[s, shard:, :])
        tok_ref[s, shard:shard + 1, :shard] = docs[s:s + 1, :].astype(F32).astype(BF)
    a0[:rows] = column_half(wq, wk, wv, 0, half, scal[2] == 0)
    p = 0
    lines = []
    line = []
    for v in vecs:
        step = rows if v.shape[1] == rows else v.shape[1] // 4
        for i in range(v.shape[1] // step):
            line.append(v[:, i * step:(i + 1) * step].astype(F32))
            p += step
            if p % half == 0:
                lines.append(jnp.concatenate(line, 1))
                line = []
    if line:
        line.append(jnp.zeros((1, half - p % half), F32))
        lines.append(jnp.concatenate(line, 1))
    lines.append(jnp.zeros((16 - len(lines), half), F32))
    a0[rows:] = jnp.concatenate(lines, 0).astype(BF)


def prep_kernel(scal, wq, wk, wv, wo, wi, wd, a1, a2, ffq):
    mc, core = scal[1], scal[2]
    my_y = mc >> 1
    width = wq.shape[1]
    half = a1.shape[1]
    low = core == 0
    sub = ffq.shape[1]
    a1[...] = column_half(wq, wk, wv, 1, half, low)
    a2[:, :half] = column_half(wq, wk, wv, 2, half, low)
    a2[:, half:] = jnp.where(low, wo[:, :half], wo[:, half:])
    block = 2 * core + my_y
    ffq[1] = wd[pl.ds(pl.multiple_of(block * sub, sub), sub), :]
    for s in range(width // sub):
        got = [wi[:, (4 * s + b) * sub:(4 * s + b + 1) * sub] for b in range(4)]
        near = jnp.where(my_y == 0, got[0], got[1])
        far = jnp.where(my_y == 0, got[2], got[3])
        ffq[0, :, s * sub:(s + 1) * sub] = jnp.where(low, near, far)


def join_kernel(a, b, c, d, out):
    lead = out.ndim == 4
    for i, ref in enumerate((a, b, c, d)):
        if lead:
            out[:, i] = ref[...]
        else:
            out[i] = ref[...]


def fetch(lo, hi, at):
    m = lo.shape[0]
    return jnp.where(at < m, lo[at & (m - 1)], hi[at & (m - 1)])


def weights_in(out, order, pm, core, rows, shards, own, got, at_col, half):
    first = core == 0
    for i in range(shards):
        at = place(i, order) ^ pm
        m = own[0].shape[0]
        pick = lambda ref: ref[at & (m - 1), :rows, at_col:at_col + half]
        in_lo = at < m
        mine = jnp.where(in_lo, pick(own[0]), pick(own[1]))
        other = jnp.where(in_lo, pick(got[0]), pick(got[1]))
        out[i * rows:(i + 1) * rows, :half] = jnp.where(first, mine, other)
        out[i * rows:(i + 1) * rows, half:2 * half] = jnp.where(first, other, mine)


def vector_kernel(order, shards, rows, sub, scal, lo, hi, vec_ref, bin_ref):
    pm = scal[0]
    half = lo.shape[2]
    m = lo.shape[0]
    for s in range(shards):
        at = place(s, order) ^ pm
        block = jnp.where(at < m, lo[at & (m - 1), rows:, :], hi[at & (m - 1), rows:, :]).astype(F32)
        for i in range(8):
            p = i * rows
            vec_ref[i:i + 1, s * rows:(s + 1) * rows] = block[p // half:p // half + 1, p % half:p % half + rows]
        for b in range(4):
            p = 8 * rows + b * sub
            c = 2 * (b & 1) + (b >> 1)
            bin_ref[c, :, s * sub:(s + 1) * sub] = block[p // half:p // half + 1, p % half:p % half + sub]


def turn_kernel(scal, t0, t1, t2, t3, out_ref):
    mc = scal[1]
    seqs, _, width = t0.shape
    shard = out_ref.shape[2] // 4
    for j, tok in enumerate((t0, t1, t2, t3)):
        where = pl.multiple_of((mc ^ j) * shard, shard)
        for s in range(seqs):
            out_ref[s, :, pl.ds(where, shard)] = tok[s, :shard, :].T


def attend_kernel(
    order, shards, seq, group, aliased,
    scal, t0, t1, t2, t3, doc_ref, own_lo, own_hi, got_lo, got_hi, bias_ref, prior_ref, *rest,
):
    if aliased:
        rest = rest[1:]
    raw_ref, e_ref, q_ref, k_ref, v_ref, o_ref, inv_ref, w_s, kt_s, mask_s, vx_s = rest
    h = pl.program_id(0)
    pm, mc, core = scal[0], scal[1], scal[2]
    rows = w_s.shape[0] // shards
    half = w_s.shape[1] // 2
    shard, cols = q_ref.shape
    head = cols // 4

    @pl.when(h == 0)
    def _():
        weights_in(w_s, order, pm, core, rows, shards, (own_lo, own_hi), (got_lo, got_hi), 0, half)
        q = dot(t0[0, :shard, :], w_s[:, :cols]) + bias_ref[0:1, :]
        q_ref[...] = (q.astype(BF).astype(F32) * (1.0 / math.sqrt(head))).astype(BF)
        mine = jnp.broadcast_to(doc_ref[seq:seq + 1, :].astype(F32), (128, shard)).T[:, :1]
        for j, tok in enumerate((t0, t1, t2, t3)):
            where = pl.multiple_of((mc ^ j) * shard, shard)
            kv = dot(tok[0, :shard, :], w_s[:, cols:])
            k_ref[pl.ds(where, shard), :] = kv[:, :cols].astype(BF)
            v = kv[:, cols:] + bias_ref[1:2, :]
            v_ref[pl.ds(where, shard), :] = v.astype(BF)
            even = (lax.broadcasted_iota(jnp.int32, (shard, cols), 1) // head) % 2 == 0
            vx_s[0, pl.ds(where, shard), :] = jnp.where(even, v, 1.0).astype(BF)
            vx_s[1, pl.ds(where, shard), :] = jnp.where(even, 1.0, v).astype(BF)
            docs = tok[0, shard:shard + 1, :shard].astype(F32)
            mask_s[:, pl.ds(where, shard)] = jnp.where(mine == docs, 0.0, NEGATIVE)
        kt_s[...] = k_ref[...].T

    lane = lax.broadcasted_iota(jnp.int32, (shard, cols), 1) // head
    this = lane == h
    qm = jnp.where(this, q_ref[...].astype(F32), 0.0).astype(BF)
    step = 64
    for r in range(0, shard, step):
        logits = dot(qm[r:r + step], kt_s[...]) + prior_ref[0, 0, r:r + step, :].astype(F32)
        raw_ref[0, 0, r:r + step, :] = logits.astype(BF)
        masked = logits + mask_s[r:r + step, :]
        top = jnp.max(masked, -1, keepdims=True)
        e_ref[0, r:r + step, :] = jnp.exp(masked - top).astype(BF)
    o = dot(e_ref[0], vx_s[h & 1])
    total = jnp.max(jnp.where(lane == (h ^ 1), o, 0.0), -1, keepdims=True)
    inv = 1.0 / total
    o_ref[...] = jnp.where(this, o * inv, o_ref[...])
    inv_ref[...] = jnp.where(this, inv, inv_ref[...])


def gelu_parts(x):
    z = jnp.abs(x) * 0.7071067811865476
    t = 1.0 / (1.0 + 0.3275911 * z)
    e = jnp.exp(-0.5 * x * x)
    poly = t * (0.254829592 + t * (-0.284496736 + t * (1.421413741 + t * (-1.453152027 + t * 1.061405429))))
    tail = 0.5 * poly * e
    phi = jnp.where(x >= 0, 1.0 - tail, tail)
    return x * phi, phi + x * (e * 0.3989422804014327)


def moments(x):
    mean = jnp.mean(x, -1, keepdims=True)
    centered = x - mean
    inverse = lax.rsqrt(jnp.mean(centered * centered, -1, keepdims=True) + EPSILON)
    return centered * inverse, inverse


def norm_back(grad, normed, inverse, gain):
    scaled = grad * gain
    return inverse * (
        scaled - jnp.mean(scaled, -1, keepdims=True)
        - normed * jnp.mean(scaled * normed, -1, keepdims=True)
    )


def ff_sources(f, which):
    lo, hi, ylo, yhi_i, yhi_d, clo, chi, cylo, cyhi_i, cyhi_d = f
    yhi, cyhi = (yhi_i, cyhi_i) if which == 0 else (yhi_d, cyhi_d)
    return [(lo.at[which], hi.at[which]), (clo.at[which], chi.at[which]),
            (ylo.at[which], yhi), (cylo.at[which], cyhi)]


def ff_copies(f, which, held, sem):
    out = []
    for j, halves in enumerate(ff_sources(f, which)):
        m = halves[0].shape[0]
        out.append([pltpu.make_async_copy(src, held.at[j, pl.ds(i * m, m)], sem.at[2 * j + i])
                    for i, src in enumerate(halves)])
    for pair in out:
        for copy in pair:
            copy.start()
    return out


def ff_wait(copies, j, held, order, pm, shards, rows, out):
    for copy in copies[j]:
        copy.wait()
    for s in range(shards):
        out[s * rows:(s + 1) * rows] = held[j, place(s, order) ^ pm]


def forward_kernel(
    order, shards,
    scal, o00, o01, o10, o11, o20, o21, tok_ref, cot_ref, vec_ref, bin_ref, wl, wh, wgl, wgh, *rest,
):
    f, rest = rest[:10], rest[10:]
    (out_ref, mix_ref, first_n_ref, inv1_ref, inner_ref, hid_ref, dg_ref, dsum2_ref, dsec_ref, vg_ref,
     wo_s, wi_s, wd_s, w_s, first_s, acc_s, isem, dsem) = rest
    pm, mc, core = scal[0], scal[1], scal[2]
    seqs, shard, width = tok_ref.shape
    rows = width // shards
    n_rows = seqs * shard
    in_copies = ff_copies(f, 0, wi_s, isem)
    down_copies = ff_copies(f, 1, wd_s, dsem)
    weights_in(wo_s, order, pm, core, rows, shards, (wl, wh), (wgl, wgh), 0, width // 2)
    mixed = jnp.concatenate(
        [jnp.concatenate([a[...].astype(BF), b[...].astype(BF)], 0) for a, b in ((o00, o01), (o10, o11), (o20, o21))], 1)
    mix_ref[...] = mixed
    tokens = tok_ref[...].reshape(n_rows, width).astype(F32)
    normed, inverse = moments(tokens + (dot(mixed, wo_s[...]) + vec_ref[2:3, :]))
    first_n_ref[...] = normed
    inv1_ref[...] = inverse
    first = normed * vec_ref[3:4, :] + vec_ref[4:5, :]
    first_s[...] = first
    inner_ref[...] = first.astype(BF)
    for j in range(4):
        ff_wait(in_copies, j, wi_s, order, pm, shards, rows, w_s)
        for r in range(0, n_rows, 128):
            pre = dot(inner_ref[r:r + 128, :], w_s[...]) + bin_ref[mc ^ j]
            hid, dg = gelu_parts(pre)
            hid_ref[j, r:r + 128, :] = hid.astype(BF)
            dg_ref[j, r:r + 128, :] = dg.astype(BF)
        ff_wait(down_copies, j, wd_s, order, pm, shards, rows, w_s)
        part = dot(hid_ref[j], w_s[...])
        acc_s[...] = part if j == 0 else acc_s[...] + part
    normed, inverse = moments(first_s[...] + (acc_s[...] + vec_ref[5:6, :]))
    gain = vec_ref[6:7, :]
    out_ref[...] = (normed * gain + vec_ref[7:8, :]).astype(BF).reshape(seqs, shard, width)
    dy = cot_ref[...].reshape(n_rows, width).astype(F32)
    dsum2 = norm_back(dy, normed, inverse, gain)
    dsum2_ref[...] = dsum2
    dsec = dsum2.astype(BF)
    dsec_ref[...] = dsec
    vg_ref[0:1, :] = jnp.sum(dy * normed, 0, keepdims=True)
    vg_ref[1:2, :] = jnp.sum(dy, 0, keepdims=True)
    vg_ref[2:3, :] = jnp.sum(dsec.astype(F32), 0, keepdims=True)


def down_grad_kernel(order, shards, scal, hid, dsec, keep, send):
    pm = scal[0]
    sub = keep.shape[2]
    for j in (1, 3, 0, 2):
        out = keep if j % 2 == 0 else send
        grad = dot_tn(hid[j], dsec[...]).astype(BF)
        for s in range(shards):
            out[j >> 1, place(s, order) ^ pm] = grad[s * sub:(s + 1) * sub]


def in_grad_kernel(order, shards, scal, inner, dg, dsec, *rest):
    f, (keep, send, dpre_ref, gbin_ref, wd_s, w_s, sem) = rest[:10], rest[10:]
    pm, mc = scal[0], scal[1]
    rows = keep.shape[2]
    step = pl.program_id(0)

    @pl.when(step == 0)
    def _():
        ff_copies(f, 1, wd_s, sem)

    for i, j in enumerate((1, 3, 0, 2)):
        @pl.when(step == i)
        def _(j=j):
            copies = {j: [pltpu.make_async_copy(src, wd_s.at[j, pl.ds(k * src.shape[0], src.shape[0])], sem.at[2 * j + k])
                          for k, src in enumerate(ff_sources(f, 1)[j])]}
            ff_wait(copies, j, wd_s, order, pm, shards, rows, w_s)

    j = jnp.where(step < 2, 2 * step + 1, 2 * step - 4)
    dpre = (dot_nt(dsec[...], w_s[...]) * dg[0].astype(F32)).astype(BF)
    dpre_ref[0] = dpre
    gbin_ref[mc ^ j] = jnp.sum(dpre.astype(F32), 0, keepdims=True)
    grad = dot_tn(inner[...], dpre).astype(BF)

    @pl.when(step < 2)
    def _():
        for s in range(shards):
            send[0, place(s, order) ^ pm] = grad[s * rows:(s + 1) * rows]

    @pl.when(step >= 2)
    def _():
        for s in range(shards):
            keep[0, place(s, order) ^ pm] = grad[s * rows:(s + 1) * rows]


def first_grad_kernel(
    order, shards, scal, mix_ref, first_n, inv1, dpre, dsum2, vec_ref, wl, wh, wgl, wgh, *rest,
):
    f, (go_keep, go_send, dsum1_ref, dmix_ref, vg_ref, wo_s, wi_s, w_s, sem) = rest[:10], rest[10:]
    pm, core = scal[0], scal[2]
    n_rows, width = dsum2.shape
    rows = width // shards
    half = width // 2
    in_copies = ff_copies(f, 0, wi_s, sem)
    weights_in(wo_s, order, pm, core, rows, shards, (wl, wh), (wgl, wgh), 0, half)
    dfirst = dsum2[...]
    for j in range(4):
        ff_wait(in_copies, j, wi_s, order, pm, shards, rows, w_s)
        dfirst = dfirst + dot_nt(dpre[j], w_s[...])
    normed = first_n[...]
    dsum1 = norm_back(dfirst, normed, inv1[...], vec_ref[3:4, :])
    dsum1_ref[...] = dsum1
    dbranch = dsum1.astype(BF)
    vg_ref[0:1, :] = jnp.sum(dfirst * normed, 0, keepdims=True)
    vg_ref[1:2, :] = jnp.sum(dfirst, 0, keepdims=True)
    vg_ref[2:3, :] = jnp.sum(dbranch.astype(F32), 0, keepdims=True)
    dmix_ref[...] = dot_nt(dbranch, wo_s[...]).astype(BF)
    grad_o = dot_tn(mix_ref[...], dbranch).astype(BF)
    first_core = core == 0
    for s in range(shards):
        block = grad_o[s * rows:(s + 1) * rows]
        at = place(s, order) ^ pm
        go_keep[at] = jnp.where(first_core, block[:, :half], block[:, half:])
        go_send[at] = jnp.where(first_core, block[:, half:], block[:, :half])


def attend_back_kernel(
    aliased,
    scal, e_ref, dm_ref, q_ref, k_ref, v_ref, o_ref, inv_ref, *rest,
):
    if aliased:
        rest = rest[1:]
    gp_ref, dq_ref, dkv_ref, vt_s, qt_s, dmt_s, dmi_s, dl_s, dkt_s, dvt_s, dq_s = rest
    h = pl.program_id(0)
    shard, cols = q_ref.shape
    head = cols // 4

    @pl.when(h == 0)
    def _():
        vt_s[...] = v_ref[...].T
        dmi = (dm_ref[...].astype(F32) * inv_ref[...]).astype(BF)
        dmi_s[...] = dmi
        dl_s[...] = dmi.astype(F32) * o_ref[...]
        qt_s[...] = q_ref[...].T
        dmt_s[...] = dmi.T

    lane = lax.broadcasted_iota(jnp.int32, (shard, cols), 1) // head
    this = lane == h
    dmm = jnp.where(this, dmi_s[...].astype(F32), 0.0).astype(BF)
    delta = jnp.sum(jnp.where(this, dl_s[...], 0.0), -1, keepdims=True)
    step = 64
    for r in range(0, shard, step):
        dp = dot(dmm[r:r + step], vt_s[...])
        gp_ref[0, 0, r:r + step, :] = (
            e_ref[0, r:r + step, :].astype(F32) * (dp - delta[r:r + step])
        ).astype(BF)
    g = gp_ref[0, 0]
    dq = dot(g, k_ref[...]) * (1.0 / math.sqrt(head))
    dq_s[...] = jnp.where(this, dq, dq_s[...])
    at = pl.multiple_of(h * head, head)
    dkt_s[pl.ds(at, head), :] = dot(qt_s[pl.ds(at, head), :], g).astype(BF)
    dvt_s[pl.ds(at, head), :] = dot(dmt_s[pl.ds(at, head), :], e_ref[0]).astype(BF)

    @pl.when(h == 3)
    def _():
        dq_ref[...] = dq_s[...].astype(BF)
        dkv_ref[:, :cols] = dkt_s[...].T
        dkv_ref[:, cols:] = dvt_s[...].T


def table_rows(s, sums, gbin, rows, sub, half):
    pieces = [v[:, s * rows:(s + 1) * rows] for v in sums]
    for b in range(4):
        pieces.append(gbin[2 * (b & 1) + (b >> 1), :, s * sub:(s + 1) * sub])
    lines, line, p = [], [], 0
    for piece in pieces:
        line.append(piece)
        p += piece.shape[1]
        if p % half == 0:
            lines.append(jnp.concatenate(line, 1))
            line = []
    if line:
        line.append(jnp.zeros((1, half - p % half), F32))
        lines.append(jnp.concatenate(line, 1))
    lines.append(jnp.zeros((8 - len(lines), half), F32))
    value = jnp.concatenate(lines, 0)
    high = value.astype(BF)
    return jnp.concatenate([high.astype(F32), value - high.astype(F32)], 0).astype(BF)


def weight_grad_kernel(order, shards, kind, sub, scal, xt_ref, dq0, dq1, dkv0, dkv1, *rest):
    pm, mc, core = scal[0], scal[1], scal[2]
    shard, cols = dq0.shape
    length = dkv0.shape[0]
    extra, (g_keep, g_send, vg_ref) = rest[:-3], rest[-3:]
    mine = pl.multiple_of(mc * shard, shard)
    ones = jnp.ones((8, length), BF)
    grad_kv = dot(xt_ref[0], dkv0[...]) + dot(xt_ref[1], dkv1[...])
    grad_q = dot(xt_ref[0, :, pl.ds(mine, shard)], dq0[...]) + dot(xt_ref[1, :, pl.ds(mine, shard)], dq1[...])
    vg_ref[1:2, :] = (dot(ones, dkv0[:, cols:]) + dot(ones, dkv1[:, cols:]))[0:1]
    vg_ref[0:1, :] = (dot(ones[:, :shard], dq0[...]) + dot(ones[:, :shard], dq1[...]))[0:1]
    grad = jnp.concatenate([grad_q.astype(BF), grad_kv.astype(BF)], 1)
    rows = grad.shape[0] // shards
    half = grad.shape[1] // 2
    first_core = core == 0
    if kind == 2:
        vg0, vg1, ff1, ff2, gbin = extra
        sums = [
            jnp.concatenate([vg0[i:i + 1, :], vg1[i:i + 1, :], vg_ref[i:i + 1, :]], 1) for i in range(2)
        ] + [ff1[2:3, :], ff1[0:1, :], ff1[1:2, :], ff2[2:3, :], ff2[0:1, :], ff2[1:2, :]]
    for i in range(shards):
        block = grad[i * rows:(i + 1) * rows]
        to = place(i, order) ^ pm
        keep = jnp.where(first_core, block[:, :half], block[:, half:])
        send = jnp.where(first_core, block[:, half:], block[:, :half])
        if kind == 0:
            go_keep, go_send = extra
            near = (mc >> 1) == 0
            g_keep[0, to] = jnp.where(near, keep, go_keep[to])
            g_keep[1, to] = jnp.where(near, go_keep[to], keep)
            g_send[0, to] = jnp.where(near, send, go_send[to])
            g_send[1, to] = jnp.where(near, go_send[to], send)
        else:
            g_keep[to, :rows, :] = keep
            g_send[to, :rows, :] = send
        if kind == 2:
            table = table_rows(i, sums, gbin, rows, sub, half)
            g_keep[to, rows:, :] = table
            g_send[to, rows:, :] = table


def sum_kernel(rows, *refs):
    parts, out = refs[:-1], refs[-1]
    for i in range(out.shape[0]):
        total = parts[0][i].astype(F32)
        for part in parts[1:]:
            total = total + part[i].astype(F32)
        out[i, :rows] = total[:rows].astype(BF)
        value = total[rows:rows + 8] + total[rows + 8:]
        high = value.astype(BF).astype(F32)
        out[i, rows:] = jnp.concatenate([high, value - high], 0).astype(BF)


def token_kernel(
    order, shards, own,
    scal, dq00, dq01, dq10, dq11, dq20, dq21, dkv00, dkv01, dkv10, dkv11, dkv20, dkv21,
    a_lo, a_hi, ag_lo, ag_hi, b_lo, b_hi, bg_lo, bg_hi, c_lo, c_hi, cg_lo, cg_hi, *rest,
):
    w_s = rest[-1]
    pm, mc, core = scal[0], scal[1], scal[2]
    rows = w_s.shape[1] // shards
    half = w_s.shape[2] // 2
    shard, cols = dq00.shape
    weights_in(w_s.at[0], order, pm, core, rows, shards, (a_lo, a_hi), (ag_lo, ag_hi), 0, half)
    weights_in(w_s.at[1], order, pm, core, rows, shards, (b_lo, b_hi), (bg_lo, bg_hi), 0, half)
    weights_in(w_s.at[2], order, pm, core, rows, shards, (c_lo, c_hi), (cg_lo, cg_hi), 0, half)
    dqs = ((dq00, dq10, dq20), (dq01, dq11, dq21))
    dkvs = ((dkv00, dkv10, dkv20), (dkv01, dkv11, dkv21))
    outs = [(0, rest[1])] if own else [(1, rest[0].at[0]), (3, rest[0].at[1]), (2, rest[1])]
    for j, out in outs:
        where = pl.multiple_of((mc ^ j) * shard, shard)
        for s in range(2):
            total = rest[0][s * shard:(s + 1) * shard, :] if own else None
            for g in range(3):
                part = dot_nt(dkvs[s][g][pl.ds(where, shard), :], w_s[g, :, cols:])
                if own:
                    part = part + dot_nt(dqs[s][g][...], w_s[g, :, :cols])
                total = part if total is None else total + part
            out[s] = total.astype(out.dtype)


def by_core_order(low, mine, other):
    mine, other = mine.astype(F32), other.astype(F32)
    return jnp.where(low, mine, other), jnp.where(low, other, mine)


def finish_kernel(rows, scal, g0, g0c, g1, g1c, g2, g2c, wq, wk, wv, wo, tab):
    low = scal[2] == 0
    near = (scal[1] >> 1) == 0
    half = g1.shape[1]
    cols = wq.shape[1] // 3
    cut = half - cols

    def both(mine, other):
        return by_core_order(low, mine, other)

    zero = both(jnp.where(near, g0[0], g0[1]), jnp.where(near, g0c[0], g0c[1]))
    outer = both(jnp.where(near, g0[1], g0[0]), jnp.where(near, g0c[1], g0c[0]))
    groups = [zero, both(g1[...], g1c[...]), both(g2[:rows], g2c[:rows])]
    for g, (first, second) in enumerate(groups):
        at = g * cols
        wq[:, at:at + cols] = first[:, :cols]
        wk[:, at:at + cut] = first[:, cols:]
        wk[:, at + cut:at + cols] = second[:, :cols - cut]
        wv[:, at:at + cols] = second[:, cols - cut:]
    wo[:, :half] = outer[0]
    wo[:, half:] = outer[1]
    tab[...] = g2[rows:rows + 8, :].astype(F32) + g2[rows + 8:, :].astype(F32)


def finish_ff_kernel(sub, shards, scal, d, dc, i, ic, wi, wd):
    low = scal[2] == 0
    near = (scal[1] >> 1) == 0
    quads = []
    for mine, other in ((i, ic), (d, dc)):
        a0, a1 = by_core_order(low, mine[0], other[0])
        b0, b1 = by_core_order(low, mine[1], other[1])
        quads.append([jnp.where(near, a0, b0), jnp.where(near, b0, a0), jnp.where(near, a1, b1), jnp.where(near, b1, a1)])
    for b in range(4):
        wd[b * sub:(b + 1) * sub, :] = quads[1][b]
        for s in range(shards):
            at = (4 * s + b) * sub
            wi[:, at:at + sub] = quads[0][b][:, s * sub:(s + 1) * sub]


def on_device(
    n, far, near,
    tokens, prior_logits, doc_ids, w_query, w_key, w_value, w_out, b_query, b_value, b_out,
    first_norm_gain, norm1_shift, w_in, b_in, w_down, b_down, norm2_gain, norm2_shift, cotangent,
):
    seqs, shard, width = tokens.shape
    heads, length = prior_logits.shape[1], prior_logits.shape[3]
    ctx = length // shard
    rows = w_query.shape[0]
    sub = w_down.shape[0] // 4
    cols = width // GROUPS
    per = heads // GROUPS
    half = (3 * cols) // 2
    n_rows = seqs * shard
    m = n // 2
    order = far + near
    me_s = lax.axis_index("seq")
    me_c = lax.axis_index("ctx")
    core = me_c & 1
    pm = place(me_s, order)
    scal = jnp.stack([pm, me_c, core]).astype(jnp.int32)
    sds = jax.ShapeDtypeStruct
    hbm = pl.BlockSpec(memory_space=pltpu.HBM)

    def kernel(body, outs, ins, args, scratch=(), grid=None, alias=None, flops=0, moved=0, exps=0, name=None, limit=24):
        return pl.pallas_call(
            body,
            out_shape=outs,
            in_specs=ins[0],
            out_specs=ins[1],
            scratch_shapes=scratch,
            input_output_aliases=alias or {},
            compiler_params=params(len(grid) if grid else 0, limit),
            cost_estimate=pl.CostEstimate(flops=flops, bytes_accessed=moved, transcendentals=exps),
            name=name,
            **({"grid": grid} if grid else {}),
        )(*args)

    def by_core(value):
        return swap(value, "ctx", ctx, 0)

    def by_y(value):
        return swap(value, "ctx", ctx, 1)

    def by_x(value):
        return swap(value, "seq", n, near[-1])

    def whole(*shape):
        return pl.BlockSpec(shape, lambda *i: (0,) * len(shape))

    vectors = [b_query, b_value, b_out, first_norm_gain, norm1_shift, b_down, norm2_gain, norm2_shift, b_in]
    a0, tok0 = kernel(
        prep_first_kernel, [sds((rows + 16, half), BF), sds((seqs, shard + 16, width), BF)],
        ([smem(), whole(seqs, shard, width), whole(seqs, shard)] + [pl.BlockSpec((rows, cols), lambda i: (0, 0))] * 3
         + [whole(1, v.shape[0]) for v in vectors], [whole(rows + 16, half), whole(seqs, shard + 16, width)]),
        (scal, tokens, doc_ids, w_query, w_key, w_value, *[v.reshape(1, -1) for v in vectors]),
        grid=(1,), moved=10**6, name="prep_first", limit=60,
    )

    def exchange(held):
        return [held] + [swap_by(held, "seq", n, step) for step in far_steps(far)]

    def join(parts, name):
        lead = parts[0].ndim == 3
        shape = (2, 4, *parts[0].shape[1:]) if lead else (4, *parts[0].shape)
        out, = kernel(join_kernel, [sds(shape, BF)], ([vmem()] * 4, [vmem()]), parts, moved=10**6, name=name)
        for bit in near[:-1]:
            out = jnp.concatenate([out, swap(out, "seq", n, bit)], 1 if lead else 0)
        return out

    a_lo = join(exchange(a0), "join_a")
    a1, a2, ffq = kernel(
        prep_kernel,
        [sds((rows, half), BF), sds((rows, 2 * half), BF), sds((2, rows, width), BF)],
        ([smem()] + [vmem()] * 6, [vmem()] * 3),
        (after(scal, a0), w_query, w_key, w_value, w_out, w_in, w_down),
        moved=6 * 10**6, name="prep", limit=60,
    )
    tok2 = by_y(tok0)
    tok1 = by_core(tok0)
    ag_lo = by_core(a_lo)
    a_hi = by_x(a_lo)
    b_parts = exchange(after(a1, a_lo))
    tok3 = by_core(after(tok2, a_hi))
    tok = (tok0, tok1, tok2, tok3)
    ag_hi = by_core(a_hi)
    f_parts = exchange(after(ffq, a_lo))
    vecs, bin_all = kernel(
        functools.partial(vector_kernel, order, n, rows, sub),
        [sds((8, width), F32), sds((4, 1, width), F32)],
        ([smem()] + [vmem()] * 2, [vmem()] * 2), (scal, a_lo, a_hi), moved=10**6, name="vectors",
    )

    raw = None
    kept = []

    def attend(g, s, scal, arrays):
        nonlocal raw
        big = pl.BlockSpec((1, 1, shard, length), lambda h: (s, g * per + h, 0, 0))
        tok_spec = pl.BlockSpec((1, shard + 16, width), lambda h: (s, 0, 0))
        block = 0
        w_spec = pl.BlockSpec((m, arrays[0].shape[1], half), lambda h: (0, 0, block))
        args = [scal, *tok, doc_ids, *arrays, vecs, prior_logits]
        specs = [smem()] + [tok_spec] * 4 + [vmem()] + [w_spec] * 4 + [pl.BlockSpec((8, cols), lambda h: (0, g)), big]
        alias = {}
        if raw is not None:
            alias = {len(args): 0}
            args.append(raw)
            specs.append(hbm)
        raw, *rest = kernel(
            functools.partial(attend_kernel, order, n, s, g, raw is not None),
            [sds(prior_logits.shape, BF), pltpu.HBM((per, shard, length), BF), sds((shard, cols), BF),
             sds((length, cols), BF), sds((length, cols), BF), sds((shard, cols), F32), sds((shard, cols), F32)],
            (specs, [big, pl.BlockSpec((1, shard, length), lambda h: (h, 0, 0)), whole(shard, cols), whole(length, cols),
                     whole(length, cols), whole(shard, cols), whole(shard, cols)]),
            args, [VM((width, 3 * cols), BF), VM((cols, length), BF), VM((shard, length), F32), VM((2, length, cols), BF)],
            grid=(per,), alias=alias, flops=5 * 10**9, moved=10 * 10**6, exps=10**6, name=f"attend{g}{s}", limit=24,
        )
        kept.append(rest)
        return rest[2]

    a_set = (a_lo, a_hi, ag_lo, ag_hi)
    attend(0, 0, after(scal, vecs), a_set)
    mark = kept[-1][4]
    b_lo = join([after(x, mark) for x in b_parts], "join_b")
    b_hi = by_x(b_lo)
    bg_lo = by_core(b_lo)
    attend(0, 1, after(scal, b_lo), a_set)
    mark = kept[-1][4]
    bg_hi = by_core(after(b_hi, mark))
    b_set = (b_lo, b_hi, bg_lo, bg_hi)
    f_lo = join([after(x, mark) for x in f_parts], "join_f")
    f_hi, f_ylo = by_x(f_lo), by_y(f_lo)
    fc_lo = by_core(f_lo)
    c_parts = exchange(after(a2, f_lo))
    attend(1, 0, after(scal, f_lo), b_set)
    mark = kept[-1][4]
    c_lo = join([after(x, mark) for x in c_parts], "join_c")
    c_hi = by_x(c_lo)
    cg_lo = by_core(c_lo)
    attend(1, 1, after(scal, c_lo), b_set)
    x_t, = kernel(turn_kernel, [pltpu.HBM((seqs, width, length), BF)], ([smem()] + [vmem()] * 4, [vmem()]),
                  (after(scal, kept[-1][4]), *tok), moved=12 * 10**6, name="turn")
    f_yhi_i, f_yhi_d = by_y(after(f_hi, x_t)[0]), by_x(after(f_ylo, x_t)[1])
    fc_hi, fc_ylo = by_core(after(f_hi, x_t)), by_core(after(f_ylo, x_t))
    cg_hi = by_core(after(c_hi, x_t))
    c_set = (c_lo, c_hi, cg_lo, cg_hi)
    attend(2, 0, after(scal, x_t), c_set)
    attend(2, 1, scal, c_set)
    mark = kept[-1][4]
    fc_yhi_i, fc_yhi_d = by_core(after(f_yhi_i, mark)), by_core(after(f_yhi_d, mark))
    f = (f_lo, f_hi, f_ylo, f_yhi_i, f_yhi_d, fc_lo, fc_hi, fc_ylo, fc_yhi_i, fc_yhi_d)

    o_spec = pl.BlockSpec((m, rows, half), lambda i: (0, 0, 1))
    w_scratch = VM((4, n, rows, width), BF)
    w_one = VM((width, width), BF)
    sems = pltpu.SemaphoreType.DMA((8,))
    output, mixed, first_n, inv1, inner, hid, dg, dsum2, dsec, ff2 = kernel(
        functools.partial(forward_kernel, order, n),
        [
            sds((seqs, shard, width), BF), sds((n_rows, width), BF), sds((n_rows, width), F32), sds((n_rows, 1), F32),
            sds((n_rows, width), BF), sds((4, n_rows, width), BF), sds((4, n_rows, width), BF),
            sds((n_rows, width), F32), sds((n_rows, width), BF), sds((8, width), F32),
        ],
        ([smem()] + [vmem()] * 10 + [o_spec] * 4 + [hbm] * 10, [vmem()] * 10),
        (scal, *[k[4] for k in kept], tokens, cotangent, vecs, bin_all, *c_set, *f),
        [VM((width, width), BF), w_scratch, w_scratch, w_one, VM((n_rows, width), F32), VM((n_rows, width), F32), sems, sems],
        grid=(1,), flops=6 * 10**9, moved=25 * 10**6, exps=2 * 10**6, name="ff_fwd", limit=48,
    )
    def quarter(i):
        return (jnp.where(i < 2, 2 * i + 1, 2 * i - 4), 0, 0)

    pair = [sds((2, n, rows, width), BF)] * 2
    d_keep, d_send = kernel(
        functools.partial(down_grad_kernel, order, n), pair,
        ([smem()] + [vmem()] * 2, [vmem()] * 2), (scal, hid, dsec), flops=3 * 10**9, moved=8 * 10**6, name="down_grad", limit=24,
    )
    d_got = by_core(d_send)
    dx_send = add(d_keep[:, m:], d_got[:, m:])
    i_keep, i_send, dpre, gbin = kernel(
        functools.partial(in_grad_kernel, order, n),
        pair + [sds((4, n_rows, width), BF), sds((4, 1, width), F32)],
        ([smem(), whole(n_rows, width), pl.BlockSpec((1, n_rows, width), quarter), whole(n_rows, width)] + [hbm] * 10,
         [pl.BlockSpec((1, n, rows, width), lambda i: (jnp.maximum(i - 2, 0), 0, 0, 0)),
          pl.BlockSpec((1, n, rows, width), lambda i: (jnp.minimum(i, 1), 0, 0, 0)),
          pl.BlockSpec((1, n_rows, width), quarter), whole(4, 1, width)]),
        (after(scal, d_keep), inner, dg, dsec, *f), [w_scratch, w_one, sems], grid=(4,), flops=6 * 10**9, moved=20 * 10**6, name="in_grad", limit=40,
    )
    i_got = by_core(i_send)
    go_keep, go_send, dsum1, dmix, ff1 = kernel(
        functools.partial(first_grad_kernel, order, n),
        [sds((n, rows, half), BF)] * 2 + [sds((n_rows, width), F32), sds((n_rows, width), BF), sds((8, width), F32)],
        ([smem()] + [vmem()] * 6 + [o_spec] * 4 + [hbm] * 10, [vmem()] * 5),
        (after(scal, dx_send), mixed, first_n, inv1, dpre, dsum2, vecs, *c_set, *f), [VM((width, width), BF), w_scratch, w_one, sems],
        grid=(1,), flops=4 * 10**9, moved=15 * 10**6, name="first_grad", limit=40,
    )

    gp = None
    dqs, dkvs, vgs = [], [], []

    def back(g, s, scal):
        nonlocal gp
        e, q, k, v, o, inv = kept[g * seqs + s]
        big = pl.BlockSpec((1, 1, shard, length), lambda h: (s, g * per + h, 0, 0))
        args = [scal, e, dmix, q, k, v, o, inv]
        specs = [smem(), pl.BlockSpec((1, shard, length), lambda h: (h, 0, 0)),
                 pl.BlockSpec((shard, cols), lambda h: (s, g)),
                 whole(shard, cols), whole(length, cols), whole(length, cols), whole(shard, cols), whole(shard, cols)]
        alias = {}
        if gp is not None:
            alias = {len(args): 0}
            args.append(gp)
            specs.append(hbm)
        gp, dq, dkv = kernel(
            functools.partial(attend_back_kernel, gp is not None),
            [sds(prior_logits.shape, BF), sds((shard, cols), BF), sds((length, 2 * cols), BF)],
            (specs, [big, whole(shard, cols), whole(length, 2 * cols)]),
            args,
            [VM((cols, length), BF), VM((cols, shard), BF), VM((cols, shard), BF), VM((shard, cols), BF),
             VM((shard, cols), F32), VM((cols, length), BF), VM((cols, length), BF), VM((shard, cols), F32)],
            grid=(per,), alias=alias, flops=5 * 10**9, moved=10 * 10**6, name=f"back{g}{s}", limit=24,
        )
        dqs.append(dq)
        dkvs.append(dkv)
        return dq

    def weight_grad(g, scal):
        extra = ([go_keep, go_send], [], vgs + [ff1, ff2, gbin])[g]
        shape = ((2, n, rows, half), (n, rows, half), (n, rows + 16, half))[g]
        keep, send, vg = kernel(
            functools.partial(weight_grad_kernel, order, n, g, sub),
            [sds(shape, BF)] * 2 + [sds((8, cols), F32)],
            ([smem()] + [vmem()] * (5 + len(extra)), [vmem()] * 3),
            (scal, x_t, *dqs[-2:], *dkvs[-2:], *extra),
            flops=2 * 10**9, moved=8 * 10**6, name=f"weight_grad{g}", limit=24,
        )
        vgs.append(vg)
        return keep, send, vg

    def rest_near(held, axis, plus):
        for bit in reversed(near[:-1]):
            k = held.shape[axis] // 2
            keep = lax.slice_in_dim(held, 0, k, axis=axis)
            held = plus(keep, swap(lax.slice_in_dim(held, k, 2 * k, axis=axis), "seq", n, bit))
        return held

    def far_sum(blocks, plus):
        got = [swap_by(b, "seq", n, step) for b, step in zip(blocks[1:], far_steps(far))]
        return plus(blocks[0], *got)

    def plus_table(*parts):
        flat = parts[0].ndim == 2
        parts = [p[None] if flat else p for p in parts]
        out, = kernel(functools.partial(sum_kernel, rows), [sds(parts[0].shape, BF)],
                      ([vmem()] * len(parts), [vmem()]), parts, moved=10**6, name="sum_table")
        return out[0] if flat else out

    dx_got = by_x(dx_send)
    iy_send = add(i_keep[1], i_got[1])
    iy_got = by_y(iy_send)
    back(0, 0, after(scal, iy_send))
    mark = back(0, 1, scal)
    dx_got = after(dx_got, mark)
    dy_send = add(d_keep[1, :m], d_got[1, :m], dx_got[1])
    dy_got = by_y(dy_send)
    g0_keep, g0_send, _ = weight_grad(0, after(scal, dy_send))
    g0_got = by_core(g0_send)
    mark = back(1, 0, after(scal, g0_keep))
    iy_got = after(iy_got, mark)
    ix_send = add(i_keep[0, m:], i_got[0, m:], iy_got[m:])
    ix_got = by_x(ix_send)
    g0y_send = add(after(g0_keep, mark)[1], g0_got[1])
    g0y_got = by_y(g0y_send)
    back(1, 1, after(scal, ix_send, g0y_send))
    g1_keep, g1_send, mark = weight_grad(1, scal)
    g1_got = by_core(g1_send)
    dl = add(after(d_keep, mark)[0, :m], d_got[0, :m], dx_got[0], dy_got)
    il = add(after(i_keep, mark)[0, :m], i_got[0, :m], iy_got[:m], ix_got)
    lo = rest_near(jnp.stack([il, dl], 1), 0, add)
    ff_got = [swap_by(lo[i + 1], "seq", n, step) for i, step in enumerate(far_steps(far))]
    g0y_got = after(g0y_got, mark)
    g0x_send = add(g0_keep[0, m:], g0_got[0, m:], g0y_got[m:])
    g0x_got = by_x(g0x_send)
    mark = back(2, 0, after(scal, lo, g0x_send))
    g1x_send = add(after(g1_keep, mark)[m:], g1_got[m:])
    g1x_got = by_x(g1x_send)
    g0 = rest_near(add(after(g0_keep, mark)[0, :m], g0_got[0, :m], g0y_got[:m], g0x_got), 0, add)
    g0_far = [swap_by(g0[i + 1], "seq", n, step) for i, step in enumerate(far_steps(far))]
    back(2, 1, after(scal, g0, g1x_send))
    g2_keep, g2_send, mark = weight_grad(2, scal)
    g2_got = by_core(g2_send)
    ff = add(after(lo, mark)[0], *ff_got)
    ff_y = by_y(ff)
    g1 = rest_near(add(after(g1_keep, mark)[:m], g1_got[:m], g1x_got), 0, add)
    g1_far = [swap_by(g1[i + 1], "seq", n, step) for i, step in enumerate(far_steps(far))]
    g0 = add(after(g0, mark)[0], *g0_far)
    g0_y = by_y(g0)
    g2x_send = plus_table(g2_keep[m:], g2_got[m:])
    g2x_got = by_x(g2x_send)
    all_sets = (*a_set, *b_set, *c_set)
    set_specs = [whole(m, a.shape[1], half) for a in a_set + b_set] + [whole(m, rows, half)] * 4
    w_all = VM((GROUPS, width, 3 * cols), BF)
    far_a, far_b = kernel(
        functools.partial(token_kernel, order, n, False),
        [sds((2, seqs, shard, width), BF), sds((seqs, shard, width), BF)],
        ([smem()] + [vmem()] * 12 + set_specs, [vmem()] * 2),
        (after(scal, mark, g1, g0, ff, g2x_send), *dqs, *dkvs, *all_sets),
        [w_all], grid=(1,), flops=6 * 10**9, moved=15 * 10**6, name="token_far", limit=30,
    )
    far_got = by_core(far_a)
    g1 = add(after(g1, far_b)[0], *g1_far)
    g1_y = by_y(g1)
    g2 = rest_near(plus_table(g2_keep[:m], g2_got[:m], after(g2x_got, far_b)), 0, plus_table)
    g2_far = [swap_by(g2[i + 1], "seq", n, step) for i, step in enumerate(far_steps(far))]
    across = by_y(add(far_b, far_got[1]))
    own_part, = kernel(
        functools.partial(token_kernel, order, n, True),
        [sds((seqs, shard, width), F32)],
        ([smem()] + [vmem()] * 12 + set_specs + [vmem()], [vmem()]),
        (after(scal, far_b, g2, g1), *dqs, *dkvs, *all_sets, dsum1),
        [w_all], grid=(1,), flops=4 * 10**9, moved=15 * 10**6, name="token_own", limit=30,
    )
    two = jnp.stack([ff, ff_y], 1)
    two_got = by_core(two)
    g_wi, g_wd = kernel(
        functools.partial(finish_ff_kernel, sub, n), [sds(w.shape, F32) for w in (w_in, w_down)],
        ([smem()] + [vmem()] * 4, [vmem()] * 2), (after(scal, own_part), two[1], two_got[1], two[0], two_got[0]),
        moved=4 * 10**6, name="finish_ff",
    )
    g1 = add(after(g1, own_part), g1_y)
    g2 = plus_table(after(g2, g_wi)[0], *g2_far)
    g2 = plus_table(g2, by_y(g2))
    g0 = jnp.stack([g0, g0_y])
    grad_tokens = own_part + far_got[0].astype(F32) + across.astype(F32)
    g_wq, g_wk, g_wv, g_wo, table = kernel(
        functools.partial(finish_kernel, rows),
        [sds(w.shape, F32) for w in (w_query, w_key, w_value, w_out)] + [sds((8, half), F32)],
        ([smem()] + [vmem()] * 6, [vmem()] * 5),
        (scal, g0, by_core(g0), g1, by_core(g1), g2, by_core(g2)),
        moved=4 * 10**6, name="finish",
    )
    table = table.reshape(-1)
    cut = [table[i * rows:(i + 1) * rows] for i in range(8)]
    g_bq, g_bv, g_bo, g_g1, g_s1, g_bd, g_g2, g_s2 = cut
    g_bin = table[8 * rows:8 * rows + 4 * sub]
    return (
        output, raw, grad_tokens, gp, g_wq, g_wk, g_wv, g_wo,
        g_bq, g_bv, g_bo, g_g1, g_s1, g_wi, g_bin, g_wd, g_bd, g_g2, g_s2,
    )


def solution(mesh):
    n = mesh.shape["seq"]
    top = n.bit_length() - 1
    far, near = (top - 2, top - 1), tuple(reversed(range(top - 2)))
    in_specs = (
        P("seq", "ctx", None), P("seq", None, "ctx", None), P("seq", "ctx"),
        P("seq", None), P("seq", None), P("seq", None), P("seq", None),
        P("seq"), P("seq"), P("seq"), P("seq"), P("seq"),
        P("seq", None), P("seq"), P("seq", None), P("seq"), P("seq"), P("seq"),
        P("seq", "ctx", None),
    )
    out_specs = (
        P("seq", "ctx", None), P("seq", None, "ctx", None), P("seq", "ctx", None), P("seq", None, "ctx", None),
        P("seq", None), P("seq", None), P("seq", None), P("seq", None),
        P("seq"), P("seq"), P("seq"), P("seq"), P("seq"),
        P("seq", None), P("seq"), P("seq", None), P("seq"), P("seq"), P("seq"),
    )
    return jax.shard_map(
        functools.partial(on_device, n, far, near),
        mesh=mesh, in_specs=in_specs, out_specs=out_specs, check_vma=False,
    )
```

```python
import functools
import math

import jax
import jax.numpy as jnp
from jax import lax
from jax.experimental import pallas as pl
from jax.experimental.pallas import tpu as pltpu
from jax.sharding import PartitionSpec as P

EPSILON = 1e-05
NEGATIVE = -1e30
BF = jnp.bfloat16
F32 = jnp.float32
VM = pltpu.VMEM
ANY = pl.ANY
GROUPS = 3


def dot(a, b):
    return lax.dot_general(a, b, (((1,), (0,)), ((), ())), preferred_element_type=F32)


def dot_nt(a, b):
    return lax.dot_general(a, b, (((1,), (1,)), ((), ())), preferred_element_type=F32)


def dot_tn(a, b):
    return lax.dot_general(a, b, (((0,), (0,)), ((), ())), preferred_element_type=F32)


def vmem(shape=None, index=None):
    if shape is None:
        return pl.BlockSpec(memory_space=VM)
    return pl.BlockSpec(shape, index)


def params(n_grid, limit):
    return pltpu.CompilerParams(
        vmem_limit_bytes=limit * 1024 * 1024,
        dimension_semantics=("arbitrary",) * n_grid if n_grid else None,
    )


def smem():
    return pl.BlockSpec(memory_space=pltpu.SMEM)


def after(value, *marks):
    return lax.optimization_barrier((value, *marks))[0]


def swap_by(value, axis, size, step):
    return lax.ppermute(value, axis, [(i, i ^ step) for i in range(size)])


def swap(value, axis, size, bit):
    return swap_by(value, axis, size, 1 << bit)


def far_steps(far):
    a, b = 1 << far[0], 1 << far[1]
    return (a, b, a | b)


def add(*parts):
    total = parts[0].astype(F32)
    for part in parts[1:]:
        total = total + part.astype(F32)
    return total.astype(BF)


def place(index, order):
    out = 0
    for step, bit in enumerate(order):
        out = out | (((index >> bit) & 1) << step)
    return out


def column_half(wq, wk, wv, g, half, low):
    cols = (2 * half) // 3
    cut = half - cols
    at = g * cols
    first = jnp.concatenate([wq[:, at:at + cols], wk[:, at:at + cut]], 1)
    second = jnp.concatenate([wk[:, at + cut:at + cols], wv[:, at:at + cols]], 1)
    return jnp.where(low, first, second)


def prep_first_kernel(scal, tok, docs, wq, wk, wv, *rest):
    vecs, (a0, tok_ref) = rest[:9], rest[9:]
    seqs, shard = tok.shape[:2]
    rows = wq.shape[0]
    half = a0.shape[1]
    for s in range(seqs):
        tok_ref[s, :shard, :] = tok[s]
        tok_ref[s, shard:, :] = jnp.zeros_like(tok_ref[s, shard:, :])
        tok_ref[s, shard:shard + 1, :shard] = docs[s:s + 1, :].astype(F32).astype(BF)
    a0[:rows] = column_half(wq, wk, wv, 0, half, scal[2] == 0)
    p = 0
    lines = []
    line = []
    for v in vecs:
        step = rows if v.shape[1] == rows else v.shape[1] // 4
        for i in range(v.shape[1] // step):
            line.append(v[:, i * step:(i + 1) * step].astype(F32))
            p += step
            if p % half == 0:
                lines.append(jnp.concatenate(line, 1))
                line = []
    if line:
        line.append(jnp.zeros((1, half - p % half), F32))
        lines.append(jnp.concatenate(line, 1))
    lines.append(jnp.zeros((16 - len(lines), half), F32))
    a0[rows:] = jnp.concatenate(lines, 0).astype(BF)


def prep_kernel(scal, wq, wk, wv, wo, wi, wd, a1, ffq):
    mc, core = scal[1], scal[2]
    my_y = mc >> 1
    width = wq.shape[1]
    half = a1.shape[1] // 3
    low = core == 0
    sub = ffq.shape[1]
    a1[:, :half] = column_half(wq, wk, wv, 1, half, low)
    a1[:, half:2 * half] = column_half(wq, wk, wv, 2, half, low)
    a1[:, 2 * half:] = jnp.where(low, wo[:, :half], wo[:, half:])
    block = 2 * core + my_y
    ffq[1] = wd[pl.ds(pl.multiple_of(block * sub, sub), sub), :]
    for s in range(width // sub):
        got = [wi[:, (4 * s + b) * sub:(4 * s + b + 1) * sub] for b in range(4)]
        near = jnp.where(my_y == 0, got[0], got[1])
        far = jnp.where(my_y == 0, got[2], got[3])
        ffq[0, :, s * sub:(s + 1) * sub] = jnp.where(low, near, far)


def join_kernel(a, b, c, d, out):
    lead = out.ndim == 4
    for i, ref in enumerate((a, b, c, d)):
        if lead:
            out[:, i] = ref[...]
        else:
            out[i] = ref[...]


def fetch(lo, hi, at):
    m = lo.shape[0]
    return jnp.where(at < m, lo[at & (m - 1)], hi[at & (m - 1)])


def join_split_kernel(a, b, c, d, first, second):
    half = first.shape[2]
    for i, ref in enumerate((a, b, c, d)):
        first[i] = ref[:, :half]
        second[i] = ref[:, half:]


def join_pair_kernel(a, b, out):
    k = a.shape[1]
    out[:, :k] = a[...]
    out[:, k:] = b[...]


def pair_kernel(a, b, near, far):
    half = a.shape[2]
    for i in range(4):
        out = near if i < 2 else far
        out[i % 2, :, :half] = a[i]
        out[i % 2, :, half:] = b[i]


def ends_kernel(rows, p0, p1, p2, p3, pair, out):
    total = p0[...].astype(F32) + p1[...].astype(F32) + p2[...].astype(F32) + p3[...].astype(F32)
    out[:rows] = total[:rows].astype(BF)
    value = total[rows:rows + 8] + total[rows + 8:]
    high = value.astype(BF).astype(F32)
    out[rows:rows + 16] = jnp.concatenate([high, value - high], 0).astype(BF)
    half = out.shape[1]
    out[rows + 16:2 * rows + 16] = pair[:, :half]
    out[2 * rows + 16:] = pair[:, half:]


def weights_in(out, order, pm, core, rows, shards, held):
    first = core == 0
    m = held[0].shape[0]
    half = held[0].shape[2]
    for i in range(shards):
        at = place(i, order) ^ pm
        spot = at & (m - 1)
        in_lo = at < m
        four = [ref[spot, :rows, :] for ref in held]
        mine = jnp.where(in_lo, four[0], four[1])
        other = jnp.where(in_lo, four[2], four[3])
        out[i * rows:(i + 1) * rows, :half] = jnp.where(first, mine, other)
        out[i * rows:(i + 1) * rows, half:2 * half] = jnp.where(first, other, mine)


def vector_kernel(order, shards, rows, sub, scal, lo, hi, vec_ref, bin_ref):
    pm = scal[0]
    half = lo.shape[2]
    m = lo.shape[0]
    for s in range(shards):
        at = place(s, order) ^ pm
        block = jnp.where(at < m, lo[at & (m - 1), rows:, :], hi[at & (m - 1), rows:, :]).astype(F32)
        for i in range(8):
            p = i * rows
            vec_ref[i:i + 1, s * rows:(s + 1) * rows] = block[p // half:p // half + 1, p % half:p % half + rows]
        for b in range(4):
            p = 8 * rows + b * sub
            c = 2 * (b & 1) + (b >> 1)
            bin_ref[c, :, s * sub:(s + 1) * sub] = block[p // half:p // half + 1, p % half:p % half + sub]


def turn_kernel(scal, t0, t1, t2, t3, out_ref):
    mc = scal[1]
    seqs, _, width = t0.shape
    shard = out_ref.shape[2] // 4
    for j, tok in enumerate((t0, t1, t2, t3)):
        where = pl.multiple_of((mc ^ j) * shard, shard)
        for s in range(seqs):
            out_ref[s, :, pl.ds(where, shard)] = tok[s, :shard, :].T


def attend_kernel(
    order, shards, seq, group, aliased,
    scal, t0, t1, t2, t3, doc_ref, bias_ref, prior_ref, *rest,
):
    held, rest = rest[:4], rest[4:]
    if aliased:
        rest = rest[1:]
    raw_ref, e_ref, q_ref, k_ref, v_ref, o_ref, inv_ref, w_s, kt_s, mask_s, vx_s = rest
    h = pl.program_id(0)
    pm, mc, core = scal[0], scal[1], scal[2]
    rows = w_s.shape[0] // shards
    shard, cols = q_ref.shape
    head = cols // 4

    @pl.when(h == 0)
    def _():
        weights_in(w_s, order, pm, core, rows, shards, held)
        q = dot(t0[0, :shard, :], w_s[:, :cols]) + bias_ref[0:1, :]
        q_ref[...] = (q.astype(BF).astype(F32) * (1.0 / math.sqrt(head))).astype(BF)
        mine = jnp.broadcast_to(doc_ref[seq:seq + 1, :].astype(F32), (128, shard)).T[:, :1]
        for j, tok in enumerate((t0, t1, t2, t3)):
            where = pl.multiple_of((mc ^ j) * shard, shard)
            kv = dot(tok[0, :shard, :], w_s[:, cols:])
            k_ref[pl.ds(where, shard), :] = kv[:, :cols].astype(BF)
            v = kv[:, cols:] + bias_ref[1:2, :]
            v_ref[pl.ds(where, shard), :] = v.astype(BF)
            even = (lax.broadcasted_iota(jnp.int32, (shard, cols), 1) // head) % 2 == 0
            vx_s[0, pl.ds(where, shard), :] = jnp.where(even, v, 1.0).astype(BF)
            vx_s[1, pl.ds(where, shard), :] = jnp.where(even, 1.0, v).astype(BF)
            docs = tok[0, shard:shard + 1, :shard].astype(F32)
            mask_s[:, pl.ds(where, shard)] = jnp.where(mine == docs, 0.0, NEGATIVE)
        kt_s[...] = k_ref[...].T

    lane = lax.broadcasted_iota(jnp.int32, (shard, cols), 1) // head
    this = lane == h
    qm = jnp.where(this, q_ref[...].astype(F32), 0.0).astype(BF)
    step = 64
    for r in range(0, shard, step):
        logits = dot(qm[r:r + step], kt_s[...]) + prior_ref[0, 0, r:r + step, :].astype(F32)
        raw_ref[0, 0, r:r + step, :] = logits.astype(BF)
        masked = logits + mask_s[r:r + step, :]
        top = jnp.max(masked, -1, keepdims=True)
        e_ref[0, r:r + step, :] = jnp.exp(masked - top).astype(BF)
    o = dot(e_ref[0], vx_s[h & 1])
    total = jnp.max(jnp.where(lane == (h ^ 1), o, 0.0), -1, keepdims=True)
    inv = 1.0 / total
    o_ref[...] = jnp.where(this, o * inv, o_ref[...])
    inv_ref[...] = jnp.where(this, inv, inv_ref[...])


def gelu_parts(x):
    z = jnp.abs(x) * 0.7071067811865476
    t = 1.0 / (1.0 + 0.3275911 * z)
    e = jnp.exp(-0.5 * x * x)
    poly = t * (0.254829592 + t * (-0.284496736 + t * (1.421413741 + t * (-1.453152027 + t * 1.061405429))))
    tail = 0.5 * poly * e
    phi = jnp.where(x >= 0, 1.0 - tail, tail)
    return x * phi, phi + x * (e * 0.3989422804014327)


def moments(x):
    mean = jnp.mean(x, -1, keepdims=True)
    centered = x - mean
    inverse = lax.rsqrt(jnp.mean(centered * centered, -1, keepdims=True) + EPSILON)
    return centered * inverse, inverse


def norm_back(grad, normed, inverse, gain):
    scaled = grad * gain
    return inverse * (
        scaled - jnp.mean(scaled, -1, keepdims=True)
        - normed * jnp.mean(scaled * normed, -1, keepdims=True)
    )


def ff_sources(f, which):
    lo, hi, ylo, yhi_i, yhi_d, clo, chi, cylo, cyhi_i, cyhi_d = f
    yhi, cyhi = (yhi_i, cyhi_i) if which == 0 else (yhi_d, cyhi_d)
    return [(lo.at[which], hi.at[which]), (clo.at[which], chi.at[which]),
            (ylo.at[which], yhi), (cylo.at[which], cyhi)]


def ff_copies(f, which, held, sem):
    out = []
    for j, halves in enumerate(ff_sources(f, which)):
        m = halves[0].shape[0]
        out.append([pltpu.make_async_copy(src, held.at[j, pl.ds(i * m, m)], sem.at[2 * j + i])
                    for i, src in enumerate(halves)])
    for pair in out:
        for copy in pair:
            copy.start()
    return out


def ff_wait(copies, j, held, order, pm, shards, rows, out):
    for copy in copies[j]:
        copy.wait()
    for s in range(shards):
        out[s * rows:(s + 1) * rows] = held[j, place(s, order) ^ pm]


def forward_kernel(
    order, shards,
    scal, o00, o01, o10, o11, o20, o21, tok_ref, cot_ref, vec_ref, bin_ref, *rest,
):
    held, f, rest = rest[:4], rest[4:14], rest[14:]
    (out_ref, mix_ref, first_n_ref, inv1_ref, inner_ref, hid_ref, dg_ref, dsum2_ref, dsec_ref, vg_ref,
     wo_s, wi_s, wd_s, w_s, first_s, acc_s, isem, dsem) = rest
    pm, mc, core = scal[0], scal[1], scal[2]
    seqs, shard, width = tok_ref.shape
    rows = width // shards
    n_rows = seqs * shard
    in_copies = ff_copies(f, 0, wi_s, isem)
    down_copies = ff_copies(f, 1, wd_s, dsem)
    weights_in(wo_s, order, pm, core, rows, shards, held)
    mixed = jnp.concatenate(
        [jnp.concatenate([a[...].astype(BF), b[...].astype(BF)], 0) for a, b in ((o00, o01), (o10, o11), (o20, o21))], 1)
    mix_ref[...] = mixed
    tokens = tok_ref[...].reshape(n_rows, width).astype(F32)
    normed, inverse = moments(tokens + (dot(mixed, wo_s[...]) + vec_ref[2:3, :]))
    first_n_ref[...] = normed
    inv1_ref[...] = inverse
    first = normed * vec_ref[3:4, :] + vec_ref[4:5, :]
    first_s[...] = first
    inner_ref[...] = first.astype(BF)
    for j in range(4):
        ff_wait(in_copies, j, wi_s, order, pm, shards, rows, w_s)
        for r in range(0, n_rows, 128):
            pre = dot(inner_ref[r:r + 128, :], w_s[...]) + bin_ref[mc ^ j]
            hid, dg = gelu_parts(pre)
            hid_ref[j, r:r + 128, :] = hid.astype(BF)
            dg_ref[j, r:r + 128, :] = dg.astype(BF)
        ff_wait(down_copies, j, wd_s, order, pm, shards, rows, w_s)
        part = dot(hid_ref[j], w_s[...])
        acc_s[...] = part if j == 0 else acc_s[...] + part
    normed, inverse = moments(first_s[...] + (acc_s[...] + vec_ref[5:6, :]))
    gain = vec_ref[6:7, :]
    out_ref[...] = (normed * gain + vec_ref[7:8, :]).astype(BF).reshape(seqs, shard, width)
    dy = cot_ref[...].reshape(n_rows, width).astype(F32)
    dsum2 = norm_back(dy, normed, inverse, gain)
    dsum2_ref[...] = dsum2
    dsec = dsum2.astype(BF)
    dsec_ref[...] = dsec
    vg_ref[0:1, :] = jnp.sum(dy * normed, 0, keepdims=True)
    vg_ref[1:2, :] = jnp.sum(dy, 0, keepdims=True)
    vg_ref[2:3, :] = jnp.sum(dsec.astype(F32), 0, keepdims=True)


def down_grad_kernel(order, shards, scal, hid, dsec, keep, send):
    pm = scal[0]
    sub = keep.shape[2]
    for j in (1, 3, 0, 2):
        out = keep if j % 2 == 0 else send
        grad = dot_tn(hid[j], dsec[...]).astype(BF)
        for s in range(shards):
            out[j >> 1, place(s, order) ^ pm] = grad[s * sub:(s + 1) * sub]


def in_grad_kernel(order, shards, scal, inner, dg, dsec, *rest):
    f, (keep, send, dpre_ref, gbin_ref, wd_s, w_s, sem) = rest[:10], rest[10:]
    pm, mc = scal[0], scal[1]
    rows = keep.shape[2]
    step = pl.program_id(0)

    @pl.when(step == 0)
    def _():
        ff_copies(f, 1, wd_s, sem)

    for i, j in enumerate((1, 3, 0, 2)):
        @pl.when(step == i)
        def _(j=j):
            copies = {j: [pltpu.make_async_copy(src, wd_s.at[j, pl.ds(k * src.shape[0], src.shape[0])], sem.at[2 * j + k])
                          for k, src in enumerate(ff_sources(f, 1)[j])]}
            ff_wait(copies, j, wd_s, order, pm, shards, rows, w_s)

    j = jnp.where(step < 2, 2 * step + 1, 2 * step - 4)
    dpre = (dot_nt(dsec[...], w_s[...]) * dg[0].astype(F32)).astype(BF)
    dpre_ref[0] = dpre
    gbin_ref[mc ^ j] = jnp.sum(dpre.astype(F32), 0, keepdims=True)
    grad = dot_tn(inner[...], dpre).astype(BF)

    @pl.when(step < 2)
    def _():
        for s in range(shards):
            send[0, place(s, order) ^ pm] = grad[s * rows:(s + 1) * rows]

    @pl.when(step >= 2)
    def _():
        for s in range(shards):
            keep[0, place(s, order) ^ pm] = grad[s * rows:(s + 1) * rows]


def first_grad_kernel(
    order, shards, scal, mix_ref, first_n, inv1, dpre, dsum2, vec_ref, *rest,
):
    held, rest = rest[:4], rest[4:]
    f, (go_keep, go_send, dsum1_ref, dmix_ref, vg_ref, wo_s, wi_s, w_s, sem) = rest[:10], rest[10:]
    pm, core = scal[0], scal[2]
    n_rows, width = dsum2.shape
    rows = width // shards
    half = width // 2
    in_copies = ff_copies(f, 0, wi_s, sem)
    weights_in(wo_s, order, pm, core, rows, shards, held)
    dfirst = dsum2[...]
    for j in range(4):
        ff_wait(in_copies, j, wi_s, order, pm, shards, rows, w_s)
        dfirst = dfirst + dot_nt(dpre[j], w_s[...])
    normed = first_n[...]
    dsum1 = norm_back(dfirst, normed, inv1[...], vec_ref[3:4, :])
    dsum1_ref[...] = dsum1
    dbranch = dsum1.astype(BF)
    vg_ref[0:1, :] = jnp.sum(dfirst * normed, 0, keepdims=True)
    vg_ref[1:2, :] = jnp.sum(dfirst, 0, keepdims=True)
    vg_ref[2:3, :] = jnp.sum(dbranch.astype(F32), 0, keepdims=True)
    dmix_ref[...] = dot_nt(dbranch, wo_s[...]).astype(BF)
    grad_o = dot_tn(mix_ref[...], dbranch).astype(BF)
    first_core = core == 0
    for s in range(shards):
        block = grad_o[s * rows:(s + 1) * rows]
        at = place(s, order) ^ pm
        go_keep[at] = jnp.where(first_core, block[:, :half], block[:, half:])
        go_send[at] = jnp.where(first_core, block[:, half:], block[:, :half])


def attend_back_kernel(
    aliased,
    scal, e_ref, dm_ref, q_ref, k_ref, v_ref, o_ref, inv_ref, *rest,
):
    if aliased:
        rest = rest[1:]
    gp_ref, dq_ref, dkv_ref, vt_s, qt_s, dmt_s, dmi_s, dl_s, dkt_s, dvt_s, dq_s = rest
    h = pl.program_id(0)
    shard, cols = q_ref.shape
    head = cols // 4

    @pl.when(h == 0)
    def _():
        vt_s[...] = v_ref[...].T
        dmi = (dm_ref[...].astype(F32) * inv_ref[...]).astype(BF)
        dmi_s[...] = dmi
        dl_s[...] = dmi.astype(F32) * o_ref[...]
        qt_s[...] = q_ref[...].T
        dmt_s[...] = dmi.T

    lane = lax.broadcasted_iota(jnp.int32, (shard, cols), 1) // head
    this = lane == h
    dmm = jnp.where(this, dmi_s[...].astype(F32), 0.0).astype(BF)
    delta = jnp.sum(jnp.where(this, dl_s[...], 0.0), -1, keepdims=True)
    step = 64
    for r in range(0, shard, step):
        dp = dot(dmm[r:r + step], vt_s[...])
        gp_ref[0, 0, r:r + step, :] = (
            e_ref[0, r:r + step, :].astype(F32) * (dp - delta[r:r + step])
        ).astype(BF)
    g = gp_ref[0, 0]
    dq = dot(g, k_ref[...]) * (1.0 / math.sqrt(head))
    dq_s[...] = jnp.where(this, dq, dq_s[...])
    at = pl.multiple_of(h * head, head)
    dkt_s[pl.ds(at, head), :] = dot(qt_s[pl.ds(at, head), :], g).astype(BF)
    dvt_s[pl.ds(at, head), :] = dot(dmt_s[pl.ds(at, head), :], e_ref[0]).astype(BF)

    @pl.when(h == 3)
    def _():
        dq_ref[...] = dq_s[...].astype(BF)
        dkv_ref[:, :cols] = dkt_s[...].T
        dkv_ref[:, cols:] = dvt_s[...].T


def table_rows(s, sums, gbin, rows, sub, half):
    pieces = [v[:, s * rows:(s + 1) * rows] for v in sums]
    for b in range(4):
        pieces.append(gbin[2 * (b & 1) + (b >> 1), :, s * sub:(s + 1) * sub])
    lines, line, p = [], [], 0
    for piece in pieces:
        line.append(piece)
        p += piece.shape[1]
        if p % half == 0:
            lines.append(jnp.concatenate(line, 1))
            line = []
    if line:
        line.append(jnp.zeros((1, half - p % half), F32))
        lines.append(jnp.concatenate(line, 1))
    lines.append(jnp.zeros((8 - len(lines), half), F32))
    value = jnp.concatenate(lines, 0)
    high = value.astype(BF)
    return jnp.concatenate([high.astype(F32), value - high.astype(F32)], 0).astype(BF)


def weight_grad_kernel(order, shards, kind, sub, scal, xt_ref, dq0, dq1, dkv0, dkv1, *rest):
    pm, mc, core = scal[0], scal[1], scal[2]
    shard, cols = dq0.shape
    length = dkv0.shape[0]
    extra, (g_keep, g_send, vg_ref) = rest[:-3], rest[-3:]
    mine = pl.multiple_of(mc * shard, shard)
    ones = jnp.ones((8, length), BF)
    grad_kv = dot(xt_ref[0], dkv0[...]) + dot(xt_ref[1], dkv1[...])
    grad_q = dot(xt_ref[0, :, pl.ds(mine, shard)], dq0[...]) + dot(xt_ref[1, :, pl.ds(mine, shard)], dq1[...])
    vg_ref[1:2, :] = (dot(ones, dkv0[:, cols:]) + dot(ones, dkv1[:, cols:]))[0:1]
    vg_ref[0:1, :] = (dot(ones[:, :shard], dq0[...]) + dot(ones[:, :shard], dq1[...]))[0:1]
    grad = jnp.concatenate([grad_q.astype(BF), grad_kv.astype(BF)], 1)
    rows = grad.shape[0] // shards
    half = grad.shape[1] // 2
    first_core = core == 0
    if kind == 2:
        vg0, vg1, ff1, ff2, gbin = extra
        sums = [
            jnp.concatenate([vg0[i:i + 1, :], vg1[i:i + 1, :], vg_ref[i:i + 1, :]], 1) for i in range(2)
        ] + [ff1[2:3, :], ff1[0:1, :], ff1[1:2, :], ff2[2:3, :], ff2[0:1, :], ff2[1:2, :]]
    for i in range(shards):
        block = grad[i * rows:(i + 1) * rows]
        to = place(i, order) ^ pm
        keep = jnp.where(first_core, block[:, :half], block[:, half:])
        send = jnp.where(first_core, block[:, half:], block[:, :half])
        if kind == 0:
            go_keep, go_send = extra
            near = (mc >> 1) == 0
            g_keep[0, to] = jnp.where(near, keep, go_keep[to])
            g_keep[1, to] = jnp.where(near, go_keep[to], keep)
            g_send[0, to] = jnp.where(near, send, go_send[to])
            g_send[1, to] = jnp.where(near, go_send[to], send)
        else:
            g_keep[to, :rows, :] = keep
            g_send[to, :rows, :] = send
        if kind == 2:
            table = table_rows(i, sums, gbin, rows, sub, half)
            g_keep[to, rows:, :] = table
            g_send[to, rows:, :] = table


def sum_kernel(rows, *refs):
    parts, out = refs[:-1], refs[-1]
    for i in range(out.shape[0]):
        total = parts[0][i].astype(F32)
        for part in parts[1:]:
            total = total + part[i].astype(F32)
        out[i, :rows] = total[:rows].astype(BF)
        value = total[rows:rows + 8] + total[rows + 8:]
        high = value.astype(BF).astype(F32)
        out[i, rows:] = jnp.concatenate([high, value - high], 0).astype(BF)


def token_kernel(
    order, shards, own,
    scal, dq00, dq01, dq10, dq11, dq20, dq21, dkv00, dkv01, dkv10, dkv11, dkv20, dkv21,
    *rest,
):
    held, rest = rest[:12], rest[12:]
    w_s = rest[-1]
    pm, mc, core = scal[0], scal[1], scal[2]
    rows = w_s.shape[1] // shards
    shard, cols = dq00.shape
    weights_in(w_s.at[0], order, pm, core, rows, shards, held[:4])
    weights_in(w_s.at[1], order, pm, core, rows, shards, held[4:8])
    weights_in(w_s.at[2], order, pm, core, rows, shards, held[8:])
    dqs = ((dq00, dq10, dq20), (dq01, dq11, dq21))
    dkvs = ((dkv00, dkv10, dkv20), (dkv01, dkv11, dkv21))
    outs = [(0, rest[1])] if own else [(1, rest[0].at[0]), (3, rest[0].at[1]), (2, rest[1])]
    for j, out in outs:
        where = pl.multiple_of((mc ^ j) * shard, shard)
        for s in range(2):
            total = rest[0][s * shard:(s + 1) * shard, :] if own else None
            for g in range(3):
                part = dot_nt(dkvs[s][g][pl.ds(where, shard), :], w_s[g, :, cols:])
                if own:
                    part = part + dot_nt(dqs[s][g][...], w_s[g, :, :cols])
                total = part if total is None else total + part
            out[s] = total.astype(out.dtype)


def finish_kernel(rows, sub, shards, scal, f, fy, fc, fyc, e, ey, ec, eyc, wq, wk, wv, wo, wi, wd, tab):
    low = scal[2] == 0
    near = (scal[1] >> 1) == 0
    half = e.shape[1]
    cols = wq.shape[1] // 3
    cut = half - cols
    zero_at, one_at = rows + 16, 2 * rows + 16

    def both(mine, other):
        mine, other = mine.astype(F32), other.astype(F32)
        return jnp.where(low, mine, other), jnp.where(low, other, mine)

    def four(a, b, c, d):
        return both(jnp.where(near, a, b), jnp.where(near, c, d)), both(jnp.where(near, b, a), jnp.where(near, d, c))

    def added(at):
        parts = [ref[at:at + rows].astype(F32) for ref in (e, ey, ec, eyc)]
        return both(parts[0] + parts[1], parts[2] + parts[3])

    zero, outer = four(*[ref[zero_at:zero_at + rows] for ref in (e, ey, ec, eyc)])
    groups = [zero, added(one_at), added(0)]
    for g, (first, second) in enumerate(groups):
        at = g * cols
        wq[:, at:at + cols] = first[:, :cols]
        wk[:, at:at + cut] = first[:, cols:]
        wk[:, at + cut:at + cols] = second[:, :cols - cut]
        wv[:, at:at + cols] = second[:, cols - cut:]
    wo[:, :half] = outer[0]
    wo[:, half:] = outer[1]
    tab[...] = sum(ref[at:at + 8, :].astype(F32) for ref in (e, ey) for at in (rows, rows + 8))
    (i00, i10), (i01, i11) = four(f[0], fy[0], fc[0], fyc[0])
    (d00, d10), (d01, d11) = four(f[1], fy[1], fc[1], fyc[1])
    for b, (i_part, d_part) in enumerate(((i00, d00), (i01, d01), (i10, d10), (i11, d11))):
        wd[b * sub:(b + 1) * sub, :] = d_part
        for s in range(shards):
            at = (4 * s + b) * sub
            wi[:, at:at + sub] = i_part[:, s * sub:(s + 1) * sub]


def on_device(
    n, far, near,
    tokens, prior_logits, doc_ids, w_query, w_key, w_value, w_out, b_query, b_value, b_out,
    first_norm_gain, norm1_shift, w_in, b_in, w_down, b_down, norm2_gain, norm2_shift, cotangent,
):
    seqs, shard, width = tokens.shape
    heads, length = prior_logits.shape[1], prior_logits.shape[3]
    ctx = length // shard
    rows = w_query.shape[0]
    sub = w_down.shape[0] // 4
    cols = width // GROUPS
    per = heads // GROUPS
    half = (3 * cols) // 2
    n_rows = seqs * shard
    m = n // 2
    order = far + near
    me_s = lax.axis_index("seq")
    me_c = lax.axis_index("ctx")
    core = me_c & 1
    pm = place(me_s, order)
    scal = jnp.stack([pm, me_c, core]).astype(jnp.int32)
    sds = jax.ShapeDtypeStruct
    hbm = pl.BlockSpec(memory_space=pltpu.HBM)

    def kernel(body, outs, ins, args, scratch=(), grid=None, alias=None, flops=0, moved=0, exps=0, name=None, limit=24):
        return pl.pallas_call(
            body,
            out_shape=outs,
            in_specs=ins[0],
            out_specs=ins[1],
            scratch_shapes=scratch,
            input_output_aliases=alias or {},
            compiler_params=params(len(grid) if grid else 0, limit),
            cost_estimate=pl.CostEstimate(flops=flops, bytes_accessed=moved, transcendentals=exps),
            name=name,
            **({"grid": grid} if grid else {}),
        )(*args)

    def by_core(value):
        return swap(value, "ctx", ctx, 0)

    def by_y(value):
        return swap(value, "ctx", ctx, 1)

    def by_x(value):
        return swap(value, "seq", n, near[-1])

    def whole(*shape):
        return pl.BlockSpec(shape, lambda *i: (0,) * len(shape))

    vectors = [b_query, b_value, b_out, first_norm_gain, norm1_shift, b_down, norm2_gain, norm2_shift, b_in]
    a0, tok0 = kernel(
        prep_first_kernel, [sds((rows + 16, half), BF), sds((seqs, shard + 16, width), BF)],
        ([smem(), whole(seqs, shard, width), whole(seqs, shard)] + [pl.BlockSpec((rows, cols), lambda i: (0, 0))] * 3
         + [whole(1, v.shape[0]) for v in vectors], [whole(rows + 16, half), whole(seqs, shard + 16, width)]),
        (scal, tokens, doc_ids, w_query, w_key, w_value, *[v.reshape(1, -1) for v in vectors]),
        grid=(1,), moved=10**6, name="prep_first", limit=60,
    )

    def exchange(held):
        return [held] + [swap_by(held, "seq", n, step) for step in far_steps(far)]

    def join(parts, name):
        lead = parts[0].ndim == 3
        shape = (2, 4, *parts[0].shape[1:]) if lead else (4, *parts[0].shape)
        out, = kernel(join_kernel, [sds(shape, BF)], ([vmem()] * 4, [vmem()]), parts, moved=10**6, name=name)
        for bit in near[:-1]:
            out = jnp.concatenate([out, swap(out, "seq", n, bit)], 1 if lead else 0)
        return out

    a_parts = exchange(a0)
    a1, ffq = kernel(
        prep_kernel,
        [sds((rows, 3 * half), BF), sds((2, rows, width), BF)],
        ([smem()] + [vmem()] * 6, [vmem()] * 2),
        (after(scal, a0), w_query, w_key, w_value, w_out, w_in, w_down),
        moved=6 * 10**6, name="prep", limit=60,
    )
    a_lo = join([after(x, a1) for x in a_parts], "join_a")
    tok2 = by_y(tok0)
    a_hi = by_x(a_lo)
    b_parts = exchange(after(a1, a_lo))
    tok1 = by_core(after(tok0, a_hi))
    ag_lo = by_core(after(a_lo, a_hi))
    ag_hi = by_core(a_hi)
    tok3 = by_core(after(tok2, a_hi))
    tok = (tok0, tok1, tok2, tok3)

    def doubled(a, b, name):
        a, b = a.reshape(2, -1, *a.shape[-2:]), b.reshape(2, -1, *b.shape[-2:])
        shape = (2, 2 * a.shape[1], *a.shape[2:])
        out, = kernel(join_pair_kernel, [sds(shape, BF)], ([vmem()] * 2, [vmem()]), (a, b), moved=10**6, name=name)
        return out

    vecs, bin_all = kernel(
        functools.partial(vector_kernel, order, n, rows, sub),
        [sds((8, width), F32), sds((4, 1, width), F32)],
        ([smem()] + [vmem()] * 2, [vmem()] * 2), (after(scal, ag_lo, tok1, ag_hi, tok3), a_lo, a_hi), moved=10**6, name="vectors",
    )

    raw = None
    kept = []

    def attend(g, s, scal, arrays):
        nonlocal raw
        big = pl.BlockSpec((1, 1, shard, length), lambda h: (s, g * per + h, 0, 0))
        tok_spec = pl.BlockSpec((1, shard + 16, width), lambda h: (s, 0, 0))
        block = 0
        w_spec = pl.BlockSpec((m, arrays[0].shape[1], half), lambda h: (0, 0, block))
        args = [scal, *tok, doc_ids, vecs, prior_logits, *arrays]
        specs = [smem()] + [tok_spec] * 4 + [vmem(), pl.BlockSpec((8, cols), lambda h: (0, g)), big] + [w_spec] * len(arrays)
        alias = {}
        if raw is not None:
            alias = {len(args): 0}
            args.append(raw)
            specs.append(hbm)
        raw, *rest = kernel(
            functools.partial(attend_kernel, order, n, s, g, raw is not None),
            [sds(prior_logits.shape, BF), pltpu.HBM((per, shard, length), BF), pltpu.HBM((shard, cols), BF),
             pltpu.HBM((length, cols), BF), pltpu.HBM((length, cols), BF), pltpu.HBM((shard, cols), F32), pltpu.HBM((shard, cols), F32)],
            (specs, [big, pl.BlockSpec((1, shard, length), lambda h: (h, 0, 0)), whole(shard, cols), whole(length, cols),
                     whole(length, cols), whole(shard, cols), whole(shard, cols)]),
            args, [VM((width, 3 * cols), BF), VM((cols, length), BF), VM((shard, length), F32), VM((2, length, cols), BF)],
            grid=(per,), alias=alias, flops=5 * 10**9, moved=10 * 10**6, exps=10**6, name=f"attend{g}{s}", limit=48,
        )
        kept.append(rest)
        return rest[2]

    a_set = (a_lo, a_hi, ag_lo, ag_hi)
    attend(0, 0, after(scal, vecs), a_set)
    mark = kept[-1][4]
    def nearer(held, axis):
        for bit in near[:-1]:
            held = jnp.concatenate([held, swap(held, "seq", n, bit)], axis)
        return held

    b_lo, c_lo = kernel(join_split_kernel, [sds((4, rows, half), BF), sds((4, rows, 2 * half), BF)], ([vmem()] * 4, [vmem()] * 2),
                        [after(x, mark) for x in b_parts], moved=10**6, name="join_bc")
    b_lo, c_lo = nearer(b_lo, 0), nearer(c_lo, 0)
    b_hi = by_x(b_lo)
    f_half = swap_by(after(ffq, b_lo), "seq", n, 1 << far[0])
    c_hi = by_x(c_lo)
    attend(0, 1, after(scal, b_lo), a_set)
    mark = kept[-1][4]
    f_two = doubled(after(ffq, mark), f_half, "join_f")
    b_hi = after(b_hi, f_two)
    bg_lo, bg_hi = by_core(after(b_lo, b_hi)), by_core(b_hi)
    f_far = swap_by(after(f_two, b_hi), "seq", n, 1 << far[1])
    b_set = (b_lo, b_hi, bg_lo, bg_hi)
    attend(1, 0, scal, b_set)
    mark = kept[-1][4]
    f_lo = nearer(doubled(after(f_two, mark), f_far, "join_ff"), 1)
    c_hi = after(c_hi, f_lo)
    cg_lo, cg_hi = by_core(after(c_lo, c_hi)), by_core(c_hi)
    f_lo = after(f_lo, cg_lo, cg_hi)
    f_ylo, f_hi = by_y(f_lo), by_x(f_lo)
    c_set = (c_lo, c_hi, cg_lo, cg_hi)
    attend(1, 1, after(scal, f_lo, cg_lo, cg_hi), b_set)
    x_t, = kernel(turn_kernel, [pltpu.HBM((seqs, width, length), BF)], ([smem()] + [vmem()] * 4, [vmem()]),
                  (after(scal, kept[-1][4]), *tok), moved=12 * 10**6, name="turn")
    attend(2, 0, after(scal, x_t), c_set)
    mark = kept[-1][4]
    f_hi, f_ylo = after(f_hi, mark, f_ylo), after(f_ylo, mark, f_hi)
    f_yhi_i, f_yhi_d = by_y(f_hi[0]), by_x(f_ylo[1])
    fc_hi, fc_ylo = by_core(f_hi), by_core(f_ylo)
    fc_lo = by_core(after(f_lo, f_hi, f_ylo))
    attend(2, 1, after(scal, f_hi, f_ylo), c_set)
    mark = kept[-1][4]
    f_yhi_i, f_yhi_d = after(f_yhi_i, mark, fc_lo, fc_hi, fc_ylo), after(f_yhi_d, mark, fc_lo, fc_hi, fc_ylo)
    fc_yhi_i, fc_yhi_d = by_core(f_yhi_i), by_core(f_yhi_d)
    f = (f_lo, f_hi, f_ylo, f_yhi_i, f_yhi_d, fc_lo, fc_hi, fc_ylo, fc_yhi_i, fc_yhi_d)

    o_spec = pl.BlockSpec((m, rows, half), lambda i: (0, 0, 1))
    w_scratch = VM((4, n, rows, width), BF)
    w_one = VM((width, width), BF)
    sems = pltpu.SemaphoreType.DMA((8,))
    output, mixed, first_n, inv1, inner, hid, dg, dsum2, dsec, ff2 = kernel(
        functools.partial(forward_kernel, order, n),
        [
            sds((seqs, shard, width), BF), sds((n_rows, width), BF), sds((n_rows, width), F32), sds((n_rows, 1), F32),
            sds((n_rows, width), BF), sds((4, n_rows, width), BF), sds((4, n_rows, width), BF),
            sds((n_rows, width), F32), sds((n_rows, width), BF), sds((8, width), F32),
        ],
        ([smem()] + [vmem()] * 10 + [o_spec] * 4 + [pl.BlockSpec(memory_space=ANY)] * 10, [vmem()] * 10),
        (scal, *[k[4] for k in kept], tokens, cotangent, vecs, bin_all, *c_set, *f),
        [VM((width, width), BF), w_scratch, w_scratch, w_one, VM((n_rows, width), F32), VM((n_rows, width), F32), sems, sems],
        grid=(1,), flops=6 * 10**9, moved=25 * 10**6, exps=2 * 10**6, name="ff_fwd", limit=48,
    )
    def quarter(i):
        return (jnp.where(i < 2, 2 * i + 1, 2 * i - 4), 0, 0)

    pair = [sds((2, n, rows, width), BF)] * 2
    d_keep, d_send = kernel(
        functools.partial(down_grad_kernel, order, n), pair,
        ([smem()] + [vmem()] * 2, [vmem()] * 2), (scal, hid, dsec), flops=3 * 10**9, moved=8 * 10**6, name="down_grad", limit=24,
    )
    d_got = by_core(d_send)
    dx_send = add(d_keep[:, m:], d_got[:, m:])
    i_keep, i_send, dpre, gbin = kernel(
        functools.partial(in_grad_kernel, order, n),
        pair + [sds((4, n_rows, width), BF), sds((4, 1, width), F32)],
        ([smem(), whole(n_rows, width), pl.BlockSpec((1, n_rows, width), quarter), whole(n_rows, width)] + [pl.BlockSpec(memory_space=ANY)] * 10,
         [pl.BlockSpec((1, n, rows, width), lambda i: (jnp.maximum(i - 2, 0), 0, 0, 0)),
          pl.BlockSpec((1, n, rows, width), lambda i: (jnp.minimum(i, 1), 0, 0, 0)),
          pl.BlockSpec((1, n_rows, width), quarter), whole(4, 1, width)]),
        (after(scal, d_keep), inner, dg, dsec, *f), [w_scratch, w_one, sems], grid=(4,), flops=6 * 10**9, moved=20 * 10**6, name="in_grad", limit=40,
    )
    i_got = by_core(i_send)
    go_keep, go_send, dsum1, dmix, ff1 = kernel(
        functools.partial(first_grad_kernel, order, n),
        [sds((n, rows, half), BF)] * 2 + [sds((n_rows, width), F32), sds((n_rows, width), BF), sds((8, width), F32)],
        ([smem()] + [vmem()] * 6 + [o_spec] * 4 + [pl.BlockSpec(memory_space=ANY)] * 10, [vmem()] * 5),
        (after(scal, dx_send), mixed, first_n, inv1, dpre, dsum2, vecs, *c_set, *f), [VM((width, width), BF), w_scratch, w_one, sems],
        grid=(1,), flops=4 * 10**9, moved=15 * 10**6, name="first_grad", limit=40,
    )

    gp = None
    dqs, dkvs, vgs = [], [], []

    def back(g, s, scal):
        nonlocal gp
        e, q, k, v, o, inv = kept[g * seqs + s]
        big = pl.BlockSpec((1, 1, shard, length), lambda h: (s, g * per + h, 0, 0))
        args = [scal, e, dmix, q, k, v, o, inv]
        specs = [smem(), pl.BlockSpec((1, shard, length), lambda h: (h, 0, 0)),
                 pl.BlockSpec((shard, cols), lambda h: (s, g)),
                 whole(shard, cols), whole(length, cols), whole(length, cols), whole(shard, cols), whole(shard, cols)]
        alias = {}
        if gp is not None:
            alias = {len(args): 0}
            args.append(gp)
            specs.append(hbm)
        gp, dq, dkv = kernel(
            functools.partial(attend_back_kernel, gp is not None),
            [sds(prior_logits.shape, BF), sds((shard, cols), BF), sds((length, 2 * cols), BF)],
            (specs, [big, whole(shard, cols), whole(length, 2 * cols)]),
            args,
            [VM((cols, length), BF), VM((cols, shard), BF), VM((cols, shard), BF), VM((shard, cols), BF),
             VM((shard, cols), F32), VM((cols, length), BF), VM((cols, length), BF), VM((shard, cols), F32)],
            grid=(per,), alias=alias, flops=5 * 10**9, moved=10 * 10**6, name=f"back{g}{s}", limit=24,
        )
        dqs.append(dq)
        dkvs.append(dkv)
        return dq

    def weight_grad(g, scal):
        extra = ([go_keep, go_send], [], vgs + [ff1, ff2, gbin])[g]
        shape = ((2, n, rows, half), (n, rows, half), (n, rows + 16, half))[g]
        keep, send, vg = kernel(
            functools.partial(weight_grad_kernel, order, n, g, sub),
            [sds(shape, BF)] * 2 + [sds((8, cols), F32)],
            ([smem()] + [vmem()] * (5 + len(extra)), [vmem()] * 3),
            (scal, x_t, *dqs[-2:], *dkvs[-2:], *extra),
            flops=2 * 10**9, moved=8 * 10**6, name=f"weight_grad{g}", limit=24,
        )
        vgs.append(vg)
        return keep, send, vg

    def rest_near(held, axis, plus):
        for bit in reversed(near[:-1]):
            k = held.shape[axis] // 2
            keep = lax.slice_in_dim(held, 0, k, axis=axis)
            held = plus(keep, swap(lax.slice_in_dim(held, k, 2 * k, axis=axis), "seq", n, bit))
        return held

    def far_sum(blocks, plus):
        got = [swap_by(b, "seq", n, step) for b, step in zip(blocks[1:], far_steps(far))]
        return plus(blocks[0], *got)

    def plus_table(*parts):
        flat = parts[0].ndim == 2
        parts = [p[None] if flat else p for p in parts]
        out, = kernel(functools.partial(sum_kernel, rows), [sds(parts[0].shape, BF)],
                      ([vmem()] * len(parts), [vmem()]), parts, moved=10**6, name="sum_table")
        return out[0] if flat else out

    dx_got = by_x(dx_send)
    iy_send = add(i_keep[1], i_got[1])
    iy_got = by_y(iy_send)
    back(0, 0, after(scal, iy_send))
    mark = back(0, 1, scal)
    dx_got = after(dx_got, mark)
    dy_send = add(d_keep[1, :m], d_got[1, :m], dx_got[1])
    dy_got = by_y(dy_send)
    g0_keep, g0_send, _ = weight_grad(0, after(scal, dy_send))
    g0_got = by_core(g0_send)
    mark = back(1, 0, after(scal, g0_keep))
    iy_got = after(iy_got, mark)
    ix_send = add(i_keep[0, m:], i_got[0, m:], iy_got[m:])
    ix_got = by_x(ix_send)
    g0y_send = add(after(g0_keep, mark)[1], g0_got[1])
    g0y_got = by_y(g0y_send)
    back(1, 1, after(scal, ix_send, g0y_send))
    g1_keep, g1_send, mark = weight_grad(1, scal)
    g1_got = by_core(g1_send)
    dl = add(after(d_keep, mark)[0, :m], d_got[0, :m], dx_got[0], dy_got)
    il = add(after(i_keep, mark)[0, :m], i_got[0, :m], iy_got[:m], ix_got)
    lo = rest_near(jnp.stack([il, dl], 1), 0, add)
    ff_far = swap_by(lo[2:], "seq", n, 1 << far[1])
    g0y_got = after(g0y_got, mark)
    g0x_send = add(g0_keep[0, m:], g0_got[0, m:], g0y_got[m:])
    g0x_got = by_x(g0x_send)
    mark = back(2, 0, after(scal, lo, g0x_send))
    g1x_send = add(after(g1_keep, mark)[m:], g1_got[m:])
    g1x_got = by_x(g1x_send)
    g0 = rest_near(add(after(g0_keep, mark)[0, :m], g0_got[0, :m], g0y_got[:m], g0x_got), 0, add)
    ff_two = add(after(lo, mark)[:2], ff_far)
    ff_got = swap_by(ff_two[1], "seq", n, 1 << far[0])
    mark = back(2, 1, after(scal, g0, g1x_send, ff_two))
    ff = add(after(ff_two, mark)[0], ff_got)
    g1 = rest_near(add(after(g1_keep, mark)[:m], g1_got[:m], g1x_got), 0, add)
    pair, pair_send = kernel(pair_kernel, [sds((2, rows, 2 * half), BF)] * 2, ([vmem()] * 2, [vmem()] * 2), (after(g0, ff), g1),
                             moved=10**6, name="pair")
    pair_got = swap_by(pair_send, "seq", n, 1 << far[1])
    ff_y = by_y(after(ff, pair))
    g2_keep, g2_send, mark = weight_grad(2, after(scal, pair))
    pair = add(after(pair, mark), pair_got)
    g2_got = by_core(after(g2_send, pair))
    pair_got = swap_by(pair[1], "seq", n, 1 << far[0])
    g2x_send = plus_table(g2_keep[m:], g2_got[m:])
    g2x_got = by_x(g2x_send)
    all_sets = (*a_set, *b_set, *c_set)
    set_specs = [whole(m, a.shape[1], half) for a in a_set + b_set] + [whole(m, rows, half)] * 4
    w_all = VM((GROUPS, width, 3 * cols), BF)
    far_a, far_b = kernel(
        functools.partial(token_kernel, order, n, False),
        [sds((2, seqs, shard, width), BF), sds((seqs, shard, width), BF)],
        ([smem()] + [vmem()] * 12 + set_specs, [vmem()] * 2),
        (after(scal, mark, g2x_send, pair), *dqs, *dkvs, *all_sets),
        [w_all], grid=(1,), flops=6 * 10**9, moved=15 * 10**6, name="token_far", limit=30,
    )
    pair = add(after(pair, far_b)[0], pair_got)
    g2 = rest_near(plus_table(g2_keep[:m], g2_got[:m], after(g2x_got, far_b)), 0, plus_table)
    far_got = by_core(after(far_a, g2, pair))
    g2_far = [swap_by(after(g2, pair)[i + 1], "seq", n, step) for i, step in enumerate(far_steps(far))]
    across_send = add(far_b, far_got[1])
    across = by_y(across_send)
    own_part, = kernel(
        functools.partial(token_kernel, order, n, True),
        [sds((seqs, shard, width), F32)],
        ([smem()] + [vmem()] * 12 + set_specs + [vmem()], [vmem()]),
        (after(scal, across_send, g2, pair), *dqs, *dkvs, *all_sets, dsum1),
        [w_all], grid=(1,), flops=4 * 10**9, moved=15 * 10**6, name="token_own", limit=30,
    )
    ends, = kernel(functools.partial(ends_kernel, rows), [sds((3 * rows + 16, half), BF)], ([vmem()] * 5, [vmem()]),
                   (after(g2, own_part)[0], *g2_far, pair), moved=10**6, name="ends")
    grad_tokens = own_part + far_got[0].astype(F32) + across.astype(F32)
    ends = after(ends, grad_tokens)
    ends_y = by_y(ends)
    ends_c = by_core(ends)
    ff_c, ff_yc = by_core(after(ff, ends)), by_core(after(ff_y, ends))
    g_wq, g_wk, g_wv, g_wo, g_wi, g_wd, table = kernel(
        functools.partial(finish_kernel, rows, sub, n),
        [sds(w.shape, F32) for w in (w_query, w_key, w_value, w_out, w_in, w_down)] + [sds((8, half), F32)],
        ([smem()] + [vmem()] * 8, [vmem()] * 7),
        (scal, ff, ff_y, ff_c, ff_yc, ends, ends_y, ends_c, by_core(ends_y)),
        moved=4 * 10**6, name="finish",
    )
    table = table.reshape(-1)
    cut = [table[i * rows:(i + 1) * rows] for i in range(8)]
    g_bq, g_bv, g_bo, g_g1, g_s1, g_bd, g_g2, g_s2 = cut
    g_bin = table[8 * rows:8 * rows + 4 * sub]
    return (
        output, raw, grad_tokens, gp, g_wq, g_wk, g_wv, g_wo,
        g_bq, g_bv, g_bo, g_g1, g_s1, g_wi, g_bin, g_wd, g_bd, g_g2, g_s2,
    )


def solution(mesh):
    n = mesh.shape["seq"]
    top = n.bit_length() - 1
    far, near = (top - 1, top - 2), tuple(reversed(range(top - 2)))
    in_specs = (
        P("seq", "ctx", None), P("seq", None, "ctx", None), P("seq", "ctx"),
        P("seq", None), P("seq", None), P("seq", None), P("seq", None),
        P("seq"), P("seq"), P("seq"), P("seq"), P("seq"),
        P("seq", None), P("seq"), P("seq", None), P("seq"), P("seq"), P("seq"),
        P("seq", "ctx", None),
    )
    out_specs = (
        P("seq", "ctx", None), P("seq", None, "ctx", None), P("seq", "ctx", None), P("seq", None, "ctx", None),
        P("seq", None), P("seq", None), P("seq", None), P("seq", None),
        P("seq"), P("seq"), P("seq"), P("seq"), P("seq"),
        P("seq", None), P("seq"), P("seq", None), P("seq"), P("seq"), P("seq"),
    )
    return jax.shard_map(
        functools.partial(on_device, n, far, near),
        mesh=mesh, in_specs=in_specs, out_specs=out_specs, check_vma=False,
    )
```

```python
import functools
import math

import jax
import jax.numpy as jnp
from jax import lax
from jax.experimental import pallas as pl
from jax.experimental.pallas import tpu as pltpu
from jax.sharding import PartitionSpec as P

EPSILON = 1e-05
NEGATIVE = -1e30
BF = jnp.bfloat16
F32 = jnp.float32
VM = pltpu.VMEM
ANY = pl.ANY
GROUPS = 3


def dot(a, b):
    return lax.dot_general(a, b, (((1,), (0,)), ((), ())), preferred_element_type=F32)


def dot_nt(a, b):
    return lax.dot_general(a, b, (((1,), (1,)), ((), ())), preferred_element_type=F32)


def dot_tn(a, b):
    return lax.dot_general(a, b, (((0,), (0,)), ((), ())), preferred_element_type=F32)


def vmem(shape=None, index=None):
    if shape is None:
        return pl.BlockSpec(memory_space=VM)
    return pl.BlockSpec(shape, index)


def params(n_grid, limit):
    return pltpu.CompilerParams(
        vmem_limit_bytes=limit * 1024 * 1024,
        dimension_semantics=("arbitrary",) * n_grid if n_grid else None,
    )


def smem():
    return pl.BlockSpec(memory_space=pltpu.SMEM)


def after(value, *marks):
    return lax.optimization_barrier((value, *marks))[0]


def swap_by(value, axis, size, step):
    return lax.ppermute(value, axis, [(i, i ^ step) for i in range(size)])


def swap(value, axis, size, bit):
    return swap_by(value, axis, size, 1 << bit)


def far_steps(far):
    a, b = 1 << far[0], 1 << far[1]
    return (a, b, a | b)


def add(*parts):
    total = parts[0].astype(F32)
    for part in parts[1:]:
        total = total + part.astype(F32)
    return total.astype(BF)


def place(index, order):
    out = 0
    for step, bit in enumerate(order):
        out = out | (((index >> bit) & 1) << step)
    return out


def column_half(wq, wk, wv, g, half, low):
    cols = (2 * half) // 3
    cut = half - cols
    at = g * cols
    first = jnp.concatenate([wq[:, at:at + cols], wk[:, at:at + cut]], 1)
    second = jnp.concatenate([wk[:, at + cut:at + cols], wv[:, at:at + cols]], 1)
    return jnp.where(low, first, second)


def prep_kernel(scal, tok, docs, wq, wk, wv, wo, *rest):
    vecs, (a0, tok_ref) = rest[:9], rest[9:]
    seqs, shard = tok.shape[:2]
    rows = wq.shape[0]
    half = a0.shape[1] // 4
    low = scal[2] == 0
    for s in range(seqs):
        tok_ref[s, :shard, :] = tok[s]
        tok_ref[s, shard:, :] = jnp.zeros_like(tok_ref[s, shard:, :])
        tok_ref[s, shard:shard + 1, :shard] = docs[s:s + 1, :].astype(F32).astype(BF)
    for g in range(3):
        a0[:rows, g * half:(g + 1) * half] = column_half(wq, wk, wv, g, half, low)
    a0[:rows, 3 * half:] = jnp.where(low, wo[:, :half], wo[:, half:])
    p = 0
    lines = []
    line = []
    for v in vecs:
        step = rows if v.shape[1] == rows else v.shape[1] // 4
        for i in range(v.shape[1] // step):
            line.append(v[:, i * step:(i + 1) * step].astype(F32))
            p += step
            if p % half == 0:
                lines.append(jnp.concatenate(line, 1))
                line = []
    if line:
        line.append(jnp.zeros((1, half - p % half), F32))
        lines.append(jnp.concatenate(line, 1))
    lines.append(jnp.zeros((16 - len(lines), half), F32))
    a0[rows:, :half] = jnp.concatenate(lines, 0).astype(BF)
    a0[rows:, half:] = jnp.zeros_like(a0[rows:, half:])


def prep_ff_kernel(scal, wi, wd, ffq):
    mc, core = scal[1], scal[2]
    my_y = mc >> 1
    low = core == 0
    sub = ffq.shape[1]
    width = ffq.shape[2]
    block = 2 * core + my_y
    ffq[1] = wd[pl.ds(pl.multiple_of(block * sub, sub), sub), :]
    for s in range(width // sub):
        got = [wi[:, (4 * s + b) * sub:(4 * s + b + 1) * sub] for b in range(4)]
        near = jnp.where(my_y == 0, got[0], got[1])
        far = jnp.where(my_y == 0, got[2], got[3])
        ffq[0, :, s * sub:(s + 1) * sub] = jnp.where(low, near, far)


def join_kernel(a, b, c, d, out):
    lead = out.ndim == 4
    for i, ref in enumerate((a, b, c, d)):
        if lead:
            out[:, i] = ref[...]
        else:
            out[i] = ref[...]


def fetch(lo, hi, at):
    m = lo.shape[0]
    return jnp.where(at < m, lo[at & (m - 1)], hi[at & (m - 1)])


def join_split_kernel(a, b, c, d, first, second, third):
    half = first.shape[2]
    rows = second.shape[1]
    for i, ref in enumerate((a, b, c, d)):
        first[i] = ref[:, :half]
        second[i] = ref[:rows, half:2 * half]
        third[i] = ref[:rows, 2 * half:]


def join_pair_kernel(a, b, out):
    k = a.shape[1]
    out[:, :k] = a[...]
    out[:, k:] = b[...]


def pair_kernel(a, b, near, far):
    half = a.shape[2]
    for i in range(4):
        out = near if i < 2 else far
        out[i % 2, :, :half] = a[i]
        out[i % 2, :, half:] = b[i]


def ends_kernel(rows, p0, p1, p2, p3, pair, out):
    total = p0[...].astype(F32) + p1[...].astype(F32) + p2[...].astype(F32) + p3[...].astype(F32)
    out[:rows] = total[:rows].astype(BF)
    value = total[rows:rows + 8] + total[rows + 8:]
    high = value.astype(BF).astype(F32)
    out[rows:rows + 16] = jnp.concatenate([high, value - high], 0).astype(BF)
    half = out.shape[1]
    out[rows + 16:2 * rows + 16] = pair[:, :half]
    out[2 * rows + 16:] = pair[:, half:]


def weights_in(out, order, pm, core, rows, shards, held):
    first = core == 0
    m = held[0].shape[0]
    half = held[0].shape[2]
    for i in range(shards):
        at = place(i, order) ^ pm
        spot = at & (m - 1)
        in_lo = at < m
        four = [ref[spot, :rows, :] for ref in held]
        mine = jnp.where(in_lo, four[0], four[1])
        other = jnp.where(in_lo, four[2], four[3])
        out[i * rows:(i + 1) * rows, :half] = jnp.where(first, mine, other)
        out[i * rows:(i + 1) * rows, half:2 * half] = jnp.where(first, other, mine)


def vector_kernel(order, shards, rows, sub, scal, lo, hi, vec_ref, bin_ref):
    pm = scal[0]
    half = lo.shape[2]
    m = lo.shape[0]
    for s in range(shards):
        at = place(s, order) ^ pm
        block = jnp.where(at < m, lo[at & (m - 1), rows:, :], hi[at & (m - 1), rows:, :]).astype(F32)
        for i in range(8):
            p = i * rows
            vec_ref[i:i + 1, s * rows:(s + 1) * rows] = block[p // half:p // half + 1, p % half:p % half + rows]
        for b in range(4):
            p = 8 * rows + b * sub
            c = 2 * (b & 1) + (b >> 1)
            bin_ref[c, :, s * sub:(s + 1) * sub] = block[p // half:p // half + 1, p % half:p % half + sub]


def turn_kernel(scal, t0, t1, t2, t3, out_ref):
    mc = scal[1]
    seqs, _, width = t0.shape
    shard = out_ref.shape[2] // 4
    for j, tok in enumerate((t0, t1, t2, t3)):
        where = pl.multiple_of((mc ^ j) * shard, shard)
        for s in range(seqs):
            out_ref[s, :, pl.ds(where, shard)] = tok[s, :shard, :].T


def attend_kernel(
    order, shards, seq, group, aliased,
    scal, t0, t1, t2, t3, doc_ref, bias_ref, prior_ref, *rest,
):
    held, rest = rest[:4], rest[4:]
    if aliased:
        rest = rest[1:]
    raw_ref, e_ref, q_ref, k_ref, v_ref, o_ref, inv_ref, w_s, kt_s, mask_s, vx_s = rest
    h = pl.program_id(0)
    pm, mc, core = scal[0], scal[1], scal[2]
    rows = w_s.shape[0] // shards
    shard, cols = q_ref.shape
    head = cols // 4

    @pl.when(h == 0)
    def _():
        weights_in(w_s, order, pm, core, rows, shards, held)
        q = dot(t0[0, :shard, :], w_s[:, :cols]) + bias_ref[0:1, :]
        q_ref[...] = (q.astype(BF).astype(F32) * (1.0 / math.sqrt(head))).astype(BF)
        mine = jnp.broadcast_to(doc_ref[seq:seq + 1, :].astype(F32), (128, shard)).T[:, :1]
        for j, tok in enumerate((t0, t1, t2, t3)):
            where = pl.multiple_of((mc ^ j) * shard, shard)
            kv = dot(tok[0, :shard, :], w_s[:, cols:])
            k_ref[pl.ds(where, shard), :] = kv[:, :cols].astype(BF)
            v = kv[:, cols:] + bias_ref[1:2, :]
            v_ref[pl.ds(where, shard), :] = v.astype(BF)
            even = (lax.broadcasted_iota(jnp.int32, (shard, cols), 1) // head) % 2 == 0
            vx_s[0, pl.ds(where, shard), :] = jnp.where(even, v, 1.0).astype(BF)
            vx_s[1, pl.ds(where, shard), :] = jnp.where(even, 1.0, v).astype(BF)
            docs = tok[0, shard:shard + 1, :shard].astype(F32)
            mask_s[:, pl.ds(where, shard)] = jnp.where(mine == docs, 0.0, NEGATIVE)
        kt_s[...] = k_ref[...].T

    lane = lax.broadcasted_iota(jnp.int32, (shard, cols), 1) // head
    this = lane == h
    qm = jnp.where(this, q_ref[...].astype(F32), 0.0).astype(BF)
    step = 64
    for r in range(0, shard, step):
        logits = dot(qm[r:r + step], kt_s[...]) + prior_ref[0, 0, r:r + step, :].astype(F32)
        raw_ref[0, 0, r:r + step, :] = logits.astype(BF)
        masked = logits + mask_s[r:r + step, :]
        top = jnp.max(masked, -1, keepdims=True)
        e_ref[0, r:r + step, :] = jnp.exp(masked - top).astype(BF)
    o = dot(e_ref[0], vx_s[h & 1])
    total = jnp.max(jnp.where(lane == (h ^ 1), o, 0.0), -1, keepdims=True)
    inv = 1.0 / total
    o_ref[...] = jnp.where(this, o * inv, o_ref[...])
    inv_ref[...] = jnp.where(this, inv, inv_ref[...])


def gelu_parts(x):
    z = jnp.abs(x) * 0.7071067811865476
    t = 1.0 / (1.0 + 0.3275911 * z)
    e = jnp.exp(-0.5 * x * x)
    poly = t * (0.254829592 + t * (-0.284496736 + t * (1.421413741 + t * (-1.453152027 + t * 1.061405429))))
    tail = 0.5 * poly * e
    phi = jnp.where(x >= 0, 1.0 - tail, tail)
    return x * phi, phi + x * (e * 0.3989422804014327)


def moments(x):
    mean = jnp.mean(x, -1, keepdims=True)
    centered = x - mean
    inverse = lax.rsqrt(jnp.mean(centered * centered, -1, keepdims=True) + EPSILON)
    return centered * inverse, inverse


def norm_back(grad, normed, inverse, gain):
    scaled = grad * gain
    return inverse * (
        scaled - jnp.mean(scaled, -1, keepdims=True)
        - normed * jnp.mean(scaled * normed, -1, keepdims=True)
    )


def ff_sources(f, which):
    lo, hi, ylo, yhi_i, yhi_d, clo, chi, cylo, cyhi_i, cyhi_d = f
    yhi, cyhi = (yhi_i, cyhi_i) if which == 0 else (yhi_d, cyhi_d)
    return [(lo.at[which], hi.at[which]), (clo.at[which], chi.at[which]),
            (ylo.at[which], yhi), (cylo.at[which], cyhi)]


def ff_copies(f, which, held, sem):
    out = []
    for j, halves in enumerate(ff_sources(f, which)):
        m = halves[0].shape[0]
        out.append([pltpu.make_async_copy(src, held.at[j, pl.ds(i * m, m)], sem.at[2 * j + i])
                    for i, src in enumerate(halves)])
    for pair in out:
        for copy in pair:
            copy.start()
    return out


def ff_wait(copies, j, held, order, pm, shards, rows, out):
    for copy in copies[j]:
        copy.wait()
    for s in range(shards):
        out[s * rows:(s + 1) * rows] = held[j, place(s, order) ^ pm]


def forward_kernel(
    order, shards,
    scal, o00, o01, o10, o11, o20, o21, tok_ref, cot_ref, vec_ref, bin_ref, *rest,
):
    held, f, rest = rest[:4], rest[4:14], rest[14:]
    (out_ref, mix_ref, first_n_ref, inv1_ref, inner_ref, hid_ref, dg_ref, dsum2_ref, dsec_ref, vg_ref,
     wo_s, wi_s, wd_s, w_s, first_s, acc_s, isem, dsem) = rest
    pm, mc, core = scal[0], scal[1], scal[2]
    seqs, shard, width = tok_ref.shape
    rows = width // shards
    n_rows = seqs * shard
    in_copies = ff_copies(f, 0, wi_s, isem)
    down_copies = ff_copies(f, 1, wd_s, dsem)
    weights_in(wo_s, order, pm, core, rows, shards, held)
    mixed = jnp.concatenate(
        [jnp.concatenate([a[...].astype(BF), b[...].astype(BF)], 0) for a, b in ((o00, o01), (o10, o11), (o20, o21))], 1)
    mix_ref[...] = mixed
    tokens = tok_ref[...].reshape(n_rows, width).astype(F32)
    normed, inverse = moments(tokens + (dot(mixed, wo_s[...]) + vec_ref[2:3, :]))
    first_n_ref[...] = normed
    inv1_ref[...] = inverse
    first = normed * vec_ref[3:4, :] + vec_ref[4:5, :]
    first_s[...] = first
    inner_ref[...] = first.astype(BF)
    for j in range(4):
        ff_wait(in_copies, j, wi_s, order, pm, shards, rows, w_s)
        for r in range(0, n_rows, 128):
            pre = dot(inner_ref[r:r + 128, :], w_s[...]) + bin_ref[mc ^ j]
            hid, dg = gelu_parts(pre)
            hid_ref[j, r:r + 128, :] = hid.astype(BF)
            dg_ref[j, r:r + 128, :] = dg.astype(BF)
        ff_wait(down_copies, j, wd_s, order, pm, shards, rows, w_s)
        part = dot(hid_ref[j], w_s[...])
        acc_s[...] = part if j == 0 else acc_s[...] + part
    normed, inverse = moments(first_s[...] + (acc_s[...] + vec_ref[5:6, :]))
    gain = vec_ref[6:7, :]
    out_ref[...] = (normed * gain + vec_ref[7:8, :]).astype(BF).reshape(seqs, shard, width)
    dy = cot_ref[...].reshape(n_rows, width).astype(F32)
    dsum2 = norm_back(dy, normed, inverse, gain)
    dsum2_ref[...] = dsum2
    dsec = dsum2.astype(BF)
    dsec_ref[...] = dsec
    vg_ref[0:1, :] = jnp.sum(dy * normed, 0, keepdims=True)
    vg_ref[1:2, :] = jnp.sum(dy, 0, keepdims=True)
    vg_ref[2:3, :] = jnp.sum(dsec.astype(F32), 0, keepdims=True)


def down_grad_kernel(order, shards, scal, hid, dsec, keep, send):
    pm = scal[0]
    sub = keep.shape[2]
    for j in (1, 3, 0, 2):
        out = keep if j % 2 == 0 else send
        grad = dot_tn(hid[j], dsec[...]).astype(BF)
        for s in range(shards):
            out[j >> 1, place(s, order) ^ pm] = grad[s * sub:(s + 1) * sub]


def in_grad_kernel(order, shards, scal, inner, dg, dsec, *rest):
    f, (keep, send, dpre_ref, gbin_ref, wd_s, w_s, sem) = rest[:10], rest[10:]
    pm, mc = scal[0], scal[1]
    rows = keep.shape[2]
    step = pl.program_id(0)

    @pl.when(step == 0)
    def _():
        ff_copies(f, 1, wd_s, sem)

    for i, j in enumerate((1, 3, 0, 2)):
        @pl.when(step == i)
        def _(j=j):
            copies = {j: [pltpu.make_async_copy(src, wd_s.at[j, pl.ds(k * src.shape[0], src.shape[0])], sem.at[2 * j + k])
                          for k, src in enumerate(ff_sources(f, 1)[j])]}
            ff_wait(copies, j, wd_s, order, pm, shards, rows, w_s)

    j = jnp.where(step < 2, 2 * step + 1, 2 * step - 4)
    dpre = (dot_nt(dsec[...], w_s[...]) * dg[0].astype(F32)).astype(BF)
    dpre_ref[0] = dpre
    gbin_ref[mc ^ j] = jnp.sum(dpre.astype(F32), 0, keepdims=True)
    grad = dot_tn(inner[...], dpre).astype(BF)

    @pl.when(step < 2)
    def _():
        for s in range(shards):
            send[0, place(s, order) ^ pm] = grad[s * rows:(s + 1) * rows]

    @pl.when(step >= 2)
    def _():
        for s in range(shards):
            keep[0, place(s, order) ^ pm] = grad[s * rows:(s + 1) * rows]


def first_grad_kernel(
    order, shards, scal, mix_ref, first_n, inv1, dpre, dsum2, vec_ref, *rest,
):
    held, rest = rest[:4], rest[4:]
    f, (go_keep, go_send, dsum1_ref, dmix_ref, vg_ref, wo_s, wi_s, w_s, sem) = rest[:10], rest[10:]
    pm, core = scal[0], scal[2]
    n_rows, width = dsum2.shape
    rows = width // shards
    half = width // 2
    in_copies = ff_copies(f, 0, wi_s, sem)
    weights_in(wo_s, order, pm, core, rows, shards, held)
    dfirst = dsum2[...]
    for j in range(4):
        ff_wait(in_copies, j, wi_s, order, pm, shards, rows, w_s)
        dfirst = dfirst + dot_nt(dpre[j], w_s[...])
    normed = first_n[...]
    dsum1 = norm_back(dfirst, normed, inv1[...], vec_ref[3:4, :])
    dsum1_ref[...] = dsum1
    dbranch = dsum1.astype(BF)
    vg_ref[0:1, :] = jnp.sum(dfirst * normed, 0, keepdims=True)
    vg_ref[1:2, :] = jnp.sum(dfirst, 0, keepdims=True)
    vg_ref[2:3, :] = jnp.sum(dbranch.astype(F32), 0, keepdims=True)
    dmix_ref[...] = dot_nt(dbranch, wo_s[...]).astype(BF)
    grad_o = dot_tn(mix_ref[...], dbranch).astype(BF)
    first_core = core == 0
    for s in range(shards):
        block = grad_o[s * rows:(s + 1) * rows]
        at = place(s, order) ^ pm
        go_keep[at] = jnp.where(first_core, block[:, :half], block[:, half:])
        go_send[at] = jnp.where(first_core, block[:, half:], block[:, :half])


def attend_back_kernel(
    aliased,
    scal, e_ref, dm_ref, q_ref, k_ref, v_ref, o_ref, inv_ref, *rest,
):
    if aliased:
        rest = rest[1:]
    gp_ref, dq_ref, dkv_ref, vt_s, qt_s, dmt_s, dmi_s, dl_s, dkt_s, dvt_s, dq_s = rest
    h = pl.program_id(0)
    shard, cols = q_ref.shape
    head = cols // 4

    @pl.when(h == 0)
    def _():
        vt_s[...] = v_ref[...].T
        dmi = (dm_ref[...].astype(F32) * inv_ref[...]).astype(BF)
        dmi_s[...] = dmi
        dl_s[...] = dmi.astype(F32) * o_ref[...]
        qt_s[...] = q_ref[...].T
        dmt_s[...] = dmi.T

    lane = lax.broadcasted_iota(jnp.int32, (shard, cols), 1) // head
    this = lane == h
    dmm = jnp.where(this, dmi_s[...].astype(F32), 0.0).astype(BF)
    delta = jnp.sum(jnp.where(this, dl_s[...], 0.0), -1, keepdims=True)
    step = 64
    for r in range(0, shard, step):
        dp = dot(dmm[r:r + step], vt_s[...])
        gp_ref[0, 0, r:r + step, :] = (
            e_ref[0, r:r + step, :].astype(F32) * (dp - delta[r:r + step])
        ).astype(BF)
    g = gp_ref[0, 0]
    dq = dot(g, k_ref[...]) * (1.0 / math.sqrt(head))
    dq_s[...] = jnp.where(this, dq, dq_s[...])
    at = pl.multiple_of(h * head, head)
    dkt_s[pl.ds(at, head), :] = dot(qt_s[pl.ds(at, head), :], g).astype(BF)
    dvt_s[pl.ds(at, head), :] = dot(dmt_s[pl.ds(at, head), :], e_ref[0]).astype(BF)

    @pl.when(h == 3)
    def _():
        dq_ref[...] = dq_s[...].astype(BF)
        dkv_ref[:, :cols] = dkt_s[...].T
        dkv_ref[:, cols:] = dvt_s[...].T


def table_rows(s, sums, gbin, rows, sub, half):
    pieces = [v[:, s * rows:(s + 1) * rows] for v in sums]
    for b in range(4):
        pieces.append(gbin[2 * (b & 1) + (b >> 1), :, s * sub:(s + 1) * sub])
    lines, line, p = [], [], 0
    for piece in pieces:
        line.append(piece)
        p += piece.shape[1]
        if p % half == 0:
            lines.append(jnp.concatenate(line, 1))
            line = []
    if line:
        line.append(jnp.zeros((1, half - p % half), F32))
        lines.append(jnp.concatenate(line, 1))
    lines.append(jnp.zeros((8 - len(lines), half), F32))
    value = jnp.concatenate(lines, 0)
    high = value.astype(BF)
    return jnp.concatenate([high.astype(F32), value - high.astype(F32)], 0).astype(BF)


def weight_grad_kernel(order, shards, kind, sub, scal, xt_ref, dq0, dq1, dkv0, dkv1, *rest):
    pm, mc, core = scal[0], scal[1], scal[2]
    shard, cols = dq0.shape
    length = dkv0.shape[0]
    extra, (g_keep, g_send, vg_ref) = rest[:-3], rest[-3:]
    mine = pl.multiple_of(mc * shard, shard)
    ones = jnp.ones((8, length), BF)
    grad_kv = dot(xt_ref[0], dkv0[...]) + dot(xt_ref[1], dkv1[...])
    grad_q = dot(xt_ref[0, :, pl.ds(mine, shard)], dq0[...]) + dot(xt_ref[1, :, pl.ds(mine, shard)], dq1[...])
    vg_ref[1:2, :] = (dot(ones, dkv0[:, cols:]) + dot(ones, dkv1[:, cols:]))[0:1]
    vg_ref[0:1, :] = (dot(ones[:, :shard], dq0[...]) + dot(ones[:, :shard], dq1[...]))[0:1]
    grad = jnp.concatenate([grad_q.astype(BF), grad_kv.astype(BF)], 1)
    rows = grad.shape[0] // shards
    half = grad.shape[1] // 2
    first_core = core == 0
    if kind == 2:
        vg0, vg1, ff1, ff2, gbin = extra
        sums = [
            jnp.concatenate([vg0[i:i + 1, :], vg1[i:i + 1, :], vg_ref[i:i + 1, :]], 1) for i in range(2)
        ] + [ff1[2:3, :], ff1[0:1, :], ff1[1:2, :], ff2[2:3, :], ff2[0:1, :], ff2[1:2, :]]
    for i in range(shards):
        block = grad[i * rows:(i + 1) * rows]
        to = place(i, order) ^ pm
        keep = jnp.where(first_core, block[:, :half], block[:, half:])
        send = jnp.where(first_core, block[:, half:], block[:, :half])
        if kind == 0:
            go_keep, go_send = extra
            near = (mc >> 1) == 0
            g_keep[0, to] = jnp.where(near, keep, go_keep[to])
            g_keep[1, to] = jnp.where(near, go_keep[to], keep)
            g_send[0, to] = jnp.where(near, send, go_send[to])
            g_send[1, to] = jnp.where(near, go_send[to], send)
        else:
            g_keep[to, :rows, :] = keep
            g_send[to, :rows, :] = send
        if kind == 2:
            table = table_rows(i, sums, gbin, rows, sub, half)
            g_keep[to, rows:, :] = table
            g_send[to, rows:, :] = table


def sum_kernel(rows, *refs):
    parts, out = refs[:-1], refs[-1]
    for i in range(out.shape[0]):
        total = parts[0][i].astype(F32)
        for part in parts[1:]:
            total = total + part[i].astype(F32)
        out[i, :rows] = total[:rows].astype(BF)
        value = total[rows:rows + 8] + total[rows + 8:]
        high = value.astype(BF).astype(F32)
        out[i, rows:] = jnp.concatenate([high, value - high], 0).astype(BF)


def token_kernel(
    order, shards, own,
    scal, dq00, dq01, dq10, dq11, dq20, dq21, dkv00, dkv01, dkv10, dkv11, dkv20, dkv21,
    *rest,
):
    held, rest = rest[:12], rest[12:]
    w_s = rest[-1]
    pm, mc, core = scal[0], scal[1], scal[2]
    rows = w_s.shape[1] // shards
    shard, cols = dq00.shape
    weights_in(w_s.at[0], order, pm, core, rows, shards, held[:4])
    weights_in(w_s.at[1], order, pm, core, rows, shards, held[4:8])
    weights_in(w_s.at[2], order, pm, core, rows, shards, held[8:])
    dqs = ((dq00, dq10, dq20), (dq01, dq11, dq21))
    dkvs = ((dkv00, dkv10, dkv20), (dkv01, dkv11, dkv21))
    outs = [(0, rest[1])] if own else [(1, rest[0].at[0]), (3, rest[0].at[1]), (2, rest[1])]
    for j, out in outs:
        where = pl.multiple_of((mc ^ j) * shard, shard)
        for s in range(2):
            total = rest[0][s * shard:(s + 1) * shard, :] if own else None
            for g in range(3):
                part = dot_nt(dkvs[s][g][pl.ds(where, shard), :], w_s[g, :, cols:])
                if own:
                    part = part + dot_nt(dqs[s][g][...], w_s[g, :, :cols])
                total = part if total is None else total + part
            out[s] = total.astype(out.dtype)


def finish_kernel(rows, sub, shards, scal, f, fy, fc, fyc, e, ey, ec, eyc, wq, wk, wv, wo, wi, wd, tab):
    low = scal[2] == 0
    near = (scal[1] >> 1) == 0
    half = e.shape[1]
    cols = wq.shape[1] // 3
    cut = half - cols
    zero_at, one_at = rows + 16, 2 * rows + 16

    def both(mine, other):
        mine, other = mine.astype(F32), other.astype(F32)
        return jnp.where(low, mine, other), jnp.where(low, other, mine)

    def four(a, b, c, d):
        return both(jnp.where(near, a, b), jnp.where(near, c, d)), both(jnp.where(near, b, a), jnp.where(near, d, c))

    def added(at):
        parts = [ref[at:at + rows].astype(F32) for ref in (e, ey, ec, eyc)]
        return both(parts[0] + parts[1], parts[2] + parts[3])

    zero, outer = four(*[ref[zero_at:zero_at + rows] for ref in (e, ey, ec, eyc)])
    groups = [zero, added(one_at), added(0)]
    for g, (first, second) in enumerate(groups):
        at = g * cols
        wq[:, at:at + cols] = first[:, :cols]
        wk[:, at:at + cut] = first[:, cols:]
        wk[:, at + cut:at + cols] = second[:, :cols - cut]
        wv[:, at:at + cols] = second[:, cols - cut:]
    wo[:, :half] = outer[0]
    wo[:, half:] = outer[1]
    tab[...] = sum(ref[at:at + 8, :].astype(F32) for ref in (e, ey) for at in (rows, rows + 8))
    (i00, i10), (i01, i11) = four(f[0], fy[0], fc[0], fyc[0])
    (d00, d10), (d01, d11) = four(f[1], fy[1], fc[1], fyc[1])
    for b, (i_part, d_part) in enumerate(((i00, d00), (i01, d01), (i10, d10), (i11, d11))):
        wd[b * sub:(b + 1) * sub, :] = d_part
        for s in range(shards):
            at = (4 * s + b) * sub
            wi[:, at:at + sub] = i_part[:, s * sub:(s + 1) * sub]


def on_device(
    n, far, near,
    tokens, prior_logits, doc_ids, w_query, w_key, w_value, w_out, b_query, b_value, b_out,
    first_norm_gain, norm1_shift, w_in, b_in, w_down, b_down, norm2_gain, norm2_shift, cotangent,
):
    seqs, shard, width = tokens.shape
    heads, length = prior_logits.shape[1], prior_logits.shape[3]
    ctx = length // shard
    rows = w_query.shape[0]
    sub = w_down.shape[0] // 4
    cols = width // GROUPS
    per = heads // GROUPS
    half = (3 * cols) // 2
    n_rows = seqs * shard
    m = n // 2
    order = far + near
    me_s = lax.axis_index("seq")
    me_c = lax.axis_index("ctx")
    core = me_c & 1
    pm = place(me_s, order)
    scal = jnp.stack([pm, me_c, core]).astype(jnp.int32)
    sds = jax.ShapeDtypeStruct
    hbm = pl.BlockSpec(memory_space=pltpu.HBM)

    def kernel(body, outs, ins, args, scratch=(), grid=None, alias=None, flops=0, moved=0, exps=0, name=None, limit=24):
        return pl.pallas_call(
            body,
            out_shape=outs,
            in_specs=ins[0],
            out_specs=ins[1],
            scratch_shapes=scratch,
            input_output_aliases=alias or {},
            compiler_params=params(len(grid) if grid else 0, limit),
            cost_estimate=pl.CostEstimate(flops=flops, bytes_accessed=moved, transcendentals=exps),
            name=name,
            **({"grid": grid} if grid else {}),
        )(*args)

    def by_core(value):
        return swap(value, "ctx", ctx, 0)

    def by_y(value):
        return swap(value, "ctx", ctx, 1)

    def by_x(value):
        return swap(value, "seq", n, near[-1])

    def whole(*shape):
        return pl.BlockSpec(shape, lambda *i: (0,) * len(shape))

    vectors = [b_query, b_value, b_out, first_norm_gain, norm1_shift, b_down, norm2_gain, norm2_shift, b_in]
    a0, tok0 = kernel(
        prep_kernel, [sds((rows + 16, 4 * half), BF), sds((seqs, shard + 16, width), BF)],
        ([smem()] + [vmem()] * 15, [vmem()] * 2),
        (scal, tokens, doc_ids, w_query, w_key, w_value, w_out, *[v.reshape(1, -1) for v in vectors]),
        moved=10**6, name="prep", limit=60,
    )
    ffq, = kernel(
        prep_ff_kernel, [sds((2, rows, width), BF)], ([smem()] + [vmem()] * 2, [vmem()]),
        (after(scal, a0), w_in, w_down), moved=6 * 10**6, name="prep_ff", limit=60,
    )

    def exchange(held):
        return [held] + [swap_by(held, "seq", n, step) for step in far_steps(far)]

    def join(parts, name):
        lead = parts[0].ndim == 3
        shape = (2, 4, *parts[0].shape[1:]) if lead else (4, *parts[0].shape)
        out, = kernel(join_kernel, [sds(shape, BF)], ([vmem()] * 4, [vmem()]), parts, moved=10**6, name=name)
        for bit in near[:-1]:
            out = jnp.concatenate([out, swap(out, "seq", n, bit)], 1 if lead else 0)
        return out

    tok2 = by_y(tok0)
    a_lo, b_lo, c_lo = kernel(
        join_split_kernel, [sds((4, rows + 16, half), BF), sds((4, rows, half), BF), sds((4, rows, 2 * half), BF)],
        ([vmem()] * 4, [vmem()] * 3), [after(x, ffq) for x in exchange(a0)], moved=10**6, name="join")

    def nearer(held, axis):
        for bit in near[:-1]:
            held = jnp.concatenate([held, swap(held, "seq", n, bit)], axis)
        return held

    a_lo, b_lo, c_lo = nearer(a_lo, 0), nearer(b_lo, 0), nearer(c_lo, 0)
    a_hi = by_x(a_lo)
    f_half = swap_by(after(ffq, a_lo), "seq", n, 1 << far[0])
    tok1 = by_core(after(tok0, a_lo))
    ag_lo = by_core(a_lo)
    ag_hi = by_core(a_hi)
    tok3 = by_core(after(tok2, a_hi))
    tok = (tok0, tok1, tok2, tok3)
    b_hi = by_x(after(b_lo, a_hi, ag_lo, tok1))

    def doubled(a, b, name):
        a, b = a.reshape(2, -1, *a.shape[-2:]), b.reshape(2, -1, *b.shape[-2:])
        shape = (2, 2 * a.shape[1], *a.shape[2:])
        out, = kernel(join_pair_kernel, [sds(shape, BF)], ([vmem()] * 2, [vmem()]), (a, b), moved=10**6, name=name)
        return out

    vecs, bin_all = kernel(
        functools.partial(vector_kernel, order, n, rows, sub),
        [sds((8, width), F32), sds((4, 1, width), F32)],
        ([smem()] + [vmem()] * 2, [vmem()] * 2), (after(scal, ag_lo, tok1, ag_hi, tok3), a_lo, a_hi), moved=10**6, name="vectors",
    )

    raw = None
    kept = []

    def attend(g, s, scal, arrays):
        nonlocal raw
        big = pl.BlockSpec((1, 1, shard, length), lambda h: (s, g * per + h, 0, 0))
        tok_spec = pl.BlockSpec((1, shard + 16, width), lambda h: (s, 0, 0))
        block = 0
        w_spec = pl.BlockSpec((m, arrays[0].shape[1], half), lambda h: (0, 0, block))
        args = [scal, *tok, doc_ids, vecs, prior_logits, *arrays]
        specs = [smem()] + [tok_spec] * 4 + [vmem(), pl.BlockSpec((8, cols), lambda h: (0, g)), big] + [w_spec] * len(arrays)
        alias = {}
        if raw is not None:
            alias = {len(args): 0}
            args.append(raw)
            specs.append(hbm)
        raw, *rest = kernel(
            functools.partial(attend_kernel, order, n, s, g, raw is not None),
            [sds(prior_logits.shape, BF), pltpu.HBM((per, shard, length), BF), pltpu.HBM((shard, cols), BF),
             pltpu.HBM((length, cols), BF), pltpu.HBM((length, cols), BF), pltpu.HBM((shard, cols), F32), pltpu.HBM((shard, cols), F32)],
            (specs, [big, pl.BlockSpec((1, shard, length), lambda h: (h, 0, 0)), whole(shard, cols), whole(length, cols),
                     whole(length, cols), whole(shard, cols), whole(shard, cols)]),
            args, [VM((width, 3 * cols), BF), VM((cols, length), BF), VM((shard, length), F32), VM((2, length, cols), BF)],
            grid=(per,), alias=alias, flops=5 * 10**9, moved=10 * 10**6, exps=10**6, name=f"attend{g}{s}", limit=48,
        )
        kept.append(rest)
        return rest[2]

    a_set = (a_lo, a_hi, ag_lo, ag_hi)
    attend(0, 0, after(scal, vecs), a_set)
    mark = kept[-1][4]
    f_two = doubled(after(ffq, mark), f_half, "join_f")
    b_hi = after(b_hi, f_two)
    bg_lo, bg_hi = by_core(after(b_lo, b_hi)), by_core(b_hi)
    b_set = (b_lo, b_hi, bg_lo, bg_hi)
    f_far = swap_by(after(f_two, b_hi), "seq", n, 1 << far[1])
    c_hi = by_x(after(c_lo, b_hi))
    attend(0, 1, after(scal, f_two, bg_lo, bg_hi), a_set)
    mark = kept[-1][4]
    f_lo = nearer(doubled(after(f_two, mark), f_far, "join_ff"), 1)
    c_hi = after(c_hi, f_lo)
    cg_lo, cg_hi = by_core(after(c_lo, c_hi)), by_core(c_hi)
    c_set = (c_lo, c_hi, cg_lo, cg_hi)
    f_lo = after(f_lo, cg_lo, cg_hi)
    f_ylo, f_hi = by_y(f_lo), by_x(f_lo)
    attend(1, 0, after(scal, f_lo, cg_lo, cg_hi), b_set)
    attend(1, 1, scal, b_set)
    x_t, = kernel(turn_kernel, [pltpu.HBM((seqs, width, length), BF)], ([smem()] + [vmem()] * 4, [vmem()]),
                  (after(scal, kept[-1][4]), *tok), moved=12 * 10**6, name="turn")
    f_hi, f_ylo = after(f_hi, x_t, f_ylo), after(f_ylo, x_t, f_hi)
    f_yhi_i, f_yhi_d = by_y(f_hi[0]), by_x(f_ylo[1])
    fc_hi, fc_ylo = by_core(f_hi), by_core(f_ylo)
    attend(2, 0, after(scal, x_t, f_hi, f_ylo), c_set)
    mark = kept[-1][4]
    fc_lo = by_core(after(f_lo, mark, fc_hi, fc_ylo))
    attend(2, 1, after(scal, fc_hi, fc_ylo), c_set)
    mark = kept[-1][4]
    f_yhi_i, f_yhi_d = after(f_yhi_i, mark, fc_lo), after(f_yhi_d, mark, fc_lo)
    fc_yhi_i, fc_yhi_d = by_core(f_yhi_i), by_core(f_yhi_d)
    f = (f_lo, f_hi, f_ylo, f_yhi_i, f_yhi_d, fc_lo, fc_hi, fc_ylo, fc_yhi_i, fc_yhi_d)

    o_spec = pl.BlockSpec((m, rows, half), lambda i: (0, 0, 1))
    w_scratch = VM((4, n, rows, width), BF)
    w_one = VM((width, width), BF)
    sems = pltpu.SemaphoreType.DMA((8,))
    output, mixed, first_n, inv1, inner, hid, dg, dsum2, dsec, ff2 = kernel(
        functools.partial(forward_kernel, order, n),
        [
            sds((seqs, shard, width), BF), sds((n_rows, width), BF), sds((n_rows, width), F32), sds((n_rows, 1), F32),
            sds((n_rows, width), BF), sds((4, n_rows, width), BF), sds((4, n_rows, width), BF),
            sds((n_rows, width), F32), sds((n_rows, width), BF), sds((8, width), F32),
        ],
        ([smem()] + [vmem()] * 10 + [o_spec] * 4 + [pl.BlockSpec(memory_space=ANY)] * 10, [vmem()] * 10),
        (scal, *[k[4] for k in kept], tokens, cotangent, vecs, bin_all, *c_set, *f),
        [VM((width, width), BF), w_scratch, w_scratch, w_one, VM((n_rows, width), F32), VM((n_rows, width), F32), sems, sems],
        grid=(1,), flops=6 * 10**9, moved=25 * 10**6, exps=2 * 10**6, name="ff_fwd", limit=48,
    )
    def quarter(i):
        return (jnp.where(i < 2, 2 * i + 1, 2 * i - 4), 0, 0)

    pair = [sds((2, n, rows, width), BF)] * 2
    d_keep, d_send = kernel(
        functools.partial(down_grad_kernel, order, n), pair,
        ([smem()] + [vmem()] * 2, [vmem()] * 2), (scal, hid, dsec), flops=3 * 10**9, moved=8 * 10**6, name="down_grad", limit=24,
    )
    d_got = by_core(d_send)
    dx_send = add(d_keep[:, m:], d_got[:, m:])
    i_keep, i_send, dpre, gbin = kernel(
        functools.partial(in_grad_kernel, order, n),
        pair + [sds((4, n_rows, width), BF), sds((4, 1, width), F32)],
        ([smem(), whole(n_rows, width), pl.BlockSpec((1, n_rows, width), quarter), whole(n_rows, width)] + [pl.BlockSpec(memory_space=ANY)] * 10,
         [pl.BlockSpec((1, n, rows, width), lambda i: (jnp.maximum(i - 2, 0), 0, 0, 0)),
          pl.BlockSpec((1, n, rows, width), lambda i: (jnp.minimum(i, 1), 0, 0, 0)),
          pl.BlockSpec((1, n_rows, width), quarter), whole(4, 1, width)]),
        (after(scal, d_keep), inner, dg, dsec, *f), [w_scratch, w_one, sems], grid=(4,), flops=6 * 10**9, moved=20 * 10**6, name="in_grad", limit=40,
    )
    i_got = by_core(i_send)
    go_keep, go_send, dsum1, dmix, ff1 = kernel(
        functools.partial(first_grad_kernel, order, n),
        [sds((n, rows, half), BF)] * 2 + [sds((n_rows, width), F32), sds((n_rows, width), BF), sds((8, width), F32)],
        ([smem()] + [vmem()] * 6 + [o_spec] * 4 + [pl.BlockSpec(memory_space=ANY)] * 10, [vmem()] * 5),
        (after(scal, dx_send), mixed, first_n, inv1, dpre, dsum2, vecs, *c_set, *f), [VM((width, width), BF), w_scratch, w_one, sems],
        grid=(1,), flops=4 * 10**9, moved=15 * 10**6, name="first_grad", limit=40,
    )

    gp = None
    dqs, dkvs, vgs = [], [], []

    def back(g, s, scal):
        nonlocal gp
        e, q, k, v, o, inv = kept[g * seqs + s]
        big = pl.BlockSpec((1, 1, shard, length), lambda h: (s, g * per + h, 0, 0))
        args = [scal, e, dmix, q, k, v, o, inv]
        specs = [smem(), pl.BlockSpec((1, shard, length), lambda h: (h, 0, 0)),
                 pl.BlockSpec((shard, cols), lambda h: (s, g)),
                 whole(shard, cols), whole(length, cols), whole(length, cols), whole(shard, cols), whole(shard, cols)]
        alias = {}
        if gp is not None:
            alias = {len(args): 0}
            args.append(gp)
            specs.append(hbm)
        gp, dq, dkv = kernel(
            functools.partial(attend_back_kernel, gp is not None),
            [sds(prior_logits.shape, BF), sds((shard, cols), BF), sds((length, 2 * cols), BF)],
            (specs, [big, whole(shard, cols), whole(length, 2 * cols)]),
            args,
            [VM((cols, length), BF), VM((cols, shard), BF), VM((cols, shard), BF), VM((shard, cols), BF),
             VM((shard, cols), F32), VM((cols, length), BF), VM((cols, length), BF), VM((shard, cols), F32)],
            grid=(per,), alias=alias, flops=5 * 10**9, moved=10 * 10**6, name=f"back{g}{s}", limit=24,
        )
        dqs.append(dq)
        dkvs.append(dkv)
        return dq

    def weight_grad(g, scal):
        extra = ([go_keep, go_send], [], vgs + [ff1, ff2, gbin])[g]
        shape = ((2, n, rows, half), (n, rows, half), (n, rows + 16, half))[g]
        keep, send, vg = kernel(
            functools.partial(weight_grad_kernel, order, n, g, sub),
            [sds(shape, BF)] * 2 + [sds((8, cols), F32)],
            ([smem()] + [vmem()] * (5 + len(extra)), [vmem()] * 3),
            (scal, x_t, *dqs[-2:], *dkvs[-2:], *extra),
            flops=2 * 10**9, moved=8 * 10**6, name=f"weight_grad{g}", limit=24,
        )
        vgs.append(vg)
        return keep, send, vg

    def rest_near(held, axis, plus):
        for bit in reversed(near[:-1]):
            k = held.shape[axis] // 2
            keep = lax.slice_in_dim(held, 0, k, axis=axis)
            held = plus(keep, swap(lax.slice_in_dim(held, k, 2 * k, axis=axis), "seq", n, bit))
        return held

    def far_sum(blocks, plus):
        got = [swap_by(b, "seq", n, step) for b, step in zip(blocks[1:], far_steps(far))]
        return plus(blocks[0], *got)

    def plus_table(*parts):
        flat = parts[0].ndim == 2
        parts = [p[None] if flat else p for p in parts]
        out, = kernel(functools.partial(sum_kernel, rows), [sds(parts[0].shape, BF)],
                      ([vmem()] * len(parts), [vmem()]), parts, moved=10**6, name="sum_table")
        return out[0] if flat else out

    dx_got = by_x(dx_send)
    iy_send = add(i_keep[1], i_got[1])
    iy_got = by_y(iy_send)
    back(0, 0, after(scal, iy_send))
    mark = back(0, 1, scal)
    dx_got = after(dx_got, mark)
    dy_send = add(d_keep[1, :m], d_got[1, :m], dx_got[1])
    dy_got = by_y(dy_send)
    g0_keep, g0_send, _ = weight_grad(0, after(scal, dy_send))
    g0_got = by_core(g0_send)
    mark = back(1, 0, after(scal, g0_keep))
    iy_got = after(iy_got, mark)
    ix_send = add(i_keep[0, m:], i_got[0, m:], iy_got[m:])
    ix_got = by_x(ix_send)
    g0y_send = add(after(g0_keep, mark)[1], g0_got[1])
    g0y_got = by_y(g0y_send)
    back(1, 1, after(scal, ix_send, g0y_send))
    g1_keep, g1_send, mark = weight_grad(1, scal)
    g1_got = by_core(g1_send)
    dl = add(after(d_keep, mark)[0, :m], d_got[0, :m], dx_got[0], dy_got)
    il = add(after(i_keep, mark)[0, :m], i_got[0, :m], iy_got[:m], ix_got)
    lo = rest_near(jnp.stack([il, dl], 1), 0, add)
    ff_far = swap_by(lo[2:], "seq", n, 1 << far[1])
    g0y_got = after(g0y_got, mark)
    g0x_send = add(g0_keep[0, m:], g0_got[0, m:], g0y_got[m:])
    g0x_got = by_x(g0x_send)
    mark = back(2, 0, after(scal, lo, g0x_send))
    g1x_send = add(after(g1_keep, mark)[m:], g1_got[m:])
    g1x_got = by_x(g1x_send)
    g0 = rest_near(add(after(g0_keep, mark)[0, :m], g0_got[0, :m], g0y_got[:m], g0x_got), 0, add)
    ff_two = add(after(lo, mark)[:2], ff_far)
    ff_got = swap_by(ff_two[1], "seq", n, 1 << far[0])
    mark = back(2, 1, after(scal, g0, g1x_send, ff_two))
    ff = add(after(ff_two, mark)[0], ff_got)
    g1 = rest_near(add(after(g1_keep, mark)[:m], g1_got[:m], g1x_got), 0, add)
    pair, pair_send = kernel(pair_kernel, [sds((2, rows, 2 * half), BF)] * 2, ([vmem()] * 2, [vmem()] * 2), (after(g0, ff), g1),
                             moved=10**6, name="pair")
    pair_got = swap_by(pair_send, "seq", n, 1 << far[1])
    ff_y = by_y(after(ff, pair))
    g2_keep, g2_send, mark = weight_grad(2, after(scal, pair))
    g2_got = by_core(g2_send)
    all_sets = (*a_set, *b_set, *c_set)
    set_specs = [whole(m, a.shape[1], half) for a in a_set + b_set] + [whole(m, rows, half)] * 4
    w_all = VM((GROUPS, width, 3 * cols), BF)
    far_a, far_b = kernel(
        functools.partial(token_kernel, order, n, False),
        [sds((2, seqs, shard, width), BF), sds((seqs, shard, width), BF)],
        ([smem()] + [vmem()] * 12 + set_specs, [vmem()] * 2),
        (after(scal, mark), *dqs, *dkvs, *all_sets),
        [w_all], grid=(1,), flops=6 * 10**9, moved=15 * 10**6, name="token_far", limit=30,
    )
    pair = add(after(pair, far_b), pair_got)
    g2_got = after(g2_got, pair)
    g2x_send = plus_table(g2_keep[m:], g2_got[m:])
    far_got = by_core(after(far_a, g2x_send))
    g2x_got = by_x(g2x_send)
    pair_got = swap_by(after(pair, g2x_send)[1], "seq", n, 1 << far[0])
    across_send = add(far_b, far_got[1])
    across = by_y(across_send)
    own_part, = kernel(
        functools.partial(token_kernel, order, n, True),
        [sds((seqs, shard, width), F32)],
        ([smem()] + [vmem()] * 12 + set_specs + [vmem()], [vmem()]),
        (after(scal, across_send), *dqs, *dkvs, *all_sets, dsum1),
        [w_all], grid=(1,), flops=4 * 10**9, moved=15 * 10**6, name="token_own", limit=30,
    )
    pair = add(after(pair, own_part)[0], pair_got)
    g2 = rest_near(plus_table(g2_keep[:m], g2_got[:m], after(g2x_got, pair)), 0, plus_table)
    g2_far = [swap_by(g2[i + 1], "seq", n, step) for i, step in enumerate(far_steps(far))]
    ends, = kernel(functools.partial(ends_kernel, rows), [sds((3 * rows + 16, half), BF)], ([vmem()] * 5, [vmem()]),
                   (g2[0], *g2_far, pair), moved=10**6, name="ends")
    grad_tokens = own_part + far_got[0].astype(F32) + across.astype(F32)
    ends = after(ends, grad_tokens)
    ends_y = by_y(ends)
    ends_c = by_core(ends)
    ff_c, ff_yc = by_core(after(ff, ends)), by_core(after(ff_y, ends))
    g_wq, g_wk, g_wv, g_wo, g_wi, g_wd, table = kernel(
        functools.partial(finish_kernel, rows, sub, n),
        [sds(w.shape, F32) for w in (w_query, w_key, w_value, w_out, w_in, w_down)] + [sds((8, half), F32)],
        ([smem()] + [vmem()] * 8, [vmem()] * 7),
        (scal, ff, ff_y, ff_c, ff_yc, ends, ends_y, ends_c, by_core(ends_y)),
        moved=4 * 10**6, name="finish",
    )
    table = table.reshape(-1)
    cut = [table[i * rows:(i + 1) * rows] for i in range(8)]
    g_bq, g_bv, g_bo, g_g1, g_s1, g_bd, g_g2, g_s2 = cut
    g_bin = table[8 * rows:8 * rows + 4 * sub]
    return (
        output, raw, grad_tokens, gp, g_wq, g_wk, g_wv, g_wo,
        g_bq, g_bv, g_bo, g_g1, g_s1, g_wi, g_bin, g_wd, g_bd, g_g2, g_s2,
    )


def solution(mesh):
    n = mesh.shape["seq"]
    top = n.bit_length() - 1
    far, near = (top - 1, top - 2), tuple(reversed(range(top - 2)))
    in_specs = (
        P("seq", "ctx", None), P("seq", None, "ctx", None), P("seq", "ctx"),
        P("seq", None), P("seq", None), P("seq", None), P("seq", None),
        P("seq"), P("seq"), P("seq"), P("seq"), P("seq"),
        P("seq", None), P("seq"), P("seq", None), P("seq"), P("seq"), P("seq"),
        P("seq", "ctx", None),
    )
    out_specs = (
        P("seq", "ctx", None), P("seq", None, "ctx", None), P("seq", "ctx", None), P("seq", None, "ctx", None),
        P("seq", None), P("seq", None), P("seq", None), P("seq", None),
        P("seq"), P("seq"), P("seq"), P("seq"), P("seq"),
        P("seq", None), P("seq"), P("seq", None), P("seq"), P("seq"), P("seq"),
    )
    return jax.shard_map(
        functools.partial(on_device, n, far, near),
        mesh=mesh, in_specs=in_specs, out_specs=out_specs, check_vma=False,
    )
```

```python
import functools
import math

import jax
import jax.numpy as jnp
from jax import lax
from jax.experimental import pallas as pl
from jax.experimental.pallas import tpu as pltpu
from jax.sharding import PartitionSpec as P

EPSILON = 1e-05
NEGATIVE = -1e30
BF = jnp.bfloat16
F32 = jnp.float32
VM = pltpu.VMEM
ANY = pl.ANY
GROUPS = 3


def dot(a, b):
    return lax.dot_general(a, b, (((1,), (0,)), ((), ())), preferred_element_type=F32)


def dot_nt(a, b):
    return lax.dot_general(a, b, (((1,), (1,)), ((), ())), preferred_element_type=F32)


def dot_tn(a, b):
    return lax.dot_general(a, b, (((0,), (0,)), ((), ())), preferred_element_type=F32)


def vmem(shape=None, index=None):
    if shape is None:
        return pl.BlockSpec(memory_space=VM)
    return pl.BlockSpec(shape, index)


def params(n_grid, limit):
    return pltpu.CompilerParams(
        vmem_limit_bytes=limit * 1024 * 1024,
        dimension_semantics=("arbitrary",) * n_grid if n_grid else None,
    )


def smem():
    return pl.BlockSpec(memory_space=pltpu.SMEM)


def after(value, *marks):
    return lax.optimization_barrier((value, *marks))[0]


def swap_by(value, axis, size, step):
    return lax.ppermute(value, axis, [(i, i ^ step) for i in range(size)])


def swap(value, axis, size, bit):
    return swap_by(value, axis, size, 1 << bit)


def far_steps(far):
    a, b = 1 << far[0], 1 << far[1]
    return (a, b, a | b)


def add(*parts):
    total = parts[0].astype(F32)
    for part in parts[1:]:
        total = total + part.astype(F32)
    return total.astype(BF)


def place(index, order):
    out = 0
    for step, bit in enumerate(order):
        out = out | (((index >> bit) & 1) << step)
    return out


def column_half(wq, wk, wv, g, half, low):
    cols = (2 * half) // 3
    cut = half - cols
    at = g * cols
    first = jnp.concatenate([wq[:, at:at + cols], wk[:, at:at + cut]], 1)
    second = jnp.concatenate([wk[:, at + cut:at + cols], wv[:, at:at + cols]], 1)
    return jnp.where(low, first, second)


def prep_kernel(scal, tok, docs, wq, wk, wv, wo, *rest):
    vecs, (a0, tok_ref) = rest[:9], rest[9:]
    seqs, shard = tok.shape[:2]
    rows = wq.shape[0]
    half = a0.shape[1] // 4
    low = scal[2] == 0
    for s in range(seqs):
        tok_ref[s, :shard, :] = tok[s]
        tok_ref[s, shard:, :] = jnp.zeros_like(tok_ref[s, shard:, :])
        tok_ref[s, shard:shard + 1, :shard] = docs[s:s + 1, :].astype(F32).astype(BF)
    for g in range(3):
        a0[:rows, g * half:(g + 1) * half] = column_half(wq, wk, wv, g, half, low)
    a0[:rows, 3 * half:] = jnp.where(low, wo[:, :half], wo[:, half:])
    p = 0
    lines = []
    line = []
    for v in vecs:
        step = rows if v.shape[1] == rows else v.shape[1] // 4
        for i in range(v.shape[1] // step):
            line.append(v[:, i * step:(i + 1) * step].astype(F32))
            p += step
            if p % half == 0:
                lines.append(jnp.concatenate(line, 1))
                line = []
    if line:
        line.append(jnp.zeros((1, half - p % half), F32))
        lines.append(jnp.concatenate(line, 1))
    lines.append(jnp.zeros((16 - len(lines), half), F32))
    a0[rows:, :half] = jnp.concatenate(lines, 0).astype(BF)
    a0[rows:, half:] = jnp.zeros_like(a0[rows:, half:])


def prep_ff_kernel(scal, wi, wd, ffq):
    mc, core = scal[1], scal[2]
    my_y = mc >> 1
    low = core == 0
    sub = ffq.shape[1]
    width = ffq.shape[2]
    block = 2 * core + my_y
    ffq[1] = wd[pl.ds(pl.multiple_of(block * sub, sub), sub), :]
    for s in range(width // sub):
        got = [wi[:, (4 * s + b) * sub:(4 * s + b + 1) * sub] for b in range(4)]
        near = jnp.where(my_y == 0, got[0], got[1])
        far = jnp.where(my_y == 0, got[2], got[3])
        ffq[0, :, s * sub:(s + 1) * sub] = jnp.where(low, near, far)


def join_kernel(a, b, c, d, out):
    lead = out.ndim == 4
    for i, ref in enumerate((a, b, c, d)):
        if lead:
            out[:, i] = ref[...]
        else:
            out[i] = ref[...]


def fetch(lo, hi, at):
    m = lo.shape[0]
    return jnp.where(at < m, lo[at & (m - 1)], hi[at & (m - 1)])


def join_split_kernel(a, b, c, d, first, second, third):
    half = first.shape[2]
    rows = second.shape[1]
    for i, ref in enumerate((a, b, c, d)):
        first[i] = ref[:, :half]
        second[i] = ref[:rows, half:2 * half]
        third[i] = ref[:rows, 2 * half:]


def join_pair_kernel(a, b, out):
    k = a.shape[1]
    out[:, :k] = a[...]
    out[:, k:] = b[...]


def pair_kernel(a, b, near, far):
    half = a.shape[2]
    for i in range(4):
        out = near if i < 2 else far
        out[i % 2, :, :half] = a[i]
        out[i % 2, :, half:] = b[i]


def ends_kernel(rows, p0, p1, p2, p3, pair, out):
    total = p0[...].astype(F32) + p1[...].astype(F32) + p2[...].astype(F32) + p3[...].astype(F32)
    out[:rows] = total[:rows].astype(BF)
    value = total[rows:rows + 8] + total[rows + 8:]
    high = value.astype(BF).astype(F32)
    out[rows:rows + 16] = jnp.concatenate([high, value - high], 0).astype(BF)
    half = out.shape[1]
    out[rows + 16:2 * rows + 16] = pair[:, :half]
    out[2 * rows + 16:] = pair[:, half:]


def weights_in(out, order, pm, core, rows, shards, held):
    first = core == 0
    m = held[0].shape[0]
    half = held[0].shape[2]
    for i in range(shards):
        at = place(i, order) ^ pm
        spot = at & (m - 1)
        in_lo = at < m
        four = [ref[spot, :rows, :] for ref in held]
        mine = jnp.where(in_lo, four[0], four[1])
        other = jnp.where(in_lo, four[2], four[3])
        out[i * rows:(i + 1) * rows, :half] = jnp.where(first, mine, other)
        out[i * rows:(i + 1) * rows, half:2 * half] = jnp.where(first, other, mine)


def vector_kernel(order, shards, rows, sub, scal, lo, hi, vec_ref, bin_ref):
    pm = scal[0]
    half = lo.shape[2]
    m = lo.shape[0]
    for s in range(shards):
        at = place(s, order) ^ pm
        block = jnp.where(at < m, lo[at & (m - 1), rows:, :], hi[at & (m - 1), rows:, :]).astype(F32)
        for i in range(8):
            p = i * rows
            vec_ref[i:i + 1, s * rows:(s + 1) * rows] = block[p // half:p // half + 1, p % half:p % half + rows]
        for b in range(4):
            p = 8 * rows + b * sub
            c = 2 * (b & 1) + (b >> 1)
            bin_ref[c, :, s * sub:(s + 1) * sub] = block[p // half:p // half + 1, p % half:p % half + sub]


def turn_kernel(scal, t0, t1, t2, t3, out_ref):
    mc = scal[1]
    seqs, _, width = t0.shape
    shard = out_ref.shape[2] // 4
    for j, tok in enumerate((t0, t1, t2, t3)):
        where = pl.multiple_of((mc ^ j) * shard, shard)
        for s in range(seqs):
            out_ref[s, :, pl.ds(where, shard)] = tok[s, :shard, :].T


def attend_kernel(
    order, shards, seq, group, aliased,
    scal, t0, t1, t2, t3, doc_ref, bias_ref, prior_ref, *rest,
):
    held, rest = rest[:4], rest[4:]
    if aliased:
        rest = rest[1:]
    raw_ref, e_ref, q_ref, k_ref, v_ref, o_ref, inv_ref, w_s, kt_s, mask_s, vx_s = rest
    h = pl.program_id(0)
    pm, mc, core = scal[0], scal[1], scal[2]
    rows = w_s.shape[0] // shards
    shard, cols = q_ref.shape
    head = cols // 4

    @pl.when(h == 0)
    def _():
        weights_in(w_s, order, pm, core, rows, shards, held)
        q = dot(t0[0, :shard, :], w_s[:, :cols]) + bias_ref[0:1, :]
        q_ref[...] = (q.astype(BF).astype(F32) * (1.0 / math.sqrt(head))).astype(BF)
        mine = jnp.broadcast_to(doc_ref[seq:seq + 1, :].astype(F32), (128, shard)).T[:, :1]
        for j, tok in enumerate((t0, t1, t2, t3)):
            where = pl.multiple_of((mc ^ j) * shard, shard)
            kv = dot(tok[0, :shard, :], w_s[:, cols:])
            k_ref[pl.ds(where, shard), :] = kv[:, :cols].astype(BF)
            v = kv[:, cols:] + bias_ref[1:2, :]
            v_ref[pl.ds(where, shard), :] = v.astype(BF)
            even = (lax.broadcasted_iota(jnp.int32, (shard, cols), 1) // head) % 2 == 0
            vx_s[0, pl.ds(where, shard), :] = jnp.where(even, v, 1.0).astype(BF)
            vx_s[1, pl.ds(where, shard), :] = jnp.where(even, 1.0, v).astype(BF)
            docs = tok[0, shard:shard + 1, :shard].astype(F32)
            mask_s[:, pl.ds(where, shard)] = jnp.where(mine == docs, 0.0, NEGATIVE)
        kt_s[...] = k_ref[...].T

    lane = lax.broadcasted_iota(jnp.int32, (shard, cols), 1) // head
    this = lane == h
    qm = jnp.where(this, q_ref[...].astype(F32), 0.0).astype(BF)
    step = 64
    for r in range(0, shard, step):
        logits = dot(qm[r:r + step], kt_s[...]) + prior_ref[0, 0, r:r + step, :].astype(F32)
        raw_ref[0, 0, r:r + step, :] = logits.astype(BF)
        masked = logits + mask_s[r:r + step, :]
        top = jnp.max(masked, -1, keepdims=True)
        e_ref[0, r:r + step, :] = jnp.exp(masked - top).astype(BF)
    o = dot(e_ref[0], vx_s[h & 1])
    total = jnp.max(jnp.where(lane == (h ^ 1), o, 0.0), -1, keepdims=True)
    inv = 1.0 / total
    o_ref[...] = jnp.where(this, o * inv, o_ref[...])
    inv_ref[...] = jnp.where(this, inv, inv_ref[...])


def gelu_parts(x):
    z = jnp.abs(x) * 0.7071067811865476
    t = 1.0 / (1.0 + 0.3275911 * z)
    e = jnp.exp(-0.5 * x * x)
    poly = t * (0.254829592 + t * (-0.284496736 + t * (1.421413741 + t * (-1.453152027 + t * 1.061405429))))
    tail = 0.5 * poly * e
    phi = jnp.where(x >= 0, 1.0 - tail, tail)
    return x * phi, phi + x * (e * 0.3989422804014327)


def moments(x):
    mean = jnp.mean(x, -1, keepdims=True)
    centered = x - mean
    inverse = lax.rsqrt(jnp.mean(centered * centered, -1, keepdims=True) + EPSILON)
    return centered * inverse, inverse


def norm_back(grad, normed, inverse, gain):
    scaled = grad * gain
    return inverse * (
        scaled - jnp.mean(scaled, -1, keepdims=True)
        - normed * jnp.mean(scaled * normed, -1, keepdims=True)
    )


def ff_sources(f, which):
    lo, hi, ylo, yhi_i, yhi_d, clo, chi, cylo, cyhi_i, cyhi_d = f
    yhi, cyhi = (yhi_i, cyhi_i) if which == 0 else (yhi_d, cyhi_d)
    return [(lo.at[which], hi.at[which]), (clo.at[which], chi.at[which]),
            (ylo.at[which], yhi), (cylo.at[which], cyhi)]


def ff_copies(f, which, held, sem):
    out = []
    for j, halves in enumerate(ff_sources(f, which)):
        m = halves[0].shape[0]
        out.append([pltpu.make_async_copy(src, held.at[j, pl.ds(i * m, m)], sem.at[2 * j + i])
                    for i, src in enumerate(halves)])
    for pair in out:
        for copy in pair:
            copy.start()
    return out


def ff_wait(copies, j, held, order, pm, shards, rows, out):
    for copy in copies[j]:
        copy.wait()
    for s in range(shards):
        out[s * rows:(s + 1) * rows] = held[j, place(s, order) ^ pm]


def forward_kernel(
    order, shards,
    scal, o00, o01, o10, o11, o20, o21, tok_ref, cot_ref, vec_ref, bin_ref, *rest,
):
    held, f, rest = rest[:4], rest[4:14], rest[14:]
    (out_ref, mix_ref, first_n_ref, inv1_ref, inner_ref, hid_ref, dg_ref, dsum2_ref, dsec_ref, vg_ref,
     wo_s, wi_s, wd_s, w_s, first_s, acc_s, isem, dsem) = rest
    pm, mc, core = scal[0], scal[1], scal[2]
    seqs, shard, width = tok_ref.shape
    rows = width // shards
    n_rows = seqs * shard
    in_copies = ff_copies(f, 0, wi_s, isem)
    down_copies = ff_copies(f, 1, wd_s, dsem)
    weights_in(wo_s, order, pm, core, rows, shards, held)
    mixed = jnp.concatenate(
        [jnp.concatenate([a[...].astype(BF), b[...].astype(BF)], 0) for a, b in ((o00, o01), (o10, o11), (o20, o21))], 1)
    mix_ref[...] = mixed
    tokens = tok_ref[...].reshape(n_rows, width).astype(F32)
    normed, inverse = moments(tokens + (dot(mixed, wo_s[...]) + vec_ref[2:3, :]))
    first_n_ref[...] = normed
    inv1_ref[...] = inverse
    first = normed * vec_ref[3:4, :] + vec_ref[4:5, :]
    first_s[...] = first
    inner_ref[...] = first.astype(BF)
    for j in range(4):
        ff_wait(in_copies, j, wi_s, order, pm, shards, rows, w_s)
        for r in range(0, n_rows, 128):
            pre = dot(inner_ref[r:r + 128, :], w_s[...]) + bin_ref[mc ^ j]
            hid, dg = gelu_parts(pre)
            hid_ref[j, r:r + 128, :] = hid.astype(BF)
            dg_ref[j, r:r + 128, :] = dg.astype(BF)
        ff_wait(down_copies, j, wd_s, order, pm, shards, rows, w_s)
        part = dot(hid_ref[j], w_s[...])
        acc_s[...] = part if j == 0 else acc_s[...] + part
    normed, inverse = moments(first_s[...] + (acc_s[...] + vec_ref[5:6, :]))
    gain = vec_ref[6:7, :]
    out_ref[...] = (normed * gain + vec_ref[7:8, :]).astype(BF).reshape(seqs, shard, width)
    dy = cot_ref[...].reshape(n_rows, width).astype(F32)
    dsum2 = norm_back(dy, normed, inverse, gain)
    dsum2_ref[...] = dsum2
    dsec = dsum2.astype(BF)
    dsec_ref[...] = dsec
    vg_ref[0:1, :] = jnp.sum(dy * normed, 0, keepdims=True)
    vg_ref[1:2, :] = jnp.sum(dy, 0, keepdims=True)
    vg_ref[2:3, :] = jnp.sum(dsec.astype(F32), 0, keepdims=True)


def down_grad_kernel(order, shards, scal, hid, dsec, keep, send):
    pm = scal[0]
    sub = keep.shape[2]
    for j in (1, 3, 0, 2):
        out = keep if j % 2 == 0 else send
        grad = dot_tn(hid[j], dsec[...]).astype(BF)
        for s in range(shards):
            out[j >> 1, place(s, order) ^ pm] = grad[s * sub:(s + 1) * sub]


def in_grad_kernel(order, shards, scal, inner, dg, dsec, *rest):
    f, (keep, send, dpre_ref, gbin_ref, wd_s, w_s, sem) = rest[:10], rest[10:]
    pm, mc = scal[0], scal[1]
    rows = keep.shape[2]
    step = pl.program_id(0)

    @pl.when(step == 0)
    def _():
        ff_copies(f, 1, wd_s, sem)

    for i, j in enumerate((1, 3, 0, 2)):
        @pl.when(step == i)
        def _(j=j):
            copies = {j: [pltpu.make_async_copy(src, wd_s.at[j, pl.ds(k * src.shape[0], src.shape[0])], sem.at[2 * j + k])
                          for k, src in enumerate(ff_sources(f, 1)[j])]}
            ff_wait(copies, j, wd_s, order, pm, shards, rows, w_s)

    j = jnp.where(step < 2, 2 * step + 1, 2 * step - 4)
    dpre = (dot_nt(dsec[...], w_s[...]) * dg[0].astype(F32)).astype(BF)
    dpre_ref[0] = dpre
    gbin_ref[mc ^ j] = jnp.sum(dpre.astype(F32), 0, keepdims=True)
    grad = dot_tn(inner[...], dpre).astype(BF)

    @pl.when(step < 2)
    def _():
        for s in range(shards):
            send[0, place(s, order) ^ pm] = grad[s * rows:(s + 1) * rows]

    @pl.when(step >= 2)
    def _():
        for s in range(shards):
            keep[0, place(s, order) ^ pm] = grad[s * rows:(s + 1) * rows]


def first_grad_kernel(
    order, shards, scal, mix_ref, first_n, inv1, dpre, dsum2, vec_ref, *rest,
):
    held, rest = rest[:4], rest[4:]
    f, (go_keep, go_send, dsum1_ref, dmix_ref, vg_ref, wo_s, wi_s, w_s, sem) = rest[:10], rest[10:]
    pm, core = scal[0], scal[2]
    n_rows, width = dsum2.shape
    rows = width // shards
    half = width // 2
    in_copies = ff_copies(f, 0, wi_s, sem)
    weights_in(wo_s, order, pm, core, rows, shards, held)
    dfirst = dsum2[...]
    for j in range(4):
        ff_wait(in_copies, j, wi_s, order, pm, shards, rows, w_s)
        dfirst = dfirst + dot_nt(dpre[j], w_s[...])
    normed = first_n[...]
    dsum1 = norm_back(dfirst, normed, inv1[...], vec_ref[3:4, :])
    dsum1_ref[...] = dsum1
    dbranch = dsum1.astype(BF)
    vg_ref[0:1, :] = jnp.sum(dfirst * normed, 0, keepdims=True)
    vg_ref[1:2, :] = jnp.sum(dfirst, 0, keepdims=True)
    vg_ref[2:3, :] = jnp.sum(dbranch.astype(F32), 0, keepdims=True)
    dmix_ref[...] = dot_nt(dbranch, wo_s[...]).astype(BF)
    grad_o = dot_tn(mix_ref[...], dbranch).astype(BF)
    first_core = core == 0
    for s in range(shards):
        block = grad_o[s * rows:(s + 1) * rows]
        at = place(s, order) ^ pm
        go_keep[at] = jnp.where(first_core, block[:, :half], block[:, half:])
        go_send[at] = jnp.where(first_core, block[:, half:], block[:, :half])


def attend_back_kernel(
    aliased,
    scal, e_ref, dm_ref, q_ref, k_ref, v_ref, o_ref, inv_ref, *rest,
):
    if aliased:
        rest = rest[1:]
    gp_ref, dq_ref, dkv_ref, vt_s, qt_s, dmt_s, dmi_s, dl_s, dkt_s, dvt_s, dq_s = rest
    h = pl.program_id(0)
    shard, cols = q_ref.shape
    head = cols // 4

    @pl.when(h == 0)
    def _():
        vt_s[...] = v_ref[...].T
        dmi = (dm_ref[...].astype(F32) * inv_ref[...]).astype(BF)
        dmi_s[...] = dmi
        dl_s[...] = dmi.astype(F32) * o_ref[...]
        qt_s[...] = q_ref[...].T
        dmt_s[...] = dmi.T

    lane = lax.broadcasted_iota(jnp.int32, (shard, cols), 1) // head
    this = lane == h
    dmm = jnp.where(this, dmi_s[...].astype(F32), 0.0).astype(BF)
    delta = jnp.sum(jnp.where(this, dl_s[...], 0.0), -1, keepdims=True)
    step = 64
    for r in range(0, shard, step):
        dp = dot(dmm[r:r + step], vt_s[...])
        gp_ref[0, 0, r:r + step, :] = (
            e_ref[0, r:r + step, :].astype(F32) * (dp - delta[r:r + step])
        ).astype(BF)
    g = gp_ref[0, 0]
    dq = dot(g, k_ref[...]) * (1.0 / math.sqrt(head))
    dq_s[...] = jnp.where(this, dq, dq_s[...])
    at = pl.multiple_of(h * head, head)
    dkt_s[pl.ds(at, head), :] = dot(qt_s[pl.ds(at, head), :], g).astype(BF)
    dvt_s[pl.ds(at, head), :] = dot(dmt_s[pl.ds(at, head), :], e_ref[0]).astype(BF)

    @pl.when(h == 3)
    def _():
        dq_ref[...] = dq_s[...].astype(BF)
        dkv_ref[:, :cols] = dkt_s[...].T
        dkv_ref[:, cols:] = dvt_s[...].T


def table_rows(s, sums, gbin, rows, sub, half):
    pieces = [v[:, s * rows:(s + 1) * rows] for v in sums]
    for b in range(4):
        pieces.append(gbin[2 * (b & 1) + (b >> 1), :, s * sub:(s + 1) * sub])
    lines, line, p = [], [], 0
    for piece in pieces:
        line.append(piece)
        p += piece.shape[1]
        if p % half == 0:
            lines.append(jnp.concatenate(line, 1))
            line = []
    if line:
        line.append(jnp.zeros((1, half - p % half), F32))
        lines.append(jnp.concatenate(line, 1))
    lines.append(jnp.zeros((8 - len(lines), half), F32))
    value = jnp.concatenate(lines, 0)
    high = value.astype(BF)
    return jnp.concatenate([high.astype(F32), value - high.astype(F32)], 0).astype(BF)


def weight_grad_kernel(order, shards, kind, sub, scal, xt_ref, dq0, dq1, dkv0, dkv1, *rest):
    pm, mc, core = scal[0], scal[1], scal[2]
    shard, cols = dq0.shape
    length = dkv0.shape[0]
    extra, (g_keep, g_send, vg_ref) = rest[:-3], rest[-3:]
    mine = pl.multiple_of(mc * shard, shard)
    ones = jnp.ones((8, length), BF)
    grad_kv = dot(xt_ref[0], dkv0[...]) + dot(xt_ref[1], dkv1[...])
    grad_q = dot(xt_ref[0, :, pl.ds(mine, shard)], dq0[...]) + dot(xt_ref[1, :, pl.ds(mine, shard)], dq1[...])
    vg_ref[1:2, :] = (dot(ones, dkv0[:, cols:]) + dot(ones, dkv1[:, cols:]))[0:1]
    vg_ref[0:1, :] = (dot(ones[:, :shard], dq0[...]) + dot(ones[:, :shard], dq1[...]))[0:1]
    grad = jnp.concatenate([grad_q.astype(BF), grad_kv.astype(BF)], 1)
    rows = grad.shape[0] // shards
    half = grad.shape[1] // 2
    first_core = core == 0
    if kind == 2:
        vg0, vg1, ff1, ff2, gbin = extra
        sums = [
            jnp.concatenate([vg0[i:i + 1, :], vg1[i:i + 1, :], vg_ref[i:i + 1, :]], 1) for i in range(2)
        ] + [ff1[2:3, :], ff1[0:1, :], ff1[1:2, :], ff2[2:3, :], ff2[0:1, :], ff2[1:2, :]]
    for i in range(shards):
        block = grad[i * rows:(i + 1) * rows]
        to = place(i, order) ^ pm
        keep = jnp.where(first_core, block[:, :half], block[:, half:])
        send = jnp.where(first_core, block[:, half:], block[:, :half])
        if kind == 0:
            go_keep, go_send = extra
            near = (mc >> 1) == 0
            g_keep[0, to] = jnp.where(near, keep, go_keep[to])
            g_keep[1, to] = jnp.where(near, go_keep[to], keep)
            g_send[0, to] = jnp.where(near, send, go_send[to])
            g_send[1, to] = jnp.where(near, go_send[to], send)
        else:
            g_keep[to, :rows, :] = keep
            g_send[to, :rows, :] = send
        if kind == 2:
            table = table_rows(i, sums, gbin, rows, sub, half)
            g_keep[to, rows:, :] = table
            g_send[to, rows:, :] = table


def sum_kernel(rows, *refs):
    parts, out = refs[:-1], refs[-1]
    for i in range(out.shape[0]):
        total = parts[0][i].astype(F32)
        for part in parts[1:]:
            total = total + part[i].astype(F32)
        out[i, :rows] = total[:rows].astype(BF)
        value = total[rows:rows + 8] + total[rows + 8:]
        high = value.astype(BF).astype(F32)
        out[i, rows:] = jnp.concatenate([high, value - high], 0).astype(BF)


def token_kernel(
    order, shards, own,
    scal, dq00, dq01, dq10, dq11, dq20, dq21, dkv00, dkv01, dkv10, dkv11, dkv20, dkv21,
    *rest,
):
    held, rest = rest[:12], rest[12:]
    w_s = rest[-1]
    pm, mc, core = scal[0], scal[1], scal[2]
    rows = w_s.shape[1] // shards
    shard, cols = dq00.shape
    weights_in(w_s.at[0], order, pm, core, rows, shards, held[:4])
    weights_in(w_s.at[1], order, pm, core, rows, shards, held[4:8])
    weights_in(w_s.at[2], order, pm, core, rows, shards, held[8:])
    dqs = ((dq00, dq10, dq20), (dq01, dq11, dq21))
    dkvs = ((dkv00, dkv10, dkv20), (dkv01, dkv11, dkv21))
    outs = [(0, rest[1])] if own else [(1, rest[0].at[0]), (3, rest[0].at[1]), (2, rest[1])]
    for j, out in outs:
        where = pl.multiple_of((mc ^ j) * shard, shard)
        for s in range(2):
            total = rest[0][s * shard:(s + 1) * shard, :] if own else None
            for g in range(3):
                part = dot_nt(dkvs[s][g][pl.ds(where, shard), :], w_s[g, :, cols:])
                if own:
                    part = part + dot_nt(dqs[s][g][...], w_s[g, :, :cols])
                total = part if total is None else total + part
            out[s] = total.astype(out.dtype)


def finish_kernel(rows, sub, shards, scal, f, fy, fc, fyc, e, ey, ec, eyc, wq, wk, wv, wo, wi, wd, tab):
    low = scal[2] == 0
    near = (scal[1] >> 1) == 0
    half = e.shape[1]
    cols = wq.shape[1] // 3
    cut = half - cols
    zero_at, one_at = rows + 16, 2 * rows + 16

    def both(mine, other):
        mine, other = mine.astype(F32), other.astype(F32)
        return jnp.where(low, mine, other), jnp.where(low, other, mine)

    def four(a, b, c, d):
        return both(jnp.where(near, a, b), jnp.where(near, c, d)), both(jnp.where(near, b, a), jnp.where(near, d, c))

    def added(at):
        parts = [ref[at:at + rows].astype(F32) for ref in (e, ey, ec, eyc)]
        return both(parts[0] + parts[1], parts[2] + parts[3])

    zero, outer = four(*[ref[zero_at:zero_at + rows] for ref in (e, ey, ec, eyc)])
    groups = [zero, added(one_at), added(0)]
    for g, (first, second) in enumerate(groups):
        at = g * cols
        wq[:, at:at + cols] = first[:, :cols]
        wk[:, at:at + cut] = first[:, cols:]
        wk[:, at + cut:at + cols] = second[:, :cols - cut]
        wv[:, at:at + cols] = second[:, cols - cut:]
    wo[:, :half] = outer[0]
    wo[:, half:] = outer[1]
    tab[...] = sum(ref[at:at + 8, :].astype(F32) for ref in (e, ey) for at in (rows, rows + 8))
    (i00, i10), (i01, i11) = four(f[0], fy[0], fc[0], fyc[0])
    (d00, d10), (d01, d11) = four(f[1], fy[1], fc[1], fyc[1])
    for b, (i_part, d_part) in enumerate(((i00, d00), (i01, d01), (i10, d10), (i11, d11))):
        wd[b * sub:(b + 1) * sub, :] = d_part
        for s in range(shards):
            at = (4 * s + b) * sub
            wi[:, at:at + sub] = i_part[:, s * sub:(s + 1) * sub]


def on_device(
    n, far, near,
    tokens, prior_logits, doc_ids, w_query, w_key, w_value, w_out, b_query, b_value, b_out,
    first_norm_gain, norm1_shift, w_in, b_in, w_down, b_down, norm2_gain, norm2_shift, cotangent,
):
    seqs, shard, width = tokens.shape
    heads, length = prior_logits.shape[1], prior_logits.shape[3]
    ctx = length // shard
    rows = w_query.shape[0]
    sub = w_down.shape[0] // 4
    cols = width // GROUPS
    per = heads // GROUPS
    half = (3 * cols) // 2
    n_rows = seqs * shard
    m = n // 2
    order = far + near
    me_s = lax.axis_index("seq")
    me_c = lax.axis_index("ctx")
    core = me_c & 1
    pm = place(me_s, order)
    scal = jnp.stack([pm, me_c, core]).astype(jnp.int32)
    sds = jax.ShapeDtypeStruct
    hbm = pl.BlockSpec(memory_space=pltpu.HBM)

    def kernel(body, outs, ins, args, scratch=(), grid=None, alias=None, flops=0, moved=0, exps=0, name=None, limit=24):
        return pl.pallas_call(
            body,
            out_shape=outs,
            in_specs=ins[0],
            out_specs=ins[1],
            scratch_shapes=scratch,
            input_output_aliases=alias or {},
            compiler_params=params(len(grid) if grid else 0, limit),
            cost_estimate=pl.CostEstimate(flops=flops, bytes_accessed=moved, transcendentals=exps),
            name=name,
            **({"grid": grid} if grid else {}),
        )(*args)

    def by_core(value):
        return swap(value, "ctx", ctx, 0)

    def by_y(value):
        return swap(value, "ctx", ctx, 1)

    def by_x(value):
        return swap(value, "seq", n, near[-1])

    def whole(*shape):
        return pl.BlockSpec(shape, lambda *i: (0,) * len(shape))

    vectors = [b_query, b_value, b_out, first_norm_gain, norm1_shift, b_down, norm2_gain, norm2_shift, b_in]
    a0, tok0 = kernel(
        prep_kernel, [sds((rows + 16, 4 * half), BF), sds((seqs, shard + 16, width), BF)],
        ([smem()] + [vmem()] * 15, [vmem()] * 2),
        (scal, tokens, doc_ids, w_query, w_key, w_value, w_out, *[v.reshape(1, -1) for v in vectors]),
        moved=10**6, name="prep", limit=60,
    )
    ffq, = kernel(
        prep_ff_kernel, [sds((2, rows, width), BF)], ([smem()] + [vmem()] * 2, [vmem()]),
        (after(scal, a0), w_in, w_down), moved=6 * 10**6, name="prep_ff", limit=60,
    )

    def exchange(held):
        return [held] + [swap_by(held, "seq", n, step) for step in far_steps(far)]

    def join(parts, name):
        lead = parts[0].ndim == 3
        shape = (2, 4, *parts[0].shape[1:]) if lead else (4, *parts[0].shape)
        out, = kernel(join_kernel, [sds(shape, BF)], ([vmem()] * 4, [vmem()]), parts, moved=10**6, name=name)
        for bit in near[:-1]:
            out = jnp.concatenate([out, swap(out, "seq", n, bit)], 1 if lead else 0)
        return out

    tok2 = by_y(tok0)
    a_lo, b_lo, c_lo = kernel(
        join_split_kernel, [sds((4, rows + 16, half), BF), sds((4, rows, half), BF), sds((4, rows, 2 * half), BF)],
        ([vmem()] * 4, [vmem()] * 3), [after(x, ffq) for x in exchange(a0)], moved=10**6, name="join")

    def nearer(held, axis):
        for bit in near[:-1]:
            held = jnp.concatenate([held, swap(held, "seq", n, bit)], axis)
        return held

    a_lo, b_lo, c_lo = nearer(a_lo, 0), nearer(b_lo, 0), nearer(c_lo, 0)
    a_hi = by_x(a_lo)
    f_half = swap_by(after(ffq, a_lo), "seq", n, 1 << far[0])
    tok1 = by_core(after(tok0, a_lo))
    ag_lo = by_core(a_lo)
    ag_hi = by_core(a_hi)
    tok3 = by_core(after(tok2, a_hi))
    tok = (tok0, tok1, tok2, tok3)
    b_hi = by_x(after(b_lo, a_hi, ag_lo, tok1))

    def doubled(a, b, name):
        a, b = a.reshape(2, -1, *a.shape[-2:]), b.reshape(2, -1, *b.shape[-2:])
        shape = (2, 2 * a.shape[1], *a.shape[2:])
        out, = kernel(join_pair_kernel, [sds(shape, BF)], ([vmem()] * 2, [vmem()]), (a, b), moved=10**6, name=name)
        return out

    vecs, bin_all = kernel(
        functools.partial(vector_kernel, order, n, rows, sub),
        [sds((8, width), F32), sds((4, 1, width), F32)],
        ([smem()] + [vmem()] * 2, [vmem()] * 2), (after(scal, ag_lo, tok1, ag_hi, tok3), a_lo, a_hi), moved=10**6, name="vectors",
    )

    raw = None
    kept = []

    def attend(g, s, scal, arrays):
        nonlocal raw
        big = pl.BlockSpec((1, 1, shard, length), lambda h: (s, g * per + h, 0, 0))
        tok_spec = pl.BlockSpec((1, shard + 16, width), lambda h: (s, 0, 0))
        block = 0
        w_spec = pl.BlockSpec((m, arrays[0].shape[1], half), lambda h: (0, 0, block))
        args = [scal, *tok, doc_ids, vecs, prior_logits, *arrays]
        specs = [smem()] + [tok_spec] * 4 + [vmem(), pl.BlockSpec((8, cols), lambda h: (0, g)), big] + [w_spec] * len(arrays)
        alias = {}
        if raw is not None:
            alias = {len(args): 0}
            args.append(raw)
            specs.append(hbm)
        raw, *rest = kernel(
            functools.partial(attend_kernel, order, n, s, g, raw is not None),
            [sds(prior_logits.shape, BF), pltpu.HBM((per, shard, length), BF), pltpu.HBM((shard, cols), BF),
             pltpu.HBM((length, cols), BF), pltpu.HBM((length, cols), BF), pltpu.HBM((shard, cols), F32), pltpu.HBM((shard, cols), F32)],
            (specs, [big, pl.BlockSpec((1, shard, length), lambda h: (h, 0, 0)), whole(shard, cols), whole(length, cols),
                     whole(length, cols), whole(shard, cols), whole(shard, cols)]),
            args, [VM((width, 3 * cols), BF), VM((cols, length), BF), VM((shard, length), F32), VM((2, length, cols), BF)],
            grid=(per,), alias=alias, flops=5 * 10**9, moved=10 * 10**6, exps=10**6, name=f"attend{g}{s}", limit=48,
        )
        kept.append(rest)
        return rest[2]

    a_set = (a_lo, a_hi, ag_lo, ag_hi)
    attend(0, 0, after(scal, vecs), a_set)
    mark = kept[-1][4]
    f_two = doubled(after(ffq, mark), f_half, "join_f")
    b_hi = after(b_hi, f_two)
    bg_lo, bg_hi = by_core(after(b_lo, b_hi)), by_core(b_hi)
    b_set = (b_lo, b_hi, bg_lo, bg_hi)
    f_far = swap_by(after(f_two, b_hi), "seq", n, 1 << far[1])
    c_hi = by_x(after(c_lo, b_hi))
    attend(0, 1, after(scal, f_two, bg_lo, bg_hi), a_set)
    mark = kept[-1][4]
    f_lo = nearer(doubled(after(f_two, mark), f_far, "join_ff"), 1)
    c_hi = after(c_hi, f_lo)
    cg_lo, cg_hi = by_core(after(c_lo, c_hi)), by_core(c_hi)
    c_set = (c_lo, c_hi, cg_lo, cg_hi)
    f_lo = after(f_lo, cg_lo, cg_hi)
    f_ylo, f_hi = by_y(f_lo), by_x(f_lo)
    attend(1, 0, after(scal, f_lo, cg_lo, cg_hi), b_set)
    attend(1, 1, scal, b_set)
    x_t, = kernel(turn_kernel, [pltpu.HBM((seqs, width, length), BF)], ([smem()] + [vmem()] * 4, [vmem()]),
                  (after(scal, kept[-1][4]), *tok), moved=12 * 10**6, name="turn")
    f_hi, f_ylo = after(f_hi, x_t, f_ylo), after(f_ylo, x_t, f_hi)
    f_yhi_i, f_yhi_d = by_y(f_hi[0]), by_x(f_ylo[1])
    fc_hi, fc_ylo = by_core(f_hi), by_core(f_ylo)
    attend(2, 0, after(scal, x_t, f_hi, f_ylo), c_set)
    mark = kept[-1][4]
    fc_lo = by_core(after(f_lo, mark, fc_hi, fc_ylo))
    attend(2, 1, after(scal, fc_hi, fc_ylo), c_set)
    mark = kept[-1][4]
    f_yhi_i, f_yhi_d = after(f_yhi_i, mark, fc_lo), after(f_yhi_d, mark, fc_lo)
    fc_yhi_i, fc_yhi_d = by_core(f_yhi_i), by_core(f_yhi_d)
    f = (f_lo, f_hi, f_ylo, f_yhi_i, f_yhi_d, fc_lo, fc_hi, fc_ylo, fc_yhi_i, fc_yhi_d)

    o_spec = pl.BlockSpec((m, rows, half), lambda i: (0, 0, 1))
    w_scratch = VM((4, n, rows, width), BF)
    w_one = VM((width, width), BF)
    sems = pltpu.SemaphoreType.DMA((8,))
    output, mixed, first_n, inv1, inner, hid, dg, dsum2, dsec, ff2 = kernel(
        functools.partial(forward_kernel, order, n),
        [
            sds((seqs, shard, width), BF), sds((n_rows, width), BF), sds((n_rows, width), F32), sds((n_rows, 1), F32),
            sds((n_rows, width), BF), sds((4, n_rows, width), BF), sds((4, n_rows, width), BF),
            sds((n_rows, width), F32), sds((n_rows, width), BF), sds((8, width), F32),
        ],
        ([smem()] + [vmem()] * 10 + [o_spec] * 4 + [pl.BlockSpec(memory_space=ANY)] * 10, [vmem()] * 10),
        (scal, *[k[4] for k in kept], tokens, cotangent, vecs, bin_all, *c_set, *f),
        [VM((width, width), BF), w_scratch, w_scratch, w_one, VM((n_rows, width), F32), VM((n_rows, width), F32), sems, sems],
        grid=(1,), flops=6 * 10**9, moved=25 * 10**6, exps=2 * 10**6, name="ff_fwd", limit=48,
    )
    def quarter(i):
        return (jnp.where(i < 2, 2 * i + 1, 2 * i - 4), 0, 0)

    pair = [sds((2, n, rows, width), BF)] * 2
    d_keep, d_send = kernel(
        functools.partial(down_grad_kernel, order, n), pair,
        ([smem()] + [vmem()] * 2, [vmem()] * 2), (scal, hid, dsec), flops=3 * 10**9, moved=8 * 10**6, name="down_grad", limit=24,
    )
    d_got = by_core(d_send)
    dx_send = add(d_keep[:, m:], d_got[:, m:])
    i_keep, i_send, dpre, gbin = kernel(
        functools.partial(in_grad_kernel, order, n),
        pair + [sds((4, n_rows, width), BF), sds((4, 1, width), F32)],
        ([smem(), whole(n_rows, width), pl.BlockSpec((1, n_rows, width), quarter), whole(n_rows, width)] + [pl.BlockSpec(memory_space=ANY)] * 10,
         [pl.BlockSpec((1, n, rows, width), lambda i: (jnp.maximum(i - 2, 0), 0, 0, 0)),
          pl.BlockSpec((1, n, rows, width), lambda i: (jnp.minimum(i, 1), 0, 0, 0)),
          pl.BlockSpec((1, n_rows, width), quarter), whole(4, 1, width)]),
        (after(scal, d_keep), inner, dg, dsec, *f), [w_scratch, w_one, sems], grid=(4,), flops=6 * 10**9, moved=20 * 10**6, name="in_grad", limit=40,
    )
    i_got = by_core(i_send)
    go_keep, go_send, dsum1, dmix, ff1 = kernel(
        functools.partial(first_grad_kernel, order, n),
        [sds((n, rows, half), BF)] * 2 + [sds((n_rows, width), F32), sds((n_rows, width), BF), sds((8, width), F32)],
        ([smem()] + [vmem()] * 6 + [o_spec] * 4 + [pl.BlockSpec(memory_space=ANY)] * 10, [vmem()] * 5),
        (after(scal, dx_send), mixed, first_n, inv1, dpre, dsum2, vecs, *c_set, *f), [VM((width, width), BF), w_scratch, w_one, sems],
        grid=(1,), flops=4 * 10**9, moved=15 * 10**6, name="first_grad", limit=40,
    )

    gp = None
    dqs, dkvs, vgs = [], [], []

    def back(g, s, scal):
        nonlocal gp
        e, q, k, v, o, inv = kept[g * seqs + s]
        big = pl.BlockSpec((1, 1, shard, length), lambda h: (s, g * per + h, 0, 0))
        args = [scal, e, dmix, q, k, v, o, inv]
        specs = [smem(), pl.BlockSpec((1, shard, length), lambda h: (h, 0, 0)),
                 pl.BlockSpec((shard, cols), lambda h: (s, g)),
                 whole(shard, cols), whole(length, cols), whole(length, cols), whole(shard, cols), whole(shard, cols)]
        alias = {}
        if gp is not None:
            alias = {len(args): 0}
            args.append(gp)
            specs.append(hbm)
        gp, dq, dkv = kernel(
            functools.partial(attend_back_kernel, gp is not None),
            [sds(prior_logits.shape, BF), sds((shard, cols), BF), sds((length, 2 * cols), BF)],
            (specs, [big, whole(shard, cols), whole(length, 2 * cols)]),
            args,
            [VM((cols, length), BF), VM((cols, shard), BF), VM((cols, shard), BF), VM((shard, cols), BF),
             VM((shard, cols), F32), VM((cols, length), BF), VM((cols, length), BF), VM((shard, cols), F32)],
            grid=(per,), alias=alias, flops=5 * 10**9, moved=10 * 10**6, name=f"back{g}{s}", limit=24,
        )
        dqs.append(dq)
        dkvs.append(dkv)
        return dq

    def weight_grad(g, scal):
        extra = ([go_keep, go_send], [], vgs + [ff1, ff2, gbin])[g]
        shape = ((2, n, rows, half), (n, rows, half), (n, rows + 16, half))[g]
        keep, send, vg = kernel(
            functools.partial(weight_grad_kernel, order, n, g, sub),
            [sds(shape, BF)] * 2 + [sds((8, cols), F32)],
            ([smem()] + [vmem()] * (5 + len(extra)), [vmem()] * 3),
            (scal, x_t, *dqs[-2:], *dkvs[-2:], *extra),
            flops=2 * 10**9, moved=8 * 10**6, name=f"weight_grad{g}", limit=24,
        )
        vgs.append(vg)
        return keep, send, vg

    def rest_near(held, axis, plus):
        for bit in reversed(near[:-1]):
            k = held.shape[axis] // 2
            keep = lax.slice_in_dim(held, 0, k, axis=axis)
            held = plus(keep, swap(lax.slice_in_dim(held, k, 2 * k, axis=axis), "seq", n, bit))
        return held

    def far_sum(blocks, plus):
        got = [swap_by(b, "seq", n, step) for b, step in zip(blocks[1:], far_steps(far))]
        return plus(blocks[0], *got)

    def plus_table(*parts):
        flat = parts[0].ndim == 2
        parts = [p[None] if flat else p for p in parts]
        out, = kernel(functools.partial(sum_kernel, rows), [sds(parts[0].shape, BF)],
                      ([vmem()] * len(parts), [vmem()]), parts, moved=10**6, name="sum_table")
        return out[0] if flat else out

    dx_got = by_x(dx_send)
    iy_send = add(i_keep[1], i_got[1])
    iy_got = by_y(iy_send)
    back(0, 0, after(scal, iy_send))
    mark = back(0, 1, scal)
    dx_got = after(dx_got, mark)
    dy_send = add(d_keep[1, :m], d_got[1, :m], dx_got[1])
    dy_got = by_y(dy_send)
    g0_keep, g0_send, _ = weight_grad(0, after(scal, dy_send))
    g0_got = by_core(g0_send)
    mark = back(1, 0, after(scal, g0_keep))
    iy_got = after(iy_got, mark)
    ix_send = add(i_keep[0, m:], i_got[0, m:], iy_got[m:])
    ix_got = by_x(ix_send)
    g0y_send = add(after(g0_keep, mark)[1], g0_got[1])
    g0y_got = by_y(g0y_send)
    back(1, 1, after(scal, ix_send, g0y_send))
    g1_keep, g1_send, mark = weight_grad(1, scal)
    g1_got = by_core(g1_send)
    dl = add(after(d_keep, mark)[0, :m], d_got[0, :m], dx_got[0], dy_got)
    il = add(after(i_keep, mark)[0, :m], i_got[0, :m], iy_got[:m], ix_got)
    lo = rest_near(jnp.stack([il, dl], 1), 0, add)
    ff_far = swap_by(lo[2:], "seq", n, 1 << far[1])
    g0y_got = after(g0y_got, mark)
    g0x_send = add(g0_keep[0, m:], g0_got[0, m:], g0y_got[m:])
    g0x_got = by_x(g0x_send)
    mark = back(2, 0, after(scal, lo, g0x_send))
    g1x_send = add(after(g1_keep, mark)[m:], g1_got[m:])
    g1x_got = by_x(g1x_send)
    g0 = rest_near(add(after(g0_keep, mark)[0, :m], g0_got[0, :m], g0y_got[:m], g0x_got), 0, add)
    ff_two = add(after(lo, mark)[:2], ff_far)
    ff_got = swap_by(ff_two[1], "seq", n, 1 << far[0])
    mark = back(2, 1, after(scal, g0, g1x_send, ff_two))
    ff = add(after(ff_two, mark)[0], ff_got)
    g1 = rest_near(add(after(g1_keep, mark)[:m], g1_got[:m], g1x_got), 0, add)
    pair, pair_send = kernel(pair_kernel, [sds((2, rows, 2 * half), BF)] * 2, ([vmem()] * 2, [vmem()] * 2), (after(g0, ff), g1),
                             moved=10**6, name="pair")
    pair_got = swap_by(pair_send, "seq", n, 1 << far[1])
    ff_y = by_y(after(ff, pair))
    g2_keep, g2_send, mark = weight_grad(2, after(scal, pair))
    g2_got = by_core(g2_send)
    all_sets = (*a_set, *b_set, *c_set)
    set_specs = [whole(m, a.shape[1], half) for a in a_set + b_set] + [whole(m, rows, half)] * 4
    w_all = VM((GROUPS, width, 3 * cols), BF)
    far_a, far_b = kernel(
        functools.partial(token_kernel, order, n, False),
        [sds((2, seqs, shard, width), BF), sds((seqs, shard, width), BF)],
        ([smem()] + [vmem()] * 12 + set_specs, [vmem()] * 2),
        (after(scal, mark), *dqs, *dkvs, *all_sets),
        [w_all], grid=(1,), flops=6 * 10**9, moved=15 * 10**6, name="token_far", limit=30,
    )
    pair = add(after(pair, far_b), pair_got)
    g2_got = after(g2_got, pair)
    g2x_send = plus_table(g2_keep[m:], g2_got[m:])
    far_got = by_core(after(far_a, g2x_send, ff_y))
    g2x_got = by_x(g2x_send)
    pair_got = swap_by(after(pair, g2x_send)[1], "seq", n, 1 << far[0])
    across_send = add(far_b, far_got[1])
    across = by_y(across_send)
    own_part, = kernel(
        functools.partial(token_kernel, order, n, True),
        [sds((seqs, shard, width), F32)],
        ([smem()] + [vmem()] * 12 + set_specs + [vmem()], [vmem()]),
        (after(scal, across_send), *dqs, *dkvs, *all_sets, dsum1),
        [w_all], grid=(1,), flops=4 * 10**9, moved=15 * 10**6, name="token_own", limit=30,
    )
    pair = add(after(pair, own_part)[0], pair_got)
    g2 = rest_near(plus_table(g2_keep[:m], g2_got[:m], after(g2x_got, pair)), 0, plus_table)
    g2_far = [swap_by(g2[i + 1], "seq", n, step) for i, step in enumerate(far_steps(far))]
    ends, = kernel(functools.partial(ends_kernel, rows), [sds((3 * rows + 16, half), BF)], ([vmem()] * 5, [vmem()]),
                   (g2[0], *g2_far, pair), moved=10**6, name="ends")
    grad_tokens = own_part + far_got[0].astype(F32) + across.astype(F32)
    ends = after(ends, grad_tokens)
    ends_y = by_y(ends)
    ends_c = by_core(ends)
    ff_c, ff_yc = by_core(after(ff, ends)), by_core(after(ff_y, ends))
    g_wq, g_wk, g_wv, g_wo, g_wi, g_wd, table = kernel(
        functools.partial(finish_kernel, rows, sub, n),
        [sds(w.shape, F32) for w in (w_query, w_key, w_value, w_out, w_in, w_down)] + [sds((8, half), F32)],
        ([smem()] + [vmem()] * 8, [vmem()] * 7),
        (scal, ff, ff_y, ff_c, ff_yc, ends, ends_y, ends_c, by_core(ends_y)),
        moved=4 * 10**6, name="finish",
    )
    table = table.reshape(-1)
    cut = [table[i * rows:(i + 1) * rows] for i in range(8)]
    g_bq, g_bv, g_bo, g_g1, g_s1, g_bd, g_g2, g_s2 = cut
    g_bin = table[8 * rows:8 * rows + 4 * sub]
    return (
        output, raw, grad_tokens, gp, g_wq, g_wk, g_wv, g_wo,
        g_bq, g_bv, g_bo, g_g1, g_s1, g_wi, g_bin, g_wd, g_bd, g_g2, g_s2,
    )


def solution(mesh):
    n = mesh.shape["seq"]
    top = n.bit_length() - 1
    far, near = (top - 1, top - 2), tuple(reversed(range(top - 2)))
    in_specs = (
        P("seq", "ctx", None), P("seq", None, "ctx", None), P("seq", "ctx"),
        P("seq", None), P("seq", None), P("seq", None), P("seq", None),
        P("seq"), P("seq"), P("seq"), P("seq"), P("seq"),
        P("seq", None), P("seq"), P("seq", None), P("seq"), P("seq"), P("seq"),
        P("seq", "ctx", None),
    )
    out_specs = (
        P("seq", "ctx", None), P("seq", None, "ctx", None), P("seq", "ctx", None), P("seq", None, "ctx", None),
        P("seq", None), P("seq", None), P("seq", None), P("seq", None),
        P("seq"), P("seq"), P("seq"), P("seq"), P("seq"),
        P("seq", None), P("seq"), P("seq", None), P("seq"), P("seq"), P("seq"),
    )
    return jax.shard_map(
        functools.partial(on_device, n, far, near),
        mesh=mesh, in_specs=in_specs, out_specs=out_specs, check_vma=False,
    )
```
